32 devices in a mesh: ctx: 8 (over z, y), ws: 4 (over x, core).
Axes of the slice: x: 2, y: 2, z: 4, core: 2. Of those that a mesh axis runs over, the one named last changes fastest.
Arguments:
- tokens: bfloat16 [4, 2048, 576], P('ws', 'ctx'), may hold values from -6 to 6
- attn_gain: bfloat16 [576], P('ws'), may hold values from 0.25 to 1.75
- query_weight: bfloat16 [576, 576], P('ws'), may hold values from -0.375 to 0.375
- key_weight: bfloat16 [576, 192], P('ws'), may hold values from -0.375 to 0.375
- value_weight: bfloat16 [576, 192], P('ws'), may hold values from -0.25 to 0.25
- output_weight: bfloat16 [576, 576], P('ws'), may hold values from -1 to 1
- ffn_gain: bfloat16 [576], P('ws'), may hold values from 0.25 to 1.75
- gate_weight: bfloat16 [576, 1536], P('ws'), may hold values from -0.25 to 0.25
- up_weight: bfloat16 [576, 1536], P('ws'), may hold values from -0.25 to 0.25
- down_weight: bfloat16 [1536, 576], P('ws'), may hold values from -0.21875 to 0.21875
- out_grad: bfloat16 [4, 2048, 576], P('ws', 'ctx'), may hold values from -6 to 6
Outputs:
- layer_out: bfloat16 [4, 2048, 576], P('ws', 'ctx')
- tokens_grad: bfloat16 [4, 2048, 576], P('ws', 'ctx')
- attn_gain_grad: float32 [576], P('ws')
- query_weight_grad: float32 [576, 576], P('ws')
- key_weight_grad: float32 [576, 192], P('ws')
- value_weight_grad: float32 [576, 192], P('ws')
- output_weight_grad: float32 [576, 576], P('ws')
- ffn_gain_grad: float32 [576], P('ws')
- gate_weight_grad: float32 [576, 1536], P('ws')
- up_weight_grad: float32 [576, 1536], P('ws')
- down_weight_grad: float32 [1536, 576], P('ws')
The draws below stay inside these ranges and needn't reach their ends.
All inputs are finite; a program needn't handle non-finite values.
Results may differ from the reference program's by a relative error of at most 0.022.
Values may be sent and summed in bfloat16 or wider, within the bound.
No kernel may reach another device: no remote copies, remote signals or barrier semaphores. Data moves between devices by JAX's collectives and lax.ppermute only.
A program may use at most 128 MiB of HBM per device.

```python
import math
import jax
import jax.numpy as jnp
from jax import lax

D = 576
H = 9
KV = 3
HD = 64
FF = 1536
LENGTH = 2048
SEQS = 4


def level_of(rng, dims, shards, smallest, largest):
    def one(position, blocks):
        draws = jax.random.uniform(jax.random.fold_in(jax.random.fold_in(rng, 6), position), (blocks,), jnp.float32, smallest / len(shards), largest / len(shards))
        return jnp.repeat(jnp.exp(draws), dims[position] // blocks).reshape((-1,) + (1,) * (len(dims) - position - 1))

    factor_of = one(*shards[0])
    for cut in shards[1:]:
        factor_of = factor_of * one(*cut)
    return factor_of


def centred(own_key, shape, deviation, bound, cuts=(), kind=jnp.bfloat16):
    gain = level_of(own_key, shape, cuts, -0.22, 0.18) if cuts else 1.0
    entries = jax.random.normal(own_key, shape, jnp.float32) * deviation * gain
    return jnp.minimum(jnp.maximum(entries, -bound), bound).astype(kind)


def setup_inputs(seed: int = 0) -> dict:
    arg_keys = jax.random.split(jax.random.key(seed), 12)
    tokens = centred(arg_keys[0], (SEQS, LENGTH, D), 1.0, 6.0, ((0, 4), (1, 8)))
    attn_gain = jnp.clip(1.0 + 0.15 * jax.random.normal(arg_keys[1], (D,), jnp.float32), 0.25, 1.75).astype(jnp.bfloat16)
    query_weight = centred(arg_keys[2], (D, H * HD), (D // 2) ** -0.5, 0.375, ((0, 4),))
    key_weight = centred(arg_keys[3], (D, KV * HD), (D // 2) ** -0.5, 0.375, ((0, 4),))
    value_weight = centred(arg_keys[4], (D, KV * HD), D ** -0.5, 0.25, ((0, 4),))
    output_weight = centred(arg_keys[5], (H * HD, D), (H * HD // 16) ** -0.5, 1.0, ((0, 4),))
    ffn_gain = jnp.clip(1.0 + 0.15 * jax.random.normal(arg_keys[6], (D,), jnp.float32), 0.25, 1.75).astype(jnp.bfloat16)
    gate_weight = centred(arg_keys[7], (D, FF), D ** -0.5, 0.25, ((0, 4),))
    up_weight = centred(arg_keys[8], (D, FF), D ** -0.5, 0.25, ((0, 4),))
    down_weight = centred(arg_keys[9], (FF, D), (FF // 2) ** -0.5, 0.21875, ((0, 4),))
    out_grad = centred(arg_keys[10], (SEQS, LENGTH, D), 1.0, 6.0, ((0, 4), (1, 8)))
    return dict(tokens=tokens, attn_gain=attn_gain, query_weight=query_weight, key_weight=key_weight, value_weight=value_weight, output_weight=output_weight, ffn_gain=ffn_gain, gate_weight=gate_weight, up_weight=up_weight, down_weight=down_weight, out_grad=out_grad)


EPS = 1e-05
THETA = 100000.0
NEGATIVE = -1e+30

@jax.custom_vjp
def low(v):
    return lax.optimization_barrier(v.astype(jnp.bfloat16)).astype(jnp.float32)

@jax.custom_vjp
def low_back(v):
    return v

def low_keep(v):
    return (low(v), None)

def low_pass(kept, grad):
    return (grad,)

def back_keep(v):
    return (v, None)

def back_low(kept, grad):
    return (low(grad),)
low.defvjp(low_keep, low_pass)
low_back.defvjp(back_keep, back_low)

def matmul_high(operand_left, operand_right):
    return jnp.dot(operand_left, operand_right, precision=lax.Precision.HIGHEST)

def rms_scale(values, gain_vec):
    return values * lax.rsqrt(lax.optimization_barrier(jnp.mean(values * values, -1, keepdims=True)) + EPS) * gain_vec

def rope_tables(positions, head_width):
    half_width = head_width // 2
    frequency = jnp.exp(jnp.arange(half_width).astype(positions.dtype) * (-2.0 * math.log(THETA) / head_width))
    angles = positions[:, None] * frequency[None, :]
    angles = jnp.concatenate([angles, angles], -1)
    return (jnp.cos(angles)[:, None, :], jnp.sin(angles)[:, None, :])

def rotate_pairs(values, cosine_table, sine_table):
    half_width = values.shape[-1] // 2
    turned = jnp.concatenate([-values[..., half_width:], values[..., :half_width]], -1)
    return values * cosine_table + turned * sine_table

def attend(queries, key_rows, value_rows):
    length = queries.shape[0]
    groups = H // KV
    query_heads = queries.reshape(length, KV, groups, HD).transpose(1, 2, 0, 3)
    key_heads = key_rows.transpose(1, 0, 2)
    value_heads = value_rows.transpose(1, 0, 2)
    block_rows = math.gcd(length, 512)
    key_pos = jnp.arange(length, dtype=jnp.int32)

    def one_block(block_index):
        row_start = (block_index * block_rows).astype(jnp.int32)
        query_block = lax.dynamic_slice_in_dim(query_heads, row_start, block_rows, 2)
        scores = low_back(jnp.einsum('agqd,akd->agqk', query_block, key_heads, precision=lax.Precision.HIGHEST))
        query_pos = row_start + jnp.arange(block_rows, dtype=jnp.int32)
        scores = jnp.where(query_pos[:, None] >= key_pos[None, :], scores, NEGATIVE)
        row_max = lax.optimization_barrier(jnp.max(scores, -1, keepdims=True))
        weights = jnp.exp(scores - row_max)
        prob_rows = low(weights / lax.optimization_barrier(jnp.sum(weights, -1, keepdims=True)))
        return jnp.einsum('agqk,akd->agqd', prob_rows, value_heads, precision=lax.Precision.HIGHEST)
    blocks = lax.map(jax.checkpoint(one_block), jnp.arange(length // block_rows, dtype=jnp.int32))
    return blocks.transpose(0, 3, 1, 2, 4).reshape(length, H * HD)

def layer(inputs, attn_gain, query_weight, key_weight, value_weight, output_weight, ffn_gain, gate_weight, up_weight, down_weight):
    length = inputs.shape[0]
    positions = jnp.arange(length, dtype=jnp.int32).astype(inputs.dtype)
    cosine_table, sine_table = rope_tables(positions, HD)
    normed = low(rms_scale(inputs, attn_gain))
    query_lin = low_back(matmul_high(normed, query_weight)).reshape(length, H, HD)
    key_lin = low_back(matmul_high(normed, key_weight)).reshape(length, KV, HD)
    value_rows = low_back(low(matmul_high(normed, value_weight))).reshape(length, KV, HD)
    queries = low(rotate_pairs(query_lin, cosine_table, sine_table) * (1.0 / math.sqrt(HD)))
    key_rows = low(rotate_pairs(key_lin, cosine_table, sine_table))
    attended = low_back(low(attend(queries, key_rows, value_rows)))
    middle = inputs + low_back(matmul_high(attended, output_weight))
    normed_ffn = low(rms_scale(middle, ffn_gain))
    gate_rows = low_back(matmul_high(normed_ffn, gate_weight))
    up_rows = low_back(matmul_high(normed_ffn, up_weight))
    hidden = low(jax.nn.silu(gate_rows) * up_rows)
    return middle + low_back(matmul_high(hidden, down_weight))

def reference(tokens, attn_gain, query_weight, key_weight, value_weight, output_weight, ffn_gain, gate_weight, up_weight, down_weight, out_grad):
    params = tuple((weight_arr.astype(jnp.float32) for weight_arr in (attn_gain, query_weight, key_weight, value_weight, output_weight, ffn_gain, gate_weight, up_weight, down_weight)))

    def whole(inputs, *weights):
        return lax.map(lambda sequence: layer(sequence, *weights), inputs)
    outputs, pullback = jax.vjp(whole, tokens.astype(jnp.float32), *params)
    gradients = pullback(out_grad.astype(jnp.float32))
    return (outputs.astype(jnp.bfloat16), gradients[0].astype(jnp.bfloat16), gradients[1], gradients[2], gradients[3], gradients[4], gradients[5], gradients[6], gradients[7], gradients[8], gradients[9])
```

```python
import functools
import math

import jax
import jax.numpy as jnp
from jax import lax
from jax.experimental import pallas as pl
from jax.experimental.pallas import tpu as pltpu
from jax.sharding import PartitionSpec as P

H = 9
KV = 3
HD = 64
GROUPS = H // KV
KVW = KV * HD

EPS = 1e-05
THETA = 100000.0
NEGATIVE = -1e30
LANES = 128
FF_STEP = 256
VMEM_LIMIT = 60 * 1024 * 1024

BF16 = jnp.bfloat16
F32 = jnp.float32

SMEM_SPEC = pl.BlockSpec(memory_space=pltpu.SMEM)
VMEM_SPEC = pl.BlockSpec(memory_space=pltpu.VMEM)


def mm(left, right, left_dim=1, right_dim=0):
    return lax.dot_general(
        left, right, (((left_dim,), (right_dim,)), ((), ())), preferred_element_type=F32
    )


def call(kernel, outs, args, scratch=(), flops=0, moved=0, smem=0):
    return pl.pallas_call(
        kernel,
        out_shape=outs,
        in_specs=[SMEM_SPEC] * smem + [VMEM_SPEC] * (len(args) - smem),
        out_specs=jax.tree.map(lambda _: VMEM_SPEC, outs),
        scratch_shapes=list(scratch),
        compiler_params=pltpu.CompilerParams(vmem_limit_bytes=VMEM_LIMIT),
        cost_estimate=pl.CostEstimate(flops=flops, bytes_accessed=moved, transcendentals=0),
    )(*args)


def shaped(shape, dtype):
    return jax.ShapeDtypeStruct(tuple(shape), dtype)


def swap_halves(part):
    lane = lax.broadcasted_iota(jnp.int32, part.shape, 1)
    return jnp.where(
        lane % HD < HD // 2,
        pltpu.roll(part, LANES - HD // 2, axis=1),
        pltpu.roll(part, HD // 2, axis=1),
    )


def rotated(values, cosine, signed_sine, sign):
    rows, width = values.shape
    parts = []
    for start in range(0, width, LANES):
        part = values[:, start : start + LANES]
        used = part.shape[1]
        if used < LANES:
            part = jnp.concatenate([part, jnp.zeros((rows, LANES - used), F32)], -1)
        turned = part * cosine + sign * (swap_halves(part) * signed_sine)
        parts.append(turned[:, :used])
    return jnp.concatenate(parts, -1)


def stacked_heads(ref, group):
    first = group * GROUPS
    return jnp.concatenate(
        [ref[:, (first + g) * HD : (first + g + 1) * HD] for g in range(GROUPS)], 0
    )


def kv_kernel(tokens, gain, weight, cosine, sine, normed_out, kv_out):
    values = tokens[...].astype(F32)
    scale = lax.rsqrt(jnp.mean(values * values, -1, keepdims=True) + EPS)
    normed = (values * scale * gain[...]).astype(BF16)
    normed_out[...] = normed
    linear = mm(normed, weight[...])
    kv_out[:, :KVW] = rotated(linear[:, :KVW], cosine[...], sine[...], 1.0).astype(BF16)
    kv_out[:, KVW:] = linear[:, KVW:].astype(BF16)


def query_kernel(normed, weight, cosine, sine, query_out):
    linear = mm(normed[...], weight[...])
    turned = rotated(linear, cosine[...], sine[...], 1.0) * (1.0 / math.sqrt(HD))
    query_out[...] = turned.astype(BF16)


def causal(scores, rows):
    key_pos = lax.broadcasted_iota(jnp.int32, scores.shape, 0)
    query_pos = lax.broadcasted_iota(jnp.int32, scores.shape, 1) % rows
    return jnp.where(query_pos >= key_pos, scores, NEGATIVE)


def forward_kernel(index, queries, kv_all, attended, lse_out, q_scr, acc_scr, max_scr, sum_scr):
    rows = queries.shape[0]
    here = index[0]
    for group in range(KV):
        q_scr[group] = stacked_heads(queries, group)
    acc_scr[...] = jnp.zeros_like(acc_scr)
    max_scr[...] = jnp.full_like(max_scr, NEGATIVE)
    sum_scr[...] = jnp.zeros_like(sum_scr)

    def block(j, masked):
        keys_at = pl.ds(pl.multiple_of(j * rows, rows), rows)
        for group in range(KV):
            keys = kv_all[keys_at, group * HD : (group + 1) * HD]
            values = kv_all[keys_at, KVW + group * HD : KVW + (group + 1) * HD]
            scores = mm(keys, q_scr[group], 1, 1)
            if masked:
                scores = causal(scores, rows)
            old_max = max_scr[group, 0:1, :]
            new_max = jnp.maximum(old_max, jnp.max(scores, 0, keepdims=True))
            weights = jnp.exp(scores - new_max)
            factor = jnp.exp(old_max - new_max)
            max_scr[group, 0:1, :] = new_max
            sum_scr[group, 0:1, :] = sum_scr[group, 0:1, :] * factor + jnp.sum(
                weights, 0, keepdims=True
            )
            acc_scr[group] = acc_scr[group] * factor + mm(values, weights.astype(BF16), 0, 0)

    def step(j, carry):
        block(j, False)
        return carry

    lax.fori_loop(0, here, step, 0)
    block(here, True)
    lse_out[...] = jnp.zeros_like(lse_out)
    for group in range(KV):
        total = sum_scr[group, 0:1, :]
        result = acc_scr[group] / total
        lse_out[group : group + 1, :] = max_scr[group, 0:1, :] + jnp.log(total)
        for g in range(GROUPS):
            head = group * GROUPS + g
            attended[:, head * HD : (head + 1) * HD] = result[:, g * rows : (g + 1) * rows].T


def rms_back(values, gain, grad):
    width = values.shape[-1]
    scale = lax.rsqrt(jnp.mean(values * values, -1, keepdims=True) + EPS)
    scaled = values * scale
    pulled = grad * gain
    along = jnp.sum(pulled * scaled, -1, keepdims=True) * (1.0 / width)
    return scale * (pulled - scaled * along), grad * scaled


def put_tiles(out, first_tile, first_row_width, grad):
    owners = out.shape[0]
    rows = grad.shape[0] // owners
    for tile in range(grad.shape[1] // LANES):
        part = grad[:, tile * LANES : (tile + 1) * LANES].astype(BF16)
        for owner in range(owners):
            start = first_row_width + (first_tile + tile) * rows
            out[owner, pl.ds(start, rows), :] = part[owner * rows : (owner + 1) * rows]


def ffn_kernel(
    tokens, attended, out_weight, gain, in_weight, down_weight, out_grad,
    layer_out, middle_grad_out, attended_grad_out, big_grads, out_weight_grad, gain_grad,
    result_scr, back_scr, hidden_grad_scr,
):
    ff = down_weight.shape[0]
    owners = big_grads.shape[0]
    in_rows = in_weight.shape[0] // owners
    down_rows = ff // owners
    steps = ff // FF_STEP
    attended_low = attended[...].astype(BF16)
    middle = tokens[...].astype(F32) + mm(attended_low, out_weight[...])
    scale = lax.rsqrt(jnp.mean(middle * middle, -1, keepdims=True) + EPS)
    normed = (middle * scale * gain[...]).astype(BF16)
    grad_rows = out_grad[...]
    result_scr[...] = middle
    back_scr[...] = jnp.zeros_like(back_scr)
    tiles_per_step = FF_STEP // LANES
    width = grad_rows.shape[1]
    down_base = 2 * (ff // LANES) * in_rows

    for step in range(steps):
        gate_at = slice(step * FF_STEP, (step + 1) * FF_STEP)
        up_at = slice(ff + step * FF_STEP, ff + (step + 1) * FF_STEP)
        gate = mm(normed, in_weight[:, gate_at])
        up = mm(normed, in_weight[:, up_at])
        gated = 1.0 / (1.0 + jnp.exp(-gate))
        silu = gate * gated
        hidden = (silu * up).astype(BF16)
        down = down_weight[gate_at, :]
        result_scr[...] += mm(hidden, down)
        hidden_grad = mm(grad_rows, down, 1, 1)
        gate_grad = (hidden_grad * up * (gated * (1.0 + gate * (1.0 - gated)))).astype(BF16)
        up_grad = (hidden_grad * silu).astype(BF16)
        back_scr[...] += mm(gate_grad, in_weight[:, gate_at], 1, 1) + mm(
            up_grad, in_weight[:, up_at], 1, 1
        )
        put_tiles(big_grads, step * tiles_per_step, 0, mm(normed, gate_grad, 0, 0))
        put_tiles(big_grads, ff // LANES + step * tiles_per_step, 0, mm(normed, up_grad, 0, 0))
        hidden_grad_scr[gate_at, :] = mm(hidden, grad_rows, 0, 0)

    whole = width // LANES
    put_tiles(big_grads, 0, down_base, hidden_grad_scr[:, : whole * LANES])
    half = down_rows // 2
    for owner in range(owners):
        rest = hidden_grad_scr[owner * down_rows : (owner + 1) * down_rows, whole * LANES :]
        rest = jnp.concatenate([rest[:half], rest[half:]], -1).astype(BF16)
        big_grads[owner, pl.ds(down_base + whole * down_rows, half), :] = rest

    layer_out[...] = result_scr[...].astype(BF16)
    middle_back, gain_terms = rms_back(middle, gain[...], back_scr[...])
    gain_grad[...] = jnp.sum(gain_terms, 0, keepdims=True)
    middle_grad = middle_back + grad_rows.astype(F32)
    middle_grad_out[...] = middle_grad
    branch = middle_grad.astype(BF16)
    out_weight_grad[...] = mm(attended_low, branch, 0, 0).astype(BF16)
    attended_grad_out[...] = mm(branch, out_weight[...], 1, 1).astype(BF16)


def backward_kernel(
    index, queries, kv_all, attended, attended_grad, lse, normed, query_weight, cosine, sine,
    kv_grads, query_weight_grad, normed_grad,
    q_scr, g_scr, delta_scr, acc_scr, query_grad_scr,
):
    rows = queries.shape[0]
    blocks = kv_all.shape[0] // rows
    here = index[0]
    for group in range(KV):
        q_scr[group] = stacked_heads(queries, group)
        grads = stacked_heads(attended_grad, group)
        g_scr[group] = grads
        terms = (grads.astype(F32) * stacked_heads(attended, group)).T
        delta_scr[group, 0:1, :] = jnp.sum(terms, 0, keepdims=True)
    acc_scr[...] = jnp.zeros_like(acc_scr)

    def block(j, masked):
        keys_at = pl.ds(pl.multiple_of(j * rows, rows), rows)
        for group in range(KV):
            key_lanes = slice(group * HD, (group + 1) * HD)
            value_lanes = slice(KVW + group * HD, KVW + (group + 1) * HD)
            keys = kv_all[keys_at, key_lanes]
            values = kv_all[keys_at, value_lanes]
            group_q = q_scr[group]
            group_g = g_scr[group]
            scores = mm(keys, group_q, 1, 1)
            if masked:
                scores = causal(scores, rows)
            prob = jnp.exp(scores - lse[group : group + 1, :])
            prob_grad = mm(values, group_g, 1, 1)
            score_grad = (prob * (prob_grad - delta_scr[group, 0:1, :])).astype(BF16)
            kv_grads[keys_at, value_lanes] = mm(prob.astype(BF16), group_g).astype(BF16)
            kv_grads[keys_at, key_lanes] = mm(score_grad, group_q).astype(BF16)
            acc_scr[group] += mm(keys, score_grad, 0, 0)

    def step(j, carry):
        block(j, False)
        return carry

    def clear(j, carry):
        keys_at = pl.ds(pl.multiple_of(j * rows, rows), rows)
        kv_grads[keys_at, :] = jnp.zeros((rows, kv_grads.shape[1]), BF16)
        return carry

    lax.fori_loop(0, here, step, 0)
    block(here, True)
    lax.fori_loop(here + 1, blocks, clear, 0)
    for group in range(KV):
        for g in range(GROUPS):
            head = group * GROUPS + g
            part = acc_scr[group, :, g * rows : (g + 1) * rows]
            query_grad_scr[:, head * HD : (head + 1) * HD] = part.T
    back = rotated(query_grad_scr[...], cosine[...], sine[...], -1.0) * (1.0 / math.sqrt(HD))
    back = back.astype(BF16)
    query_weight_grad[...] = mm(normed[...], back, 0, 0).astype(BF16)
    normed_grad[...] = mm(back, query_weight[...], 1, 1)


def tail_kernel(
    kv_parts, tokens, gain, normed, normed_grad, middle_grad, kv_weight, cosine, sine,
    tokens_grad, kv_weight_grad, gain_grad,
):
    rows = tokens.shape[0]
    parts = kv_parts.shape[0] // rows

    def add(j, total):
        return total + kv_parts[pl.ds(pl.multiple_of(j * rows, rows), rows), :].astype(F32)

    kv_grad = lax.fori_loop(0, parts, add, jnp.zeros((rows, 2 * KVW), F32))
    key_back = rotated(kv_grad[:, :KVW], cosine[...], sine[...], -1.0)
    back = jnp.concatenate([key_back, kv_grad[:, KVW:]], -1).astype(BF16)
    kv_weight_grad[...] = mm(normed[...], back, 0, 0).astype(BF16)
    total = normed_grad[...] + mm(back, kv_weight[...], 1, 1)
    values = tokens[...].astype(F32)
    input_grad, gain_terms = rms_back(values, gain[...], total)
    gain_grad[...] = jnp.sum(gain_terms, 0, keepdims=True)
    tokens_grad[...] = (middle_grad[...] + input_grad).astype(BF16)


def swap(value, axis, bit):
    count = lax.axis_size(axis)
    return lax.ppermute(value, axis, [(i, i ^ (1 << bit)) for i in range(count)])


def own_bit(axis, bit):
    return (lax.axis_index(axis) >> bit) & 1


def halved(value, axis, bit, dim):
    mine = own_bit(axis, bit)
    keep = lax.dynamic_index_in_dim(value, mine, dim, keepdims=False)
    send = lax.dynamic_index_in_dim(value, 1 - mine, dim, keepdims=False)
    got = swap(send, axis, bit)
    return (keep.astype(F32) + got.astype(F32)).astype(value.dtype)


def doubled(value, axis, bit, dim):
    mine = own_bit(axis, bit)
    got = swap(value, axis, bit)
    low = jnp.where(mine == 0, value, got)
    high = jnp.where(mine == 0, got, value)
    return jnp.stack([low, high], dim)


def scattered_ws(value):
    split = value.reshape((2, 2) + value.shape[1:])
    return halved(halved(split, "ws", 0, 1), "ws", 1, 0)


def summed_ctx(value, high_first):
    count = lax.axis_size("ctx")
    bits = count.bit_length() - 1
    rows = value.shape[0]
    split = value.reshape((2,) * bits + (rows // count, value.shape[1]))
    order = list(range(bits))
    if high_first:
        order.reverse()
    left = list(range(bits - 1, -1, -1))
    dims = []
    for bit in order:
        dim = left.index(bit)
        left.pop(dim)
        dims.append(dim)
        split = halved(split, "ctx", bit, dim)
    for bit, dim in zip(reversed(order), reversed(dims)):
        split = doubled(split, "ctx", bit, dim)
    return split.reshape(rows, value.shape[1])


def untiled(tiles, rows):
    count = tiles.shape[0] // rows
    return jnp.concatenate([tiles[i * rows : (i + 1) * rows] for i in range(count)], -1)


def by_owner(grad, owners):
    rows = grad.shape[0] // owners
    split = grad.reshape(owners, rows, grad.shape[1])
    return jnp.concatenate(
        [split[:, :, at : at + LANES] for at in range(0, grad.shape[1], LANES)], 1
    )


def body(
    tokens,
    attn_gain,
    query_weight,
    key_weight,
    value_weight,
    output_weight,
    ffn_gain,
    gate_weight,
    up_weight,
    down_weight,
    out_grad,
):
    seq_count, rows, width = tokens.shape
    ctx_count = lax.axis_size("ctx")
    owners = lax.axis_size("ws")
    ctx_index = lax.axis_index("ctx")
    slice_rows = query_weight.shape[0]
    ff = gate_weight.shape[1]
    tokens = tokens.reshape(rows, width)
    out_grad = out_grad.reshape(rows, width)
    index = jnp.full((1,), ctx_index, jnp.int32)

    gains = jnp.stack([attn_gain, ffn_gain], -1)
    packed = jnp.concatenate(
        [key_weight, value_weight, jnp.pad(gains, ((0, 0), (0, LANES - 2)))], -1
    )
    kv_full = lax.all_gather(packed, "ws", axis=0, tiled=True)
    full_query = lax.all_gather(query_weight, "ws", axis=0, tiled=True)
    full_output = lax.all_gather(output_weight, "ws", axis=0, tiled=True)
    full_in = lax.all_gather(
        jnp.concatenate([gate_weight, up_weight], -1), "ws", axis=0, tiled=True
    )
    full_down = lax.all_gather(down_weight, "ws", axis=0, tiled=True)
    full_kv = kv_full[:, : 2 * KVW]
    gain_rows = kv_full[:, 2 * KVW : 2 * KVW + 2].T.astype(F32)
    gain_attn = gain_rows[0:1]
    gain_ffn = gain_rows[1:2]

    positions = (ctx_index * rows + jnp.arange(rows, dtype=jnp.int32)).astype(F32)
    frequency = jnp.exp(jnp.arange(HD // 2).astype(F32) * (-2.0 * math.log(THETA) / HD))
    angles = positions[:, None] * frequency[None, :]
    cosine = jnp.cos(angles)
    sine = jnp.sin(angles)
    cosine = jnp.concatenate([cosine] * 4, -1)
    sine = jnp.concatenate([-sine, sine] * 2, -1)

    normed, kv_own = call(
        kv_kernel,
        (shaped((rows, width), BF16), shaped((rows, 2 * KVW), BF16)),
        (tokens, gain_attn, full_kv, cosine, sine),
        flops=2 * rows * width * 2 * KVW,
    )
    queries = call(
        query_kernel,
        shaped((rows, width), BF16),
        (normed, full_query, cosine, sine),
        flops=2 * rows * width * width,
    )
    kv_all = lax.all_gather(kv_own, "ctx", axis=0, tiled=True)

    attended, lse = call(
        forward_kernel,
        (shaped((rows, width), F32), shaped((8, GROUPS * rows), F32)),
        (index, queries, kv_all),
        scratch=(
            pltpu.VMEM((KV, GROUPS * rows, HD), BF16),
            pltpu.VMEM((KV, HD, GROUPS * rows), F32),
            pltpu.VMEM((KV, 8, GROUPS * rows), F32),
            pltpu.VMEM((KV, 8, GROUPS * rows), F32),
        ),
        flops=4 * rows * ctx_count * rows * width,
        smem=1,
    )

    tile_rows = (2 * slice_rows * ff + (ff // owners) * width) // LANES
    layer_out, middle_grad, attended_grad, big_grads, output_weight_grad, ffn_gain_grad = call(
        ffn_kernel,
        (
            shaped((rows, width), BF16),
            shaped((rows, width), F32),
            shaped((rows, width), BF16),
            shaped((owners, tile_rows, LANES), BF16),
            shaped((width, width), BF16),
            shaped((1, width), F32),
        ),
        (tokens, attended, full_output, gain_ffn, full_in, full_down, out_grad),
        scratch=(
            pltpu.VMEM((rows, width), F32),
            pltpu.VMEM((rows, width), F32),
            pltpu.VMEM((ff, width), F32),
        ),
        flops=18 * rows * width * ff,
    )

    big_slice = scattered_ws(big_grads)

    kv_grads, query_weight_grad, normed_grad = call(
        backward_kernel,
        (
            shaped((ctx_count * rows, 2 * KVW), BF16),
            shaped((width, width), BF16),
            shaped((rows, width), F32),
        ),
        (
            index, queries, kv_all, attended, attended_grad, lse, normed, full_query, cosine, sine,
        ),
        scratch=(
            pltpu.VMEM((KV, GROUPS * rows, HD), BF16),
            pltpu.VMEM((KV, GROUPS * rows, HD), BF16),
            pltpu.VMEM((KV, 8, GROUPS * rows), F32),
            pltpu.VMEM((KV, HD, GROUPS * rows), F32),
            pltpu.VMEM((rows, width), F32),
        ),
        flops=10 * rows * ctx_count * rows * width,
        smem=1,
    )

    kv_parts = lax.all_to_all(kv_grads, "ctx", split_axis=0, concat_axis=0, tiled=True)
    tokens_grad, kv_weight_grad, attn_gain_grad = call(
        tail_kernel,
        (
            shaped((rows, width), BF16),
            shaped((width, 2 * KVW), BF16),
            shaped((1, width), F32),
        ),
        (
            kv_parts, tokens, gain_attn, normed, normed_grad, middle_grad, full_kv, cosine, sine,
        ),
        flops=4 * rows * width * 2 * KVW,
    )

    big_total = summed_ctx(big_slice, True)
    gain_tile = jnp.concatenate([attn_gain_grad, ffn_gain_grad], 0).astype(BF16)
    gain_tile = gain_tile.reshape(2, owners, slice_rows).transpose(1, 0, 2).reshape(owners, -1)
    gain_tile = jnp.pad(gain_tile, ((0, 0), (0, 64 * LANES - 2 * slice_rows)))
    small_grads = jnp.concatenate(
        [
            by_owner(
                jnp.concatenate([query_weight_grad, output_weight_grad, kv_weight_grad], -1),
                owners,
            ),
            gain_tile.reshape(owners, 64, LANES),
        ],
        1,
    )
    small_total = summed_ctx(scattered_ws(small_grads), False)

    in_rows = ff // LANES * slice_rows
    down_rows = ff // owners
    whole = width // LANES
    gate_weight_grad = untiled(big_total[:in_rows], slice_rows)
    up_weight_grad = untiled(big_total[in_rows : 2 * in_rows], slice_rows)
    down_tiles = big_total[2 * in_rows :]
    rest = down_tiles[whole * down_rows :]
    half = LANES // 2
    down_weight_grad = jnp.concatenate(
        [
            untiled(down_tiles[: whole * down_rows], down_rows),
            jnp.concatenate([rest[:, :half], rest[:, half:]], 0),
        ],
        -1,
    )
    small = untiled(small_total[:-64], slice_rows)
    gain_out = small_total[-64:].reshape(-1)
    outs = (
        gain_out[:slice_rows],
        small[:, :width],
        small[:, 2 * width : 2 * width + KVW],
        small[:, 2 * width + KVW :],
        small[:, width : 2 * width],
        gain_out[slice_rows : 2 * slice_rows],
        gate_weight_grad,
        up_weight_grad,
        down_weight_grad,
    )
    return (
        layer_out.reshape(seq_count, rows, width),
        tokens_grad.reshape(seq_count, rows, width),
    ) + tuple(value.astype(F32) for value in outs)


def solution(mesh):
    in_specs = (
        P("ws", "ctx", None),
        P("ws"),
        P("ws", None),
        P("ws", None),
        P("ws", None),
        P("ws", None),
        P("ws"),
        P("ws", None),
        P("ws", None),
        P("ws", None),
        P("ws", "ctx", None),
    )
    out_specs = (
        P("ws", "ctx", None),
        P("ws", "ctx", None),
        P("ws"),
        P("ws", None),
        P("ws", None),
        P("ws", None),
        P("ws", None),
        P("ws"),
        P("ws", None),
        P("ws", None),
        P("ws", None),
    )
    return jax.shard_map(body, mesh=mesh, in_specs=in_specs, out_specs=out_specs, check_vma=False)
```

```python
import functools
import math

import jax
import jax.numpy as jnp
from jax import lax
from jax.experimental import pallas as pl
from jax.experimental.pallas import tpu as pltpu
from jax.sharding import PartitionSpec as P

H = 9
KV = 3
HD = 64
GROUPS = H // KV
KVW = KV * HD

EPS = 1e-05
THETA = 100000.0
NEGATIVE = -1e30
LANES = 128
FF_STEP = 256
VMEM_LIMIT = 60 * 1024 * 1024

BF16 = jnp.bfloat16
F32 = jnp.float32

SMEM_SPEC = pl.BlockSpec(memory_space=pltpu.SMEM)
VMEM_SPEC = pl.BlockSpec(memory_space=pltpu.VMEM)


def mm(left, right, left_dim=1, right_dim=0):
    return lax.dot_general(
        left, right, (((left_dim,), (right_dim,)), ((), ())), preferred_element_type=F32
    )


def call(kernel, outs, args, scratch=(), micros=1, smem=0):
    return pl.pallas_call(
        kernel,
        out_shape=outs,
        in_specs=[SMEM_SPEC] * smem + [VMEM_SPEC] * (len(args) - smem),
        out_specs=jax.tree.map(lambda _: VMEM_SPEC, outs),
        scratch_shapes=list(scratch),
        compiler_params=pltpu.CompilerParams(vmem_limit_bytes=VMEM_LIMIT),
        cost_estimate=pl.CostEstimate(
            flops=micros * 1_000_000_000, bytes_accessed=0, transcendentals=0
        ),
    )(*args)


def shaped(shape, dtype):
    return jax.ShapeDtypeStruct(tuple(shape), dtype)


def swap_halves(part):
    lane = lax.broadcasted_iota(jnp.int32, part.shape, 1)
    return jnp.where(
        lane % HD < HD // 2,
        pltpu.roll(part, LANES - HD // 2, axis=1),
        pltpu.roll(part, HD // 2, axis=1),
    )


def rotated(values, cosine, signed_sine, sign):
    rows, width = values.shape
    parts = []
    for start in range(0, width, LANES):
        part = values[:, start : start + LANES]
        used = part.shape[1]
        if used < LANES:
            part = jnp.concatenate([part, jnp.zeros((rows, LANES - used), F32)], -1)
        turned = part * cosine + sign * (swap_halves(part) * signed_sine)
        parts.append(turned[:, :used])
    return jnp.concatenate(parts, -1)


def stacked_heads(ref, group):
    first = group * GROUPS
    return jnp.concatenate(
        [ref[:, (first + g) * HD : (first + g + 1) * HD] for g in range(GROUPS)], 0
    )


def assembled(full, pieces, me):
    rows = pieces[0].shape[0]
    for relative, piece in enumerate(pieces):
        start = pl.multiple_of((me ^ relative) * rows, 16)
        full[pl.ds(start, rows), :] = piece[...]


def kv_kernel(
    tokens, packed, cosine, sine, normed_out, kv_out, weight_out, gains_out, owners, slice_rows
):
    step = packed.shape[0] // owners
    gains = []
    for owner in range(owners):
        start = owner * step
        weight_out[owner * slice_rows : (owner + 1) * slice_rows, :] = packed[
            start : start + slice_rows, :
        ]
        gains.append(packed[start + slice_rows : start + step, :slice_rows].astype(F32))
    gains = jnp.concatenate(gains, -1)
    gains_out[...] = gains[:8]
    values = tokens[...].astype(F32)
    scale = lax.rsqrt(jnp.mean(values * values, -1, keepdims=True) + EPS)
    normed = (values * scale * gains[0:1]).astype(BF16)
    normed_out[...] = normed
    linear = mm(normed, weight_out[...])
    kv_out[:, :KVW] = rotated(linear[:, :KVW], cosine[...], sine[...], 1.0).astype(BF16)
    kv_out[:, KVW:] = linear[:, KVW:].astype(BF16)


def query_kernel(index, normed, own, core, along, diagonal, cosine, sine, query_out, weight_out):
    assembled(weight_out, (own, core, along, diagonal), index[1])
    linear = mm(normed[...], weight_out[...])
    turned = rotated(linear, cosine[...], sine[...], 1.0) * (1.0 / math.sqrt(HD))
    query_out[...] = turned.astype(BF16)


def causal(scores, rows):
    key_pos = lax.broadcasted_iota(jnp.int32, scores.shape, 0)
    query_pos = lax.broadcasted_iota(jnp.int32, scores.shape, 1) % rows
    return jnp.where(query_pos >= key_pos, scores, NEGATIVE)


def forward_kernel(index, queries, *refs):
    pieces, (attended, lse_out, kv_all, q_scr, acc_scr, max_scr, sum_scr) = refs[:-7], refs[-7:]
    rows = queries.shape[0]
    here = index[0]
    if len(pieces) == 1:
        kv_all[...] = pieces[0][...]
    else:
        for place, piece in enumerate(pieces):
            owner = (here ^ (place % 2)) - 2 * (place // 2)

            @pl.when((owner >= 0) & (owner <= here))
            def _(owner=owner, piece=piece):
                kv_all[pl.ds(pl.multiple_of(owner * rows, rows), rows), :] = piece[...]

    for group in range(KV):
        q_scr[group] = stacked_heads(queries, group)
    acc_scr[...] = jnp.zeros_like(acc_scr)
    max_scr[...] = jnp.full_like(max_scr, NEGATIVE)
    sum_scr[...] = jnp.zeros_like(sum_scr)

    def block(j, masked):
        keys_at = pl.ds(pl.multiple_of(j * rows, rows), rows)
        for group in range(KV):
            keys = kv_all[keys_at, group * HD : (group + 1) * HD]
            values = kv_all[keys_at, KVW + group * HD : KVW + (group + 1) * HD]
            scores = mm(keys, q_scr[group], 1, 1)
            if masked:
                scores = causal(scores, rows)
            old_max = max_scr[group, 0:1, :]
            new_max = jnp.maximum(old_max, jnp.max(scores, 0, keepdims=True))
            weights = jnp.exp(scores - new_max)
            factor = jnp.exp(old_max - new_max)
            max_scr[group, 0:1, :] = new_max
            sum_scr[group, 0:1, :] = sum_scr[group, 0:1, :] * factor + jnp.sum(
                weights, 0, keepdims=True
            )
            acc_scr[group] = acc_scr[group] * factor + mm(values, weights.astype(BF16), 0, 0)

    def step(j, carry):
        block(j, False)
        return carry

    lax.fori_loop(0, here, step, 0)
    block(here, True)
    lse_out[...] = jnp.zeros_like(lse_out)
    for group in range(KV):
        total = sum_scr[group, 0:1, :]
        result = acc_scr[group] / total
        lse_out[group : group + 1, :] = max_scr[group, 0:1, :] + jnp.log(total)
        for g in range(GROUPS):
            head = group * GROUPS + g
            attended[:, head * HD : (head + 1) * HD] = result[:, g * rows : (g + 1) * rows].T


def rms_back(values, gain, grad):
    width = values.shape[-1]
    scale = lax.rsqrt(jnp.mean(values * values, -1, keepdims=True) + EPS)
    scaled = values * scale
    pulled = grad * gain
    along = jnp.sum(pulled * scaled, -1, keepdims=True) * (1.0 / width)
    return scale * (pulled - scaled * along), grad * scaled


def put_tiles(outs, me, grads, grad_lanes, first_row):
    rows = grads.shape[0] // len(outs)
    first, last = grad_lanes
    for relative, out in enumerate(outs):
        start = pl.multiple_of((me ^ relative) * rows, 16)
        for tile in range((last - first) // LANES):
            at = first + tile * LANES
            out[first_row + tile * rows : first_row + (tile + 1) * rows, :] = grads[
                pl.ds(start, rows), at : at + LANES
            ]


def ffn_kernel(
    index, tokens, attended, gains, out_grad,
    wo0, wo1, wo2, wo3, wi0, wi1, wi2, wi3, wd0, wd1, wd2, wd3,
    layer_out, middle_grad_out, attended_grad_out, mine, along, send, gain_grad,
    out_weight, in_weight, down_weight, result_scr, back_scr, tile_scr, down_scr,
):
    me = index[1]
    assembled(out_weight, (wo0, wo1, wo2, wo3), me)
    assembled(in_weight, (wi0, wi1, wi2, wi3), me)
    assembled(down_weight, (wd0, wd1, wd2, wd3), me)
    outs = (mine, send.at[0], along, send.at[1])
    gain = gains[1:2, :]
    ff = down_weight.shape[0]
    owners = len(outs)
    in_rows = in_weight.shape[0] // owners
    down_rows = ff // owners
    attended_low = attended[...].astype(BF16)
    middle = tokens[...].astype(F32) + mm(attended_low, out_weight[...])
    scale = lax.rsqrt(jnp.mean(middle * middle, -1, keepdims=True) + EPS)
    normed = (middle * scale * gain).astype(BF16)
    grad_rows = out_grad[...]
    result_scr[...] = middle
    back_scr[...] = jnp.zeros_like(back_scr)
    width = grad_rows.shape[1]

    for step in range(ff // FF_STEP):
        gate_at = slice(step * FF_STEP, (step + 1) * FF_STEP)
        up_at = slice(ff + step * FF_STEP, ff + (step + 1) * FF_STEP)
        gate = mm(normed, in_weight[:, gate_at])
        up = mm(normed, in_weight[:, up_at])
        gated = 1.0 / (1.0 + jnp.exp(-gate))
        silu = gate * gated
        hidden = (silu * up).astype(BF16)
        down = down_weight[gate_at, :]
        result_scr[...] += mm(hidden, down)
        hidden_grad = mm(grad_rows, down, 1, 1)
        gate_grad = (hidden_grad * up * (gated * (1.0 + gate * (1.0 - gated)))).astype(BF16)
        up_grad = (hidden_grad * silu).astype(BF16)
        back_scr[...] += mm(gate_grad, in_weight[:, gate_at], 1, 1) + mm(
            up_grad, in_weight[:, up_at], 1, 1
        )
        tile_scr[:, gate_at] = mm(normed, gate_grad, 0, 0).astype(BF16)
        tile_scr[:, up_at] = mm(normed, up_grad, 0, 0).astype(BF16)
        down_scr[gate_at, :width] = mm(hidden, grad_rows, 0, 0).astype(BF16)

    put_tiles(outs, me, tile_scr, (0, 2 * ff), 0)
    base = 2 * (ff // LANES) * in_rows
    whole = width // LANES * LANES
    put_tiles(outs, me, down_scr, (0, whole), base)
    base += whole // LANES * down_rows
    half = down_rows // 2
    for relative, out in enumerate(outs):
        start = pl.multiple_of((me ^ relative) * down_rows, 16)
        rest = jnp.concatenate(
            [
                down_scr[pl.ds(start, half), whole:width],
                down_scr[pl.ds(pl.multiple_of(start + half, 16), half), whole:width],
            ],
            -1,
        )
        out[base : base + half, :] = rest
    base += half

    layer_out[...] = result_scr[...].astype(BF16)
    middle_back, gain_terms = rms_back(middle, gain, back_scr[...])
    gain_grad[...] = jnp.zeros_like(gain_grad)
    gain_grad[0:1, :] = jnp.sum(gain_terms, 0, keepdims=True)
    middle_grad = middle_back + grad_rows.astype(F32)
    middle_grad_out[...] = middle_grad
    branch = middle_grad.astype(BF16)
    attended_grad_out[...] = mm(branch, out_weight[...], 1, 1).astype(BF16)
    out_weight_grad = mm(attended_low, branch, 0, 0).astype(BF16)
    wide = -(-width // LANES) * LANES
    tile_scr[:, :wide] = jnp.concatenate(
        [out_weight_grad, jnp.zeros((width, wide - width), BF16)], -1
    )
    put_tiles(outs, me, tile_scr, (0, wide), base)
    base += wide // LANES * in_rows
    for out in outs:
        out[base:, :] = jnp.zeros((out.shape[0] - base, LANES), BF16)


def backward_kernel(
    index, queries, kv_all, attended, attended_grad, lse, normed, query_weight, cosine, sine,
    kv_grads, query_weight_grad, normed_grad,
    q_scr, g_scr, delta_scr, acc_scr, query_grad_scr,
):
    rows = queries.shape[0]
    blocks = kv_all.shape[0] // rows
    here = index[0]
    for group in range(KV):
        q_scr[group] = stacked_heads(queries, group)
        grads = stacked_heads(attended_grad, group)
        g_scr[group] = grads
        terms = (grads.astype(F32) * stacked_heads(attended, group)).T
        delta_scr[group, 0:1, :] = jnp.sum(terms, 0, keepdims=True)
    acc_scr[...] = jnp.zeros_like(acc_scr)

    def block(j, masked):
        keys_at = pl.ds(pl.multiple_of(j * rows, rows), rows)
        for group in range(KV):
            key_lanes = slice(group * HD, (group + 1) * HD)
            value_lanes = slice(KVW + group * HD, KVW + (group + 1) * HD)
            keys = kv_all[keys_at, key_lanes]
            values = kv_all[keys_at, value_lanes]
            group_q = q_scr[group]
            group_g = g_scr[group]
            scores = mm(keys, group_q, 1, 1)
            if masked:
                scores = causal(scores, rows)
            prob = jnp.exp(scores - lse[group : group + 1, :])
            prob_grad = mm(values, group_g, 1, 1)
            score_grad = (prob * (prob_grad - delta_scr[group, 0:1, :])).astype(BF16)
            kv_grads[keys_at, value_lanes] = mm(prob.astype(BF16), group_g).astype(BF16)
            kv_grads[keys_at, key_lanes] = mm(score_grad, group_q).astype(BF16)
            acc_scr[group] += mm(keys, score_grad, 0, 0)

    def step(j, carry):
        block(j, False)
        return carry

    def clear(j, carry):
        keys_at = pl.ds(pl.multiple_of(j * rows, rows), rows)
        kv_grads[keys_at, :] = jnp.zeros((rows, kv_grads.shape[1]), BF16)
        return carry

    lax.fori_loop(0, here, step, 0)
    block(here, True)
    lax.fori_loop(here + 1, blocks, clear, 0)
    for group in range(KV):
        for g in range(GROUPS):
            head = group * GROUPS + g
            part = acc_scr[group, :, g * rows : (g + 1) * rows]
            query_grad_scr[:, head * HD : (head + 1) * HD] = part.T
    back = rotated(query_grad_scr[...], cosine[...], sine[...], -1.0) * (1.0 / math.sqrt(HD))
    back = back.astype(BF16)
    query_weight_grad[...] = mm(normed[...], back, 0, 0).astype(BF16)
    normed_grad[...] = mm(back, query_weight[...], 1, 1)


def tail_kernel(
    index, kv_parts, tokens, gains, normed, normed_grad, middle_grad, kv_weight, query_weight_grad,
    ffn_gain_grad, cosine, sine,
    tokens_grad, mine, along, send,
    tile_scr,
):
    me = index[1]
    rows, width = tokens.shape
    parts = kv_parts.shape[0] // rows

    def add(j, total):
        return total + kv_parts[pl.ds(pl.multiple_of(j * rows, rows), rows), :].astype(F32)

    kv_grad = lax.fori_loop(0, parts, add, jnp.zeros((rows, 2 * KVW), F32))
    key_back = rotated(kv_grad[:, :KVW], cosine[...], sine[...], -1.0)
    back = jnp.concatenate([key_back, kv_grad[:, KVW:]], -1).astype(BF16)
    wide = -(-width // LANES) * LANES
    tile_scr[:, wide : wide + 2 * KVW] = mm(normed[...], back, 0, 0).astype(BF16)
    total = normed_grad[...] + mm(back, kv_weight[...], 1, 1)
    values = tokens[...].astype(F32)
    input_grad, gain_terms = rms_back(values, gains[0:1, :], total)
    tokens_grad[...] = (middle_grad[...] + input_grad).astype(BF16)
    gain_grads = jnp.concatenate(
        [jnp.sum(gain_terms, 0, keepdims=True), ffn_gain_grad[0:1, :], jnp.zeros((6, width), F32)], 0
    )
    columns = jnp.concatenate([gain_grads.T, jnp.zeros((width, wide - width - 8), F32)], -1)
    tile_scr[:, :wide] = jnp.concatenate([query_weight_grad[...], columns.astype(BF16)], -1)
    outs = (mine, send.at[0], along, send.at[1])
    put_tiles(outs, me, tile_scr, (0, wide + 2 * KVW), 0)


def flattened(index, pieces, flat):
    if len(pieces) == 1:
        flat[...] = pieces[0][...]
        return
    here = index[0]
    count = len(pieces)
    rows = pieces[0].shape[0]
    for place, piece in enumerate(pieces):
        owner = ((here ^ (place % 2)) + (count - 2 * (place // 2))) % count
        flat[pl.ds(pl.multiple_of(owner * rows, 16), rows), :] = piece[...]


def big_out_kernel(index, *refs):
    pieces, (gate_out, up_out, down_out, out_out, flat) = refs[:-5], refs[-5:]
    flattened(index, pieces, flat)
    base = 0
    for out in (gate_out, up_out):
        rows = out.shape[0]
        for tile in range(out.shape[1] // LANES):
            out[:, tile * LANES : (tile + 1) * LANES] = flat[base : base + rows, :].astype(F32)
            base += rows
    rows, width = down_out.shape
    whole = width // LANES
    for tile in range(whole):
        down_out[:, tile * LANES : (tile + 1) * LANES] = flat[base : base + rows, :].astype(F32)
        base += rows
    half = rows // 2
    rest = flat[base : base + half, :].astype(F32)
    down_out[:half, whole * LANES :] = rest[:, : width - whole * LANES]
    down_out[half:, whole * LANES :] = rest[:, width - whole * LANES :]
    base += half
    rows = out_out.shape[0]
    for tile in range(whole):
        out_out[:, tile * LANES : (tile + 1) * LANES] = flat[base : base + rows, :].astype(F32)
        base += rows
    out_out[:, whole * LANES :] = flat[base : base + rows, : width - whole * LANES].astype(F32)


def small_out_kernel(index, *refs):
    pieces, (query_out, key_out, value_out, gain_out, flat) = refs[:-5], refs[-5:]
    flattened(index, pieces, flat)
    rows, width = query_out.shape
    whole = width // LANES
    tiles = [
        flat[tile * rows : (tile + 1) * rows, :].astype(F32) for tile in range(flat.shape[0] // rows)
    ]
    for tile in range(whole):
        query_out[:, tile * LANES : (tile + 1) * LANES] = tiles[tile]
    rest = width - whole * LANES
    query_out[:, whole * LANES :] = tiles[whole][:, :rest]
    gain_out[...] = tiles[whole][:, rest : rest + 8]
    both = jnp.concatenate(tiles[whole + 1 :], -1)
    key_out[...] = both[:, :KVW]
    value_out[...] = both[:, KVW : 2 * KVW]


def swap(value, axis, bit):
    count = lax.axis_size(axis)
    return lax.ppermute(value, axis, [(i, i ^ (1 << bit)) for i in range(count)])


def gathered_ws(value):
    along = swap(value, "ws", 1)
    return value, swap(value, "ws", 0), along, swap(along, "ws", 0)


def gathered_ctx(value, causal_only):
    count = lax.axis_size("ctx")
    if count != 8:
        return (lax.all_gather(value, "ctx", axis=0, tiled=True),)
    moved = [value]
    for by in (3, 2, 1):
        pairs = [(i, i + 2 * by) for i in range(count)]
        if causal_only:
            pairs = [(i, j) for i, j in pairs if j < count]
        moved.insert(1, lax.ppermute(value, "ctx", [(i, j % count) for i, j in pairs]))
    pieces = []
    for piece in moved:
        pieces += [piece, swap(piece, "ctx", 0)]
    return tuple(pieces)


def added(*values):
    total = values[0].astype(F32)
    for value in values[1:]:
        total = total + value.astype(F32)
    return total.astype(values[0].dtype)


def scattered_ctx(value):
    count = lax.axis_size("ctx")
    parts = lax.all_to_all(value, "ctx", split_axis=0, concat_axis=0, tiled=True)
    parts = parts.reshape(count, -1, LANES).astype(F32)
    return jnp.sum(parts, 0).astype(value.dtype)


def padded_rows(rows, count):
    return -(-rows // (16 * count)) * 16 * count


def body(
    tokens,
    attn_gain,
    query_weight,
    key_weight,
    value_weight,
    output_weight,
    ffn_gain,
    gate_weight,
    up_weight,
    down_weight,
    out_grad,
):
    seq_count, rows, width = tokens.shape
    ctx_count = lax.axis_size("ctx")
    owners = lax.axis_size("ws")
    slice_rows = query_weight.shape[0]
    ff = gate_weight.shape[1]
    wide = -(-width // LANES) * LANES
    tokens = tokens.reshape(rows, width)
    out_grad = out_grad.reshape(rows, width)
    ctx_index = lax.axis_index("ctx")
    index = jnp.stack([ctx_index, lax.axis_index("ws")]).astype(jnp.int32)

    gains = jnp.stack([attn_gain, ffn_gain])
    packed = jnp.concatenate(
        [
            jnp.concatenate([key_weight, value_weight], -1),
            jnp.pad(gains, ((0, 14), (0, 2 * KVW - slice_rows))),
        ],
        0,
    )
    packed = lax.all_gather(packed, "ws", axis=0, tiled=True)
    packed, query_weight, output_weight, in_weight, down_weight = lax.optimization_barrier(
        (
            packed,
            query_weight,
            output_weight,
            jnp.concatenate([gate_weight, up_weight], -1),
            down_weight,
        )
    )

    positions = (ctx_index * rows + jnp.arange(rows, dtype=jnp.int32)).astype(F32)
    frequency = jnp.exp(jnp.arange(HD // 2).astype(F32) * (-2.0 * math.log(THETA) / HD))
    angles = positions[:, None] * frequency[None, :]
    cosine = jnp.cos(angles)
    sine = jnp.sin(angles)
    cosine = jnp.concatenate([cosine] * 4, -1)
    sine = jnp.concatenate([-sine, sine] * 2, -1)

    normed, kv_own, full_kv, gains = call(
        functools.partial(kv_kernel, owners=owners, slice_rows=slice_rows),
        (
            shaped((rows, width), BF16),
            shaped((rows, 2 * KVW), BF16),
            shaped((width, 2 * KVW), BF16),
            shaped((8, width), F32),
        ),
        (tokens, packed, cosine, sine),
        micros=3,
    )
    query_pieces = gathered_ws(query_weight)
    kv_pieces = gathered_ctx(kv_own, True)
    out_pieces = gathered_ws(output_weight)
    in_pieces = gathered_ws(in_weight)
    down_pieces = gathered_ws(down_weight)

    queries, full_query = call(
        query_kernel,
        (shaped((rows, width), BF16), shaped((width, width), BF16)),
        (index, normed) + query_pieces + (cosine, sine),
        micros=3,
        smem=1,
    )
    attended, lse, kv_all = call(
        forward_kernel,
        (
            shaped((rows, width), F32),
            shaped((8, GROUPS * rows), F32),
            shaped((ctx_count * rows, 2 * KVW), BF16),
        ),
        (index, queries) + kv_pieces,
        scratch=(
            pltpu.VMEM((KV, GROUPS * rows, HD), BF16),
            pltpu.VMEM((KV, HD, GROUPS * rows), F32),
            pltpu.VMEM((KV, 8, GROUPS * rows), F32),
            pltpu.VMEM((KV, 8, GROUPS * rows), F32),
        ),
        micros=16,
        smem=1,
    )

    big_rows = (2 * slice_rows * ff + (ff // owners) * width + slice_rows * wide) // LANES
    big_rows = padded_rows(big_rows, ctx_count)
    layer_out, middle_grad, attended_grad, mine, along, send, ffn_gain_grad = call(
        ffn_kernel,
        (
            shaped((rows, width), BF16),
            shaped((rows, width), F32),
            shaped((rows, width), BF16),
            shaped((big_rows, LANES), BF16),
            shaped((big_rows, LANES), BF16),
            shaped((2, big_rows, LANES), BF16),
            shaped((8, width), F32),
        ),
        (index, tokens, attended, gains, out_grad) + out_pieces + in_pieces + down_pieces,
        scratch=(
            pltpu.VMEM((width, width), BF16),
            pltpu.VMEM((width, 2 * ff), BF16),
            pltpu.VMEM((ff, width), BF16),
            pltpu.VMEM((rows, width), F32),
            pltpu.VMEM((rows, width), F32),
            pltpu.VMEM((width, 2 * ff), BF16),
            pltpu.VMEM((ff, wide), BF16),
        ),
        micros=14,
        smem=1,
    )

    got = swap(send, "ws", 0)
    attended_grad, crossing = lax.optimization_barrier((attended_grad, added(along, got[1])))
    crossed = swap(crossing, "ws", 1)

    kv_grads, query_weight_grad, normed_grad = call(
        backward_kernel,
        (
            shaped((ctx_count * rows, 2 * KVW), BF16),
            shaped((width, width), BF16),
            shaped((rows, width), F32),
        ),
        (
            index, queries, kv_all, attended, attended_grad, lse, normed, full_query, cosine, sine,
        ),
        scratch=(
            pltpu.VMEM((KV, GROUPS * rows, HD), BF16),
            pltpu.VMEM((KV, GROUPS * rows, HD), BF16),
            pltpu.VMEM((KV, 8, GROUPS * rows), F32),
            pltpu.VMEM((KV, HD, GROUPS * rows), F32),
            pltpu.VMEM((rows, width), F32),
        ),
        micros=19,
        smem=1,
    )
    kv_parts = lax.all_to_all(kv_grads, "ctx", split_axis=0, concat_axis=0, tiled=True)

    big_share = scattered_ctx(added(mine, got[0], crossed))
    big_pieces = gathered_ctx(big_share, False)

    small_rows = padded_rows(slice_rows * (wide + 2 * KVW) // LANES, ctx_count)
    tokens_grad, mine, along, send = call(
        tail_kernel,
        (
            shaped((rows, width), BF16),
            shaped((small_rows, LANES), BF16),
            shaped((small_rows, LANES), BF16),
            shaped((2, small_rows, LANES), BF16),
        ),
        (
            index, kv_parts, tokens, gains, normed, normed_grad, middle_grad, full_kv,
            query_weight_grad, ffn_gain_grad, cosine, sine,
        ),
        scratch=(pltpu.VMEM((width, wide + 2 * KVW), BF16),),
        micros=4,
        smem=1,
    )
    got = swap(send, "ws", 0)
    crossed = swap(added(along, got[1]), "ws", 1)
    small_pieces = gathered_ctx(scattered_ctx(added(mine, got[0], crossed)), False)

    gate_weight_grad, up_weight_grad, down_weight_grad, output_weight_grad = call(
        big_out_kernel,
        (
            shaped(gate_weight.shape, F32),
            shaped(up_weight.shape, F32),
            shaped(down_weight.shape, F32),
            shaped(output_weight.shape, F32),
        ),
        (index,) + big_pieces,
        scratch=(pltpu.VMEM((big_rows, LANES), BF16),),
        micros=3,
        smem=1,
    )
    query_weight_grad, key_weight_grad, value_weight_grad, gain_grads = call(
        small_out_kernel,
        (
            shaped(query_weight.shape, F32),
            shaped(key_weight.shape, F32),
            shaped(value_weight.shape, F32),
            shaped((slice_rows, 8), F32),
        ),
        (index,) + small_pieces,
        scratch=(pltpu.VMEM((small_rows, LANES), BF16),),
        micros=2,
        smem=1,
    )
    return (
        layer_out.reshape(seq_count, rows, width),
        tokens_grad.reshape(seq_count, rows, width),
        gain_grads[:, 0],
        query_weight_grad,
        key_weight_grad,
        value_weight_grad,
        output_weight_grad,
        gain_grads[:, 1],
        gate_weight_grad,
        up_weight_grad,
        down_weight_grad,
    )


def solution(mesh):
    in_specs = (
        P("ws", "ctx", None),
        P("ws"),
        P("ws", None),
        P("ws", None),
        P("ws", None),
        P("ws", None),
        P("ws"),
        P("ws", None),
        P("ws", None),
        P("ws", None),
        P("ws", "ctx", None),
    )
    out_specs = (
        P("ws", "ctx", None),
        P("ws", "ctx", None),
        P("ws"),
        P("ws", None),
        P("ws", None),
        P("ws", None),
        P("ws", None),
        P("ws"),
        P("ws", None),
        P("ws", None),
        P("ws", None),
    )
    return jax.shard_map(body, mesh=mesh, in_specs=in_specs, out_specs=out_specs, check_vma=False)
```

```python
import functools
import math

import jax
import jax.numpy as jnp
from jax import lax
from jax.experimental import pallas as pl
from jax.experimental.pallas import tpu as pltpu
from jax.sharding import PartitionSpec as P

H = 9
KV = 3
HD = 64
GROUPS = H // KV
KVW = KV * HD

EPS = 1e-05
THETA = 100000.0
NEGATIVE = -1e30
LANES = 128
FF_STEP = 256
VMEM_LIMIT = 60 * 1024 * 1024

BF16 = jnp.bfloat16
F32 = jnp.float32

SMEM_SPEC = pl.BlockSpec(memory_space=pltpu.SMEM)
VMEM_SPEC = pl.BlockSpec(memory_space=pltpu.VMEM)


def mm(left, right, left_dim=1, right_dim=0):
    return lax.dot_general(
        left, right, (((left_dim,), (right_dim,)), ((), ())), preferred_element_type=F32
    )


def call(kernel, outs, args, scratch=(), micros=1, smem=0):
    return pl.pallas_call(
        kernel,
        out_shape=outs,
        in_specs=[SMEM_SPEC] * smem + [VMEM_SPEC] * (len(args) - smem),
        out_specs=jax.tree.map(lambda _: VMEM_SPEC, outs),
        scratch_shapes=list(scratch),
        compiler_params=pltpu.CompilerParams(vmem_limit_bytes=VMEM_LIMIT),
        cost_estimate=pl.CostEstimate(
            flops=micros * 1_000_000_000, bytes_accessed=0, transcendentals=0
        ),
    )(*args)


def shaped(shape, dtype):
    return jax.ShapeDtypeStruct(tuple(shape), dtype)


def swap_halves(part):
    lane = lax.broadcasted_iota(jnp.int32, part.shape, 1)
    return jnp.where(
        lane % HD < HD // 2,
        pltpu.roll(part, LANES - HD // 2, axis=1),
        pltpu.roll(part, HD // 2, axis=1),
    )


def rotated(values, cosine, signed_sine, sign):
    rows, width = values.shape
    parts = []
    for start in range(0, width, LANES):
        part = values[:, start : start + LANES]
        used = part.shape[1]
        if used < LANES:
            part = jnp.concatenate([part, jnp.zeros((rows, LANES - used), F32)], -1)
        turned = part * cosine + sign * (swap_halves(part) * signed_sine)
        parts.append(turned[:, :used])
    return jnp.concatenate(parts, -1)


def stacked_heads(ref, group):
    first = group * GROUPS
    return jnp.concatenate(
        [ref[:, (first + g) * HD : (first + g + 1) * HD] for g in range(GROUPS)], 0
    )


def assembled(full, pieces, me):
    rows = pieces[0].shape[0]
    for relative, piece in enumerate(pieces):
        start = pl.multiple_of((me ^ relative) * rows, 16)
        full[pl.ds(start, rows), :] = piece[...]


def projected(tokens, gain, weight, cosine, sine):
    values = tokens.astype(F32)
    scale = lax.rsqrt(jnp.mean(values * values, -1, keepdims=True) + EPS)
    normed = (values * scale * gain).astype(BF16)
    linear = mm(normed, weight)
    keys = rotated(linear[:, :KVW], cosine, sine, 1.0)
    return normed, jnp.concatenate([keys, linear[:, KVW:]], -1).astype(BF16)


def block_at(index, rows):
    return pl.ds(pl.multiple_of(index * rows, rows), rows)


def owner_of(place, here):
    return (here ^ (place % 2)) - 2 * (place // 2)


def table_at(table, owner, rows):
    if table.shape[0] == rows:
        return table[...]
    return table[block_at(jnp.clip(owner, 0, table.shape[0] // rows - 1), rows), :]


def early_kernel(index, packed, q0, q1, q2, q3, cosine, sine, *refs, places):
    pieces = refs[: len(places)]
    normed_out, kv_out, query_out, query_weight, kv_weight, gains_out = refs[len(places) :]
    here = index[0]
    assembled(query_weight, (q0, q1, q2, q3), index[1])
    slice_rows = q0.shape[0]
    owners = query_weight.shape[0] // slice_rows
    step = packed.shape[0] // owners
    gains = []
    for owner in range(owners):
        start = owner * step
        kv_weight[owner * slice_rows : (owner + 1) * slice_rows, :] = packed[
            start : start + slice_rows, :
        ]
        gains.append(packed[start + slice_rows : start + step, :slice_rows].astype(F32))
    gains = jnp.concatenate(gains, -1)
    gains_out[...] = gains[:8]
    for slot, (place, piece) in enumerate(zip(places, pieces)):
        tokens = piece[...].T
        rows = tokens.shape[0]
        tables = [table_at(table, owner_of(place, here), rows) for table in (cosine, sine)]
        normed, kv = projected(tokens, gains[0:1], kv_weight[...], *tables)
        normed_out[slot] = normed
        kv_out[slot] = kv
        if place == 0:
            linear = mm(normed, query_weight[...])
            turned = rotated(linear, *tables, 1.0) * (1.0 / math.sqrt(HD))
            query_out[...] = turned.astype(BF16)


def causal(scores, rows):
    key_pos = lax.broadcasted_iota(jnp.int32, scores.shape, 0)
    query_pos = lax.broadcasted_iota(jnp.int32, scores.shape, 1) % rows
    return jnp.where(query_pos >= key_pos, scores, NEGATIVE)


def forward_kernel(
    index, queries, early_normed, early_kv, kv_weight, gains, cosine, sine, *refs, places, late_places
):
    late, rest = refs[: len(late_places)], refs[len(late_places) :]
    attended, lse_out, kv_all, *rest = rest
    q_scr, acc_scr, max_scr, sum_scr = rest[-4:]
    rows = queries.shape[0]
    here = index[0]
    if late_places:
        normed_all = rest[0]

        def needed(place):
            owner = owner_of(place, here)
            return pl.when((owner >= 0) & (owner <= here)), owner

        for slot, place in enumerate(places):
            when, owner = needed(place)

            @when
            def _(slot=slot, owner=owner):
                normed_all[block_at(owner, rows), :] = early_normed[slot]
                kv_all[block_at(owner, rows), :] = early_kv[slot]

        for place, piece in zip(late_places, late):
            when, owner = needed(place)

            @when
            def _(piece=piece, owner=owner):
                normed, kv = projected(
                    piece[...].T,
                    gains[0:1, :],
                    kv_weight[...],
                    table_at(cosine, owner, rows),
                    table_at(sine, owner, rows),
                )
                normed_all[block_at(owner, rows), :] = normed
                kv_all[block_at(owner, rows), :] = kv
    else:
        kv_all[...] = early_kv[...]

    for group in range(KV):
        q_scr[group] = stacked_heads(queries, group)
    acc_scr[...] = jnp.zeros_like(acc_scr)
    max_scr[...] = jnp.full_like(max_scr, NEGATIVE)
    sum_scr[...] = jnp.zeros_like(sum_scr)

    def block(j, masked):
        keys_at = pl.ds(pl.multiple_of(j * rows, rows), rows)
        for group in range(KV):
            keys = kv_all[keys_at, group * HD : (group + 1) * HD]
            values = kv_all[keys_at, KVW + group * HD : KVW + (group + 1) * HD]
            scores = mm(keys, q_scr[group], 1, 1)
            if masked:
                scores = causal(scores, rows)
            old_max = max_scr[group, 0:1, :]
            new_max = jnp.maximum(old_max, jnp.max(scores, 0, keepdims=True))
            weights = jnp.exp(scores - new_max)
            factor = jnp.exp(old_max - new_max)
            max_scr[group, 0:1, :] = new_max
            sum_scr[group, 0:1, :] = sum_scr[group, 0:1, :] * factor + jnp.sum(
                weights, 0, keepdims=True
            )
            acc_scr[group] = acc_scr[group] * factor + mm(values, weights.astype(BF16), 0, 0)

    def step(j, carry):
        block(j, False)
        return carry

    lax.fori_loop(0, here, step, 0)
    block(here, True)
    lse_out[...] = jnp.zeros_like(lse_out)
    for group in range(KV):
        total = sum_scr[group, 0:1, :]
        result = acc_scr[group] / total
        lse_out[group : group + 1, :] = max_scr[group, 0:1, :] + jnp.log(total)
        for g in range(GROUPS):
            head = group * GROUPS + g
            attended[:, head * HD : (head + 1) * HD] = result[:, g * rows : (g + 1) * rows].T


def rms_back(values, gain, grad):
    width = values.shape[-1]
    scale = lax.rsqrt(jnp.mean(values * values, -1, keepdims=True) + EPS)
    scaled = values * scale
    pulled = grad * gain
    along = jnp.sum(pulled * scaled, -1, keepdims=True) * (1.0 / width)
    return scale * (pulled - scaled * along), grad * scaled


def put_tiles(outs, me, grads, grad_lanes, first_row):
    rows = grads.shape[0] // len(outs)
    first, last = grad_lanes
    for relative, out in enumerate(outs):
        start = pl.multiple_of((me ^ relative) * rows, 16)
        for tile in range((last - first) // LANES):
            at = first + tile * LANES
            out[first_row + tile * rows : first_row + (tile + 1) * rows, :] = grads[
                pl.ds(start, rows), at : at + LANES
            ]


def ffn_kernel(
    index, tokens, attended, gains, out_grad,
    wi0, wi1, wi2, wi3, wd0, wd1, wd2, wd3,
    layer_out, middle_grad_out, attended_grad_out, mine, along, send, gain_grad,
    in_weight, down_weight, result_scr, back_scr, tile_scr, down_scr,
):
    me = index[1]
    assembled(in_weight, (wi0, wi1, wi2, wi3), me)
    assembled(down_weight, (wd0, wd1, wd2, wd3), me)
    outs = (mine, send.at[0], along, send.at[1])
    gain = gains[1:2, :]
    ff = down_weight.shape[0]
    out_weight = in_weight.at[:, 2 * ff :]
    owners = len(outs)
    in_rows = in_weight.shape[0] // owners
    down_rows = ff // owners
    attended_low = attended[...].astype(BF16)
    middle = tokens[...].T.astype(F32) + mm(attended_low, out_weight[...])
    scale = lax.rsqrt(jnp.mean(middle * middle, -1, keepdims=True) + EPS)
    normed = (middle * scale * gain).astype(BF16)
    grad_rows = out_grad[...].T
    result_scr[...] = middle
    back_scr[...] = jnp.zeros_like(back_scr)
    width = grad_rows.shape[1]

    for step in range(ff // FF_STEP):
        gate_at = slice(step * FF_STEP, (step + 1) * FF_STEP)
        up_at = slice(ff + step * FF_STEP, ff + (step + 1) * FF_STEP)
        gate = mm(normed, in_weight[:, gate_at])
        up = mm(normed, in_weight[:, up_at])
        gated = 1.0 / (1.0 + jnp.exp(-gate))
        silu = gate * gated
        hidden = (silu * up).astype(BF16)
        down = down_weight[gate_at, :]
        result_scr[...] += mm(hidden, down)
        hidden_grad = mm(grad_rows, down, 1, 1)
        gate_grad = (hidden_grad * up * (gated * (1.0 + gate * (1.0 - gated)))).astype(BF16)
        up_grad = (hidden_grad * silu).astype(BF16)
        back_scr[...] += mm(gate_grad, in_weight[:, gate_at], 1, 1) + mm(
            up_grad, in_weight[:, up_at], 1, 1
        )
        tile_scr[:, gate_at] = mm(normed, gate_grad, 0, 0).astype(BF16)
        tile_scr[:, up_at] = mm(normed, up_grad, 0, 0).astype(BF16)
        down_scr[gate_at, :width] = mm(hidden, grad_rows, 0, 0).astype(BF16)

    put_tiles(outs, me, tile_scr, (0, 2 * ff), 0)
    base = 2 * (ff // LANES) * in_rows
    whole = width // LANES * LANES
    put_tiles(outs, me, down_scr, (0, whole), base)
    base += whole // LANES * down_rows
    half = down_rows // 2
    for relative, out in enumerate(outs):
        start = pl.multiple_of((me ^ relative) * down_rows, 16)
        rest = jnp.concatenate(
            [
                down_scr[pl.ds(start, half), whole:width],
                down_scr[pl.ds(pl.multiple_of(start + half, 16), half), whole:width],
            ],
            -1,
        )
        out[base : base + half, :] = rest
    base += half

    layer_out[...] = result_scr[...].astype(BF16).T
    middle_back, gain_terms = rms_back(middle, gain, back_scr[...])
    gain_grad[...] = jnp.zeros_like(gain_grad)
    gain_grad[0:1, :] = jnp.sum(gain_terms, 0, keepdims=True)
    middle_grad = middle_back + grad_rows.astype(F32)
    middle_grad_out[...] = middle_grad
    branch = middle_grad.astype(BF16)
    attended_grad_out[...] = mm(branch, out_weight[...], 1, 1).astype(BF16)
    out_weight_grad = mm(attended_low, branch, 0, 0).astype(BF16)
    wide = -(-width // LANES) * LANES
    tile_scr[:, :wide] = jnp.concatenate(
        [out_weight_grad, jnp.zeros((width, wide - width), BF16)], -1
    )
    put_tiles(outs, me, tile_scr, (0, wide), base)
    base += wide // LANES * in_rows
    for out in outs:
        out[base:, :] = jnp.zeros((out.shape[0] - base, LANES), BF16)


def put_small(outs, me, tile_scr, query_grad, kv_grad, query_weight, kv_weight, gains, ffn_gain_grad):
    width = query_grad.shape[0]
    wide = -(-width // LANES) * LANES
    gain_columns = gains[...].T
    terms = jnp.sum(query_grad * query_weight.astype(F32), -1, keepdims=True) + jnp.sum(
        kv_grad * kv_weight.astype(F32), -1, keepdims=True
    )
    columns = jnp.concatenate(
        [
            terms / gain_columns[:, 0:1],
            ffn_gain_grad[...].T[:, 0:1],
            jnp.zeros((width, wide - width - 2), F32),
        ],
        -1,
    )
    tile_scr[:, :wide] = jnp.concatenate([query_grad, columns], -1).astype(BF16)
    tile_scr[:, wide : wide + 2 * KVW] = kv_grad.astype(BF16)
    put_tiles(outs, me, tile_scr, (0, wide + 2 * KVW), 0)


def backward_kernel(
    index, queries, kv_all, attended, attended_grad, lse, normed, query_weight, kv_weight, gains,
    ffn_gain_grad, cosine, sine,
    *refs,
):
    q_scr, g_scr, delta_scr, acc_scr, query_grad_scr = refs[-5:]
    rows = queries.shape[0]
    blocks = kv_all.shape[0] // rows
    here = index[0]
    whole = normed.shape[0] > rows
    if whole:
        kv_grads, normed_grad, mine, along, send, tile_scr, weight_scr = refs[:-5]
        weight_scr[...] = jnp.zeros_like(weight_scr)
        kv_grads[...] = jnp.zeros_like(kv_grads)
    else:
        kv_grads, normed_grad, query_weight_grad = refs[:-5]
    for group in range(KV):
        q_scr[group] = stacked_heads(queries, group)
        grads = stacked_heads(attended_grad, group)
        g_scr[group] = grads
        terms = (grads.astype(F32) * stacked_heads(attended, group)).T
        delta_scr[group, 0:1, :] = jnp.sum(terms, 0, keepdims=True)
    acc_scr[...] = jnp.zeros_like(acc_scr)

    def block(j, masked):
        keys_at = block_at(j, rows)
        key_grads = []
        value_grads = []
        for group in range(KV):
            keys = kv_all[keys_at, group * HD : (group + 1) * HD]
            values = kv_all[keys_at, KVW + group * HD : KVW + (group + 1) * HD]
            group_q = q_scr[group]
            group_g = g_scr[group]
            scores = mm(keys, group_q, 1, 1)
            if masked:
                scores = causal(scores, rows)
            prob = jnp.exp(scores - lse[group : group + 1, :])
            prob_grad = mm(values, group_g, 1, 1)
            score_grad = (prob * (prob_grad - delta_scr[group, 0:1, :])).astype(BF16)
            value_grads.append(mm(prob.astype(BF16), group_g))
            key_grads.append(mm(score_grad, group_q))
            acc_scr[group] += mm(keys, score_grad, 0, 0)
        key_grad = jnp.concatenate(key_grads, -1)
        value_grad = jnp.concatenate(value_grads, -1)
        both = jnp.concatenate([key_grad, value_grad], -1).astype(BF16)
        if whole:
            across = (j ^ here) & 1
            distance = (j // 2 - here // 2) & (blocks // 2 - 1)
            kv_grads[across * (blocks // 2) + distance] = both
            turned = rotated(key_grad, cosine[keys_at, :], sine[keys_at, :], -1.0)
            linear = jnp.concatenate([turned, value_grad], -1).astype(BF16)
            weight_scr[...] += mm(normed[keys_at, :], linear, 0, 0)
        else:
            kv_grads[keys_at, :] = both

    def step(j, carry):
        block(j, False)
        return carry

    def clear(j, carry):
        kv_grads[block_at(j, rows), :] = jnp.zeros((rows, kv_grads.shape[1]), BF16)
        return carry

    lax.fori_loop(0, here, step, 0)
    block(here, True)
    if not whole:
        lax.fori_loop(here + 1, blocks, clear, 0)
    for group in range(KV):
        for g in range(GROUPS):
            head = group * GROUPS + g
            part = acc_scr[group, :, g * rows : (g + 1) * rows]
            query_grad_scr[:, head * HD : (head + 1) * HD] = part.T
    tables = (table_at(cosine, here, rows), table_at(sine, here, rows))
    back = rotated(query_grad_scr[...], *tables, -1.0) * (1.0 / math.sqrt(HD))
    back = back.astype(BF16)
    own_normed = normed[block_at(here, rows), :] if whole else normed[...]
    query_grad = mm(own_normed, back, 0, 0)
    normed_grad[...] = mm(back, query_weight[...], 1, 1)
    if whole:
        outs = (mine, send.at[0], along, send.at[1])
        put_small(
            outs, index[1], tile_scr, query_grad, weight_scr[...], query_weight[...],
            kv_weight[...], gains, ffn_gain_grad,
        )
    else:
        query_weight_grad[...] = query_grad


def small_kernel(
    index, query_grad, kv_grad, query_weight, kv_weight, gains, ffn_gain_grad,
    mine, along, send, tile_scr,
):
    outs = (mine, send.at[0], along, send.at[1])
    for out in outs:
        out[...] = jnp.zeros(out.shape, BF16)
    put_small(
        outs, index[1], tile_scr, query_grad[...], kv_grad[...], query_weight[...], kv_weight[...],
        gains, ffn_gain_grad,
    )


def tail_kernel(
    tokens, gains, normed_grad, middle_grad, kv_weight, cosine, sine, *refs
):
    kv_parts, tokens_grad = refs[:-1], refs[-1]
    rows = normed_grad.shape[0]
    if len(kv_parts) == 1:

        def add(j, total):
            return total + kv_parts[0][block_at(j, rows), :].astype(F32)

        parts = kv_parts[0].shape[0] // rows
        kv_grad = lax.fori_loop(0, parts, add, jnp.zeros((rows, 2 * KVW), F32))
    else:
        own, got, *moved = kv_parts
        kv_grad = own[0].astype(F32) + got[0].astype(F32)
        for part in moved:
            kv_grad = kv_grad + part[...].astype(F32)
    key_back = rotated(kv_grad[:, :KVW], cosine[...], sine[...], -1.0)
    back = jnp.concatenate([key_back, kv_grad[:, KVW:]], -1).astype(BF16)
    total = normed_grad[...] + mm(back, kv_weight[...], 1, 1)
    values = tokens[...].T.astype(F32)
    input_grad, _ = rms_back(values, gains[0:1, :], total)
    tokens_grad[...] = (middle_grad[...] + input_grad).astype(BF16).T


def spread_kernel(index, *refs, parts, count):
    own, keep, send = refs[-3:]
    here = index[0]
    first = 0
    for part, (base, rows) in enumerate(parts):
        mine, got, crossed = refs[3 * part : 3 * part + 3]
        to = slice(first, first + rows)
        first += rows
        for distance in range(count // 2):
            for across in range(2):
                owner = ((here ^ across) + 2 * distance) & (count - 1)
                start = pl.multiple_of(owner * rows, 16)
                at = pl.ds(pl.multiple_of(base + start, 16), rows)
                total = mine[at, :].astype(F32) + got[0, at, :].astype(F32)
                total = (total + crossed[at, :].astype(F32)).astype(BF16)
                if across:
                    send[distance, to, :] = total
                elif distance:
                    keep[distance - 1, to, :] = total
                else:
                    own[to, :] = total


def flattened(index, pieces, parts):
    here = index[0]
    if len(pieces) == 1:
        (piece,) = pieces
        total = sum(rows for _, _, rows in parts)
        count = piece.shape[0] // total
        owners = [(owner, piece, owner * total) for owner in range(count)]
    else:
        count = 2 * pieces[0].shape[0]
        owners = [
            (((here ^ across) + (count - 2 * distance)) & (count - 1), column.at[distance], 0)
            for across, column in enumerate(pieces)
            for distance in range(count // 2)
        ]
    for owner, piece, start in owners:
        for flat, base, rows in parts:
            at = pl.multiple_of(base + owner * rows, 16)
            flat[pl.ds(at, rows), :] = piece[start : start + rows, :]
            start += rows


def untile(out, flat, base, columns):
    rows = out.shape[0]
    for tile in range(columns // LANES):
        out[:, tile * LANES : (tile + 1) * LANES] = flat[base : base + rows, :].astype(F32)
        base += rows
    return base


def gate_kernel(index, *refs, parts):
    pieces, (gate_out, flat) = refs[:-2], refs[-2:]
    flattened(index, pieces, [(flat,) + part for part in parts])
    untile(gate_out, flat, 0, gate_out.shape[1])


def outputs_kernel(index, *refs, first_parts, second_parts, first_count):
    up_out, down_out, out_out, query_out, key_out, value_out, gain_out, flat, small = refs[-9:]
    pieces = refs[:-9]
    flattened(index, pieces[:first_count], [(flat,) + part for part in first_parts])
    big, little = second_parts
    flattened(index, pieces[first_count:], [(flat,) + big, (small,) + little])
    base = untile(up_out, flat, up_out.shape[1] // LANES * up_out.shape[0], up_out.shape[1])
    rows, width = down_out.shape
    whole = width // LANES * LANES
    base = untile(down_out, flat, base, whole)
    half = rows // 2
    rest = flat[base : base + half, :].astype(F32)
    down_out[:half, whole:] = rest[:, : width - whole]
    down_out[half:, whole:] = rest[:, width - whole :]
    base = untile(out_out, flat, base + half, whole)
    rows = out_out.shape[0]
    out_out[:, whole:] = flat[base : base + rows, : width - whole].astype(F32)
    base = untile(query_out, small, 0, whole)
    tile = small[base : base + rows, :].astype(F32)
    query_out[:, whole:] = tile[:, : width - whole]
    gain_out[...] = tile[:, width - whole : width - whole + 8].T
    base += rows
    both = [
        small[base + at * rows : base + (at + 1) * rows, :].astype(F32)
        for at in range(2 * KVW // LANES)
    ]
    both = jnp.concatenate(both, -1)
    key_out[...] = both[:, :KVW]
    value_out[...] = both[:, KVW:]


def swap(value, axis, bit):
    count = lax.axis_size(axis)
    return lax.ppermute(value, axis, [(i, i ^ (1 << bit)) for i in range(count)])


def gathered_ws(value):
    along = swap(value, "ws", 1)
    return value, swap(value, "ws", 0), along, swap(along, "ws", 0)


def gathered_ctx(value):
    count = lax.axis_size("ctx")
    if count != 8:
        return (lax.all_gather(value, "ctx", axis=0, tiled=True),)
    column = jnp.stack([value] + [shifted(value, by, False) for by in (1, 2, 3)])
    return column, swap(column, "ctx", 0)


def shifted(value, by, upward_only):
    count = lax.axis_size("ctx")
    pairs = [(i, i + 2 * by) for i in range(count)]
    if upward_only:
        pairs = [(i, j) for i, j in pairs if j < count]
    return lax.ppermute(value, "ctx", [(i, j % count) for i, j in pairs])


def rms_scale(values, gain_vec):
    return values * lax.rsqrt(jnp.mean(values * values, -1, keepdims=True) + EPS) * gain_vec


def added(*values):
    total = values[0].astype(F32)
    for value in values[1:]:
        total = total + value.astype(F32)
    return total.astype(values[0].dtype)


def scattered_ctx(values, counts):
    count = lax.axis_size("ctx")
    value = jnp.concatenate(
        [v.reshape(count, rows, LANES) for v, rows in zip(values, counts)], 1
    ).reshape(-1, LANES)
    parts = lax.all_to_all(value, "ctx", split_axis=0, concat_axis=0, tiled=True)
    parts = parts.reshape(count, -1, LANES).astype(F32)
    return jnp.sum(parts, 0).astype(value.dtype)


def rope_tables(positions):
    frequency = jnp.exp(jnp.arange(HD // 2).astype(F32) * (-2.0 * math.log(THETA) / HD))
    angles = positions.astype(F32)[:, None] * frequency[None, :]
    return jnp.cos(angles), jnp.sin(angles)


def turned_heads(values, cosine, sine):
    heads = values.reshape(values.shape[0], -1, 2, HD // 2)
    cosine, sine = cosine[:, None], sine[:, None]
    first, second = heads[:, :, 0], heads[:, :, 1]
    pair = [first * cosine - second * sine, second * cosine + first * sine]
    return jnp.stack(pair, 2).reshape(values.shape)


def scattered_parts(keep, got, downward_only):
    count = lax.axis_size("ctx")
    parts = [got]
    for by in (1, 2, 3):
        pairs = [(i, i + 2 * by) for i in range(count)]
        if downward_only:
            pairs = [(i, j) for i, j in pairs if j >= count]
        part = added(keep[by - 1], got[by])
        parts.append(lax.ppermute(part, "ctx", [(i, j % count) for i, j in pairs]))
    return parts


def spread(index, parts, arrays):
    count = lax.axis_size("ctx")
    rows = sum(part[1] for part in parts)
    return call(
        functools.partial(spread_kernel, parts=parts, count=count),
        (
            shaped((rows, LANES), BF16),
            shaped((count // 2 - 1, rows, LANES), BF16),
            shaped((count // 2, rows, LANES), BF16),
        ),
        (index, *arrays),
        micros=2,
        smem=1,
    )


def padded_rows(rows, count):
    return -(-rows // (16 * count)) * 16 * count


def body(
    tokens,
    attn_gain,
    query_weight,
    key_weight,
    value_weight,
    output_weight,
    ffn_gain,
    gate_weight,
    up_weight,
    down_weight,
    out_grad,
):
    seq_count, rows, width = tokens.shape
    ctx_count = lax.axis_size("ctx")
    owners = lax.axis_size("ws")
    slice_rows = query_weight.shape[0]
    ff = gate_weight.shape[1]
    wide = -(-width // LANES) * LANES
    by_hops = ctx_count == 8
    tokens = tokens.reshape(rows, width).T
    out_grad = out_grad.reshape(rows, width).T
    ctx_index = lax.axis_index("ctx")
    index = jnp.stack([ctx_index, lax.axis_index("ws")]).astype(jnp.int32)

    if by_hops:
        behind_two = shifted(tokens, 2, True)
        behind_one = shifted(tokens, 1, True)
        mate = swap(tokens, "ctx", 0)

    packed = jnp.concatenate(
        [
            jnp.concatenate([key_weight, value_weight], -1),
            jnp.pad(
                jnp.stack([attn_gain, ffn_gain]), ((0, 14), (0, 2 * KVW - slice_rows))
            ),
        ],
        0,
    )
    packed = lax.all_gather(packed, "ws", axis=0, tiled=True)
    packed, query_weight, in_weight, down_weight = lax.optimization_barrier(
        (
            packed,
            query_weight,
            jnp.concatenate([gate_weight, up_weight, output_weight], -1),
            down_weight,
        )
    )
    query_pieces = gathered_ws(query_weight)
    in_along = swap(in_weight, "ws", 1)
    down_along = swap(down_weight, "ws", 1)

    def wide_tables(positions):
        cosine, sine = rope_tables(positions)
        return jnp.concatenate([cosine] * 4, -1), jnp.concatenate([-sine, sine] * 2, -1)

    first_pos = ctx_index * rows
    cosine, sine = wide_tables(first_pos + jnp.arange(rows, dtype=jnp.int32))
    if by_hops:
        tables = wide_tables(jnp.arange(ctx_count * rows, dtype=jnp.int32))
    else:
        tables = (cosine, sine)

    places = (0, 1, 4, 2) if by_hops else (0,)
    late_places = (5, 3, 6, 7) if by_hops else ()
    early = (tokens, mate, behind_two, behind_one) if by_hops else (tokens,)
    early_normed, early_kv, queries, full_query, full_kv, gains = call(
        functools.partial(early_kernel, places=places),
        (
            shaped((len(places), rows, width), BF16),
            shaped((len(places), rows, 2 * KVW), BF16),
            shaped((rows, width), BF16),
            shaped((width, width), BF16),
            shaped((width, 2 * KVW), BF16),
            shaped((8, width), F32),
        ),
        (index, packed) + query_pieces + tables + early,
        micros=6,
        smem=1,
    )
    if by_hops:
        behind_three = shifted(behind_two, 1, True)
        behind_three, queries = lax.optimization_barrier((behind_three, queries))
        late = (
            swap(behind_two, "ctx", 0),
            swap(behind_one, "ctx", 0),
            behind_three,
            swap(behind_three, "ctx", 0),
        )
        normed_shape = (shaped((ctx_count * rows, width), BF16),)
    else:
        tokens_all = lax.all_gather(tokens.T, "ctx", axis=0, tiled=True).astype(F32)
        normed_all = rms_scale(tokens_all, gains[0]).astype(BF16)
        linear = jnp.dot(normed_all, full_kv, preferred_element_type=F32)
        full_tables = rope_tables(jnp.arange(ctx_count * rows, dtype=jnp.int32))
        early_kv = jnp.concatenate(
            [turned_heads(linear[:, :KVW], *full_tables), linear[:, KVW:]], -1
        ).astype(BF16)
        late = ()
        normed_shape = ()

    late, rest = lax.optimization_barrier((late, (in_weight, down_weight, in_along, down_along)))
    in_pieces, down_pieces = (
        (own, swap(own, "ws", 0), along, swap(along, "ws", 0))
        for own, along in zip(rest[:2], rest[2:])
    )

    attended, lse, kv_all, *normed_out = call(
        functools.partial(forward_kernel, places=places, late_places=late_places),
        (
            shaped((rows, width), F32),
            shaped((8, GROUPS * rows), F32),
            shaped((ctx_count * rows, 2 * KVW), BF16),
            *normed_shape,
        ),
        (index, queries, early_normed, early_kv, full_kv, gains, *tables, *late),
        scratch=(
            pltpu.VMEM((KV, GROUPS * rows, HD), BF16),
            pltpu.VMEM((KV, HD, GROUPS * rows), F32),
            pltpu.VMEM((KV, 8, GROUPS * rows), F32),
            pltpu.VMEM((KV, 8, GROUPS * rows), F32),
        ),
        micros=20,
        smem=1,
    )

    big_rows = (2 * slice_rows * ff + (ff // owners) * width + slice_rows * wide) // LANES
    big_rows = padded_rows(big_rows, ctx_count)
    layer_out, middle_grad, attended_grad, mine, along, send, ffn_gain_grad = call(
        ffn_kernel,
        (
            shaped((width, rows), BF16),
            shaped((rows, width), F32),
            shaped((rows, width), BF16),
            shaped((big_rows, LANES), BF16),
            shaped((big_rows, LANES), BF16),
            shaped((2, big_rows, LANES), BF16),
            shaped((8, width), F32),
        ),
        (index, tokens, attended, gains, out_grad) + in_pieces + down_pieces,
        scratch=(
            pltpu.VMEM((width, 2 * ff + width), BF16),
            pltpu.VMEM((ff, width), BF16),
            pltpu.VMEM((rows, width), F32),
            pltpu.VMEM((rows, width), F32),
            pltpu.VMEM((width, 2 * ff), BF16),
            pltpu.VMEM((ff, wide), BF16),
        ),
        micros=14,
        smem=1,
    )

    first_rows = -(-big_rows // (32 * ctx_count)) * 16
    second_rows = big_rows // ctx_count - first_rows
    cut_at = first_rows * ctx_count
    got = swap(send, "ws", 0)
    attended_grad, crossing = lax.optimization_barrier((attended_grad, added(along, got[1])))
    crossed = swap(crossing, "ws", 1)

    small_rows = padded_rows(slice_rows * (wide + 2 * KVW) // LANES, ctx_count)
    tile_shapes = (
        shaped((small_rows, LANES), BF16),
        shaped((small_rows, LANES), BF16),
        shaped((2, small_rows, LANES), BF16),
    )
    tile_scr = pltpu.VMEM((width, wide + 2 * KVW), BF16)
    if by_hops:
        kv_shape = shaped((ctx_count, rows, 2 * KVW), BF16)
        backward_normed = normed_out[0]
        more_shapes = tile_shapes
        more_scratch = (tile_scr, pltpu.VMEM((width, 2 * KVW), F32))
    else:
        kv_shape = shaped((ctx_count * rows, 2 * KVW), BF16)
        backward_normed = early_normed[0]
        more_shapes = (shaped((width, width), F32),)
        more_scratch = ()
    kv_grads, normed_grad, *small = call(
        backward_kernel,
        (kv_shape, shaped((rows, width), F32), *more_shapes),
        (
            index, queries, kv_all, attended, attended_grad, lse, backward_normed, full_query,
            full_kv, gains, ffn_gain_grad, *tables,
        ),
        scratch=(
            *more_scratch,
            pltpu.VMEM((KV, GROUPS * rows, HD), BF16),
            pltpu.VMEM((KV, GROUPS * rows, HD), BF16),
            pltpu.VMEM((KV, 8, GROUPS * rows), F32),
            pltpu.VMEM((KV, HD, GROUPS * rows), F32),
            pltpu.VMEM((rows, width), F32),
        ),
        micros=23,
        smem=1,
    )
    if not by_hops:
        linear = turned_heads(kv_grads[:, :KVW].astype(F32), full_tables[0], -full_tables[1])
        linear = jnp.concatenate([linear.astype(BF16), kv_grads[:, KVW:]], -1)
        kv_weight_grad = jnp.einsum("nd,nh->dh", normed_all, linear, preferred_element_type=F32)
        small = call(
            small_kernel,
            tile_shapes,
            (index, small[0], kv_weight_grad, full_query, full_kv, gains, ffn_gain_grad),
            scratch=(tile_scr,),
            smem=1,
        )
    small_mine, small_along, small_send = small
    small_got = swap(small_send, "ws", 0)
    small_crossed = swap(added(small_along, small_got[1]), "ws", 1)
    little_rows = small_rows // ctx_count
    first_parts = ((0, first_rows),)
    second_parts = ((cut_at, second_rows), (0, little_rows))

    if by_hops:
        own, keep, to_mate = spread(index, first_parts, (mine, got, crossed))
        from_mate = swap(to_mate, "ctx", 0)
        parts = scattered_parts(keep, from_mate, False)
        first_share = added(own, parts[0][0], *parts[1:])
        own, keep, to_mate = spread(
            index,
            second_parts,
            (mine, got, crossed, small_mine, small_got, small_crossed),
        )
        to_mate, kv_to_mate = lax.optimization_barrier((to_mate, kv_grads[ctx_count // 2 :]))
        from_mate = swap(to_mate, "ctx", 0)
        kv_from_mate = swap(kv_to_mate, "ctx", 0)
        kv_keep = kv_grads[1 : ctx_count // 2]
        kv_parts = (kv_grads, *scattered_parts(kv_keep, kv_from_mate, True))
        parts = scattered_parts(keep, from_mate, False)
        second_share = added(own, parts[0][0], *parts[1:])
    else:
        kv_parts = (lax.all_to_all(kv_grads, "ctx", split_axis=0, concat_axis=0, tiled=True),)
        first = added(mine[:cut_at], got[0, :cut_at], crossed[:cut_at])
        second = added(mine[cut_at:], got[0, cut_at:], crossed[cut_at:])
        little = added(small_mine, small_got[0], small_crossed)
        first_share = scattered_ctx((first,), (first_rows,))
        second_share = scattered_ctx((second, little), (second_rows, little_rows))
    first_pieces = gathered_ctx(first_share)
    second_pieces = gathered_ctx(second_share)

    tokens_grad = call(
        tail_kernel,
        shaped((width, rows), BF16),
        (
            tokens, gains, normed_grad, middle_grad, full_kv, cosine, sine, *kv_parts,
        ),
        micros=4,
    )

    flat_scr = pltpu.VMEM((big_rows, LANES), BF16)
    gate_weight_grad = call(
        functools.partial(gate_kernel, parts=first_parts),
        shaped(gate_weight.shape, F32),
        (index,) + first_pieces,
        scratch=(flat_scr,),
        micros=2,
        smem=1,
    )
    (
        up_weight_grad,
        down_weight_grad,
        output_weight_grad,
        query_weight_grad,
        key_weight_grad,
        value_weight_grad,
        gain_grads,
    ) = call(
        functools.partial(
            outputs_kernel,
            first_parts=first_parts,
            second_parts=second_parts,
            first_count=len(first_pieces),
        ),
        (
            shaped(up_weight.shape, F32),
            shaped(down_weight.shape, F32),
            shaped(output_weight.shape, F32),
            shaped(query_weight.shape, F32),
            shaped(key_weight.shape, F32),
            shaped(value_weight.shape, F32),
            shaped((8, slice_rows), F32),
        ),
        (index,) + first_pieces + second_pieces,
        scratch=(flat_scr, pltpu.VMEM((small_rows, LANES), BF16)),
        micros=3,
        smem=1,
    )
    return (
        layer_out.T.reshape(seq_count, rows, width),
        tokens_grad.T.reshape(seq_count, rows, width),
        gain_grads[0],
        query_weight_grad,
        key_weight_grad,
        value_weight_grad,
        output_weight_grad,
        gain_grads[1],
        gate_weight_grad,
        up_weight_grad,
        down_weight_grad,
    )


def solution(mesh):
    in_specs = (
        P("ws", "ctx", None),
        P("ws"),
        P("ws", None),
        P("ws", None),
        P("ws", None),
        P("ws", None),
        P("ws"),
        P("ws", None),
        P("ws", None),
        P("ws", None),
        P("ws", "ctx", None),
    )
    out_specs = (
        P("ws", "ctx", None),
        P("ws", "ctx", None),
        P("ws"),
        P("ws", None),
        P("ws", None),
        P("ws", None),
        P("ws", None),
        P("ws"),
        P("ws", None),
        P("ws", None),
        P("ws", None),
    )
    return jax.shard_map(body, mesh=mesh, in_specs=in_specs, out_specs=out_specs, check_vma=False)
```

```python
import functools
import math

import jax
import jax.numpy as jnp
from jax import lax
from jax.experimental import pallas as pl
from jax.experimental.pallas import tpu as pltpu
from jax.sharding import PartitionSpec as P

H = 9
KV = 3
HD = 64
GROUPS = H // KV
KVW = KV * HD

EPS = 1e-05
THETA = 100000.0
NEGATIVE = -1e30
LANES = 128
FF_STEP = 256
MIB = 1024 * 1024

BF16 = jnp.bfloat16
F32 = jnp.float32

SMEM_SPEC = pl.BlockSpec(memory_space=pltpu.SMEM)
VMEM_SPEC = pl.BlockSpec(memory_space=pltpu.VMEM)


def mm(left, right, left_dim=1, right_dim=0):
    return lax.dot_general(
        left, right, (((left_dim,), (right_dim,)), ((), ())), preferred_element_type=F32
    )


def call(kernel, outs, args, scratch=(), micros=1, smem=0, vmem=16):
    return pl.pallas_call(
        kernel,
        out_shape=outs,
        in_specs=[SMEM_SPEC] * smem + [VMEM_SPEC] * (len(args) - smem),
        out_specs=jax.tree.map(lambda _: VMEM_SPEC, outs),
        scratch_shapes=list(scratch),
        compiler_params=pltpu.CompilerParams(vmem_limit_bytes=vmem * MIB),
        cost_estimate=pl.CostEstimate(
            flops=micros * 1_000_000_000, bytes_accessed=0, transcendentals=0
        ),
    )(*args)


def shaped(shape, dtype):
    return jax.ShapeDtypeStruct(tuple(shape), dtype)


def swap_halves(part):
    lane = lax.broadcasted_iota(jnp.int32, part.shape, 1)
    return jnp.where(
        lane % HD < HD // 2,
        pltpu.roll(part, LANES - HD // 2, axis=1),
        pltpu.roll(part, HD // 2, axis=1),
    )


def rotated(values, cosine, signed_sine, sign):
    rows, width = values.shape
    parts = []
    for start in range(0, width, LANES):
        part = values[:, start : start + LANES]
        used = part.shape[1]
        if used < LANES:
            part = jnp.concatenate([part, jnp.zeros((rows, LANES - used), F32)], -1)
        turned = part * cosine + sign * (swap_halves(part) * signed_sine)
        parts.append(turned[:, :used])
    return jnp.concatenate(parts, -1)


def stacked_heads(ref, group):
    first = group * GROUPS
    return jnp.concatenate(
        [ref[:, (first + g) * HD : (first + g + 1) * HD] for g in range(GROUPS)], 0
    )


def assembled(full, pieces, me):
    rows = pieces[0].shape[0]
    for relative, piece in enumerate(pieces):
        start = pl.multiple_of((me ^ relative) * rows, 16)
        full[pl.ds(start, rows), :] = piece[...]


def projected(tokens, gain, weight, cosine, sine):
    values = tokens.astype(F32)
    scale = lax.rsqrt(jnp.mean(values * values, -1, keepdims=True) + EPS)
    normed = (values * scale * gain).astype(BF16)
    linear = mm(normed, weight)
    keys = rotated(linear[:, :KVW], cosine, sine, 1.0)
    return normed, jnp.concatenate([keys, linear[:, KVW:]], -1).astype(BF16)


def block_at(index, rows):
    return pl.ds(pl.multiple_of(index * rows, rows), rows)


def owner_of(place, here):
    return (here ^ (place % 2)) - 2 * (place // 2)


def table_at(table, owner, rows):
    if table.shape[0] == rows:
        return table[...]
    return table[block_at(jnp.clip(owner, 0, table.shape[0] // rows - 1), rows), :]


def early_kernel(index, p0, p1, p2, p3, cosine, sine, *refs, places, slice_rows):
    pieces = refs[: len(places)]
    (
        normed_out, kv_out, query_out, query_weight, kv_weight, gains_out, gain_scr, raw_scr,
    ) = refs[len(places) :]
    here = index[0]
    more = p0.shape[0] - slice_rows
    packs = (p0, p1, p2, p3)
    for relative, pack in enumerate(packs):
        owner = index[1] ^ relative
        at = pl.ds(pl.multiple_of(owner * slice_rows, 16), slice_rows)
        kv_weight[at, :] = pack[:slice_rows, : 2 * KVW]
        query_weight[at, :] = pack[:slice_rows, 2 * KVW :]
        gain_scr[pl.ds(pl.multiple_of(owner * more, 16), more), :] = pack[
            slice_rows:, : gain_scr.shape[1]
        ]
    gains = jnp.concatenate(
        [
            gain_scr[owner * more : owner * more + 8, :slice_rows].astype(F32)
            for owner in range(len(packs))
        ],
        -1,
    )
    gains_out[...] = gains
    rows = normed_out.shape[1]
    for slot, piece in enumerate(pieces):
        raw_scr[slot] = piece[...]

    def project(slot, carry):
        owner = owner_of(one_of(places, slot), here)
        tables = [table_at(table, owner, rows) for table in (cosine, sine)]
        normed, kv = projected(raw_scr[slot].T, gains_out[0:1, :], kv_weight[...], *tables)
        normed_out[slot] = normed
        kv_out[slot] = kv
        return carry

    lax.fori_loop(0, len(places), project, 0)
    tables = [table_at(table, here, rows) for table in (cosine, sine)]
    linear = mm(normed_out[0], query_weight[...])
    query_out[...] = (rotated(linear, *tables, 1.0) * (1.0 / math.sqrt(HD))).astype(BF16)


def fill_masks(masks):
    shape = masks.shape[1:]
    key_pos = lax.broadcasted_iota(jnp.int32, shape, 0)
    query_pos = lax.broadcasted_iota(jnp.int32, shape, 1)
    masks[0] = jnp.zeros(shape, F32)
    masks[1] = jnp.where(query_pos >= key_pos, 0.0, NEGATIVE)


def one_of(values, at):
    found = values[0]
    for place, value in enumerate(values[1:], 1):
        found = jnp.where(at == place, value, found)
    return found


def forward_kernel(
    index, queries, early_normed, early_kv, kv_weight, gains, cosine, sine, *refs, places, late_places
):
    late, rest = refs[: len(late_places)], refs[len(late_places) :]
    attended, lse_out, kv_all, *rest = rest
    q_scr, acc_scr, max_scr, sum_scr, masks = rest[-5:]
    fill_masks(masks)
    rows = queries.shape[0]
    here = index[0]
    if late_places:
        normed_all, raw_scr = rest[:2]
        for slot, piece in enumerate(late):
            raw_scr[slot] = piece[...]

        def copy(slot, carry):
            owner = owner_of(one_of(places, slot), here)

            @pl.when((owner >= 0) & (owner <= here))
            def _():
                normed_all[block_at(owner, rows), :] = early_normed[slot]
                kv_all[block_at(owner, rows), :] = early_kv[slot]

            return carry

        def project(slot, carry):
            owner = owner_of(one_of(late_places, slot), here)

            @pl.when((owner >= 0) & (owner <= here))
            def _():
                normed, kv = projected(
                    raw_scr[slot].T,
                    gains[0:1, :],
                    kv_weight[...],
                    table_at(cosine, owner, rows),
                    table_at(sine, owner, rows),
                )
                normed_all[block_at(owner, rows), :] = normed
                kv_all[block_at(owner, rows), :] = kv

            return carry

        lax.fori_loop(0, len(places), copy, 0)
        lax.fori_loop(0, len(late_places), project, 0)
    else:
        kv_all[...] = early_kv[...]

    for group in range(KV):
        q_scr[group] = stacked_heads(queries, group)
    acc_scr[...] = jnp.zeros_like(acc_scr)
    max_scr[...] = jnp.full_like(max_scr, NEGATIVE)
    sum_scr[...] = jnp.zeros_like(sum_scr)

    def step(j, carry):
        keys_at = block_at(j, rows)
        mask = jnp.concatenate([masks[jnp.where(j == here, 1, 0)]] * GROUPS, -1)
        for group in range(KV):
            keys = kv_all[keys_at, group * HD : (group + 1) * HD]
            values = kv_all[keys_at, KVW + group * HD : KVW + (group + 1) * HD]
            scores = mm(keys, q_scr[group], 1, 1) + mask
            old_max = max_scr[group, 0:1, :]
            new_max = jnp.maximum(old_max, jnp.max(scores, 0, keepdims=True))
            weights = jnp.exp(scores - new_max)
            factor = jnp.exp(old_max - new_max)
            max_scr[group, 0:1, :] = new_max
            sum_scr[group, 0:1, :] = sum_scr[group, 0:1, :] * factor + jnp.sum(
                weights, 0, keepdims=True
            )
            acc_scr[group] = acc_scr[group] * factor + mm(values, weights.astype(BF16), 0, 0)
        return carry

    lax.fori_loop(0, here + 1, step, 0)
    lse_out[...] = jnp.zeros_like(lse_out)
    for group in range(KV):
        total = sum_scr[group, 0:1, :]
        result = acc_scr[group] / total
        lse_out[group : group + 1, :] = max_scr[group, 0:1, :] + jnp.log(total)
        for g in range(GROUPS):
            head = group * GROUPS + g
            attended[:, head * HD : (head + 1) * HD] = result[:, g * rows : (g + 1) * rows].T


def rms_back(values, gain, grad):
    width = values.shape[-1]
    scale = lax.rsqrt(jnp.mean(values * values, -1, keepdims=True) + EPS)
    scaled = values * scale
    pulled = grad * gain
    along = jnp.sum(pulled * scaled, -1, keepdims=True) * (1.0 / width)
    return scale * (pulled - scaled * along), grad * scaled


def put_tiles(outs, me, grads, grad_lanes, first_row):
    rows = grads.shape[0] // len(outs)
    first, last = grad_lanes
    for relative, out in enumerate(outs):
        start = pl.multiple_of((me ^ relative) * rows, 16)
        for tile in range((last - first) // LANES):
            at = first + tile * LANES
            out[first_row + tile * rows : first_row + (tile + 1) * rows, :] = grads[
                pl.ds(start, rows), at : at + LANES
            ]


def ffn_kernel(
    index, tokens, attended, gains, out_grad,
    wi0, wi1, wi2, wi3, wd0, wd1, wd2, wd3,
    layer_out, middle_grad_out, attended_grad_out, gain_grad,
    in_mine, in_along, in_send, mine, along, send,
    in_weight, down_weight, result_scr, back_scr, tile_scr, down_scr,
):
    me = index[1]
    assembled(in_weight, (wi0, wi1, wi2, wi3), me)
    assembled(down_weight, (wd0, wd1, wd2, wd3), me)
    in_outs = (in_mine, in_send.at[0], in_along, in_send.at[1])
    outs = (mine, send.at[0], along, send.at[1])
    gain = gains[1:2, :]
    ff = down_weight.shape[0]
    out_weight = in_weight.at[:, 2 * ff :]
    owners = len(outs)
    in_rows = in_weight.shape[0] // owners
    down_rows = ff // owners
    attended_low = attended[...].astype(BF16)
    middle = tokens[...].T.astype(F32) + mm(attended_low, out_weight[...])
    scale = lax.rsqrt(jnp.mean(middle * middle, -1, keepdims=True) + EPS)
    normed = (middle * scale * gain).astype(BF16)
    grad_rows = out_grad[...].T
    result_scr[...] = middle
    back_scr[...] = jnp.zeros_like(back_scr)
    width = grad_rows.shape[1]

    def ff_step(step, carry):
        start = pl.multiple_of(step * FF_STEP, FF_STEP)
        gate_at = pl.ds(start, FF_STEP)
        up_at = pl.ds(pl.multiple_of(ff + start, FF_STEP), FF_STEP)
        gate = mm(normed, in_weight[:, gate_at])
        up = mm(normed, in_weight[:, up_at])
        gated = 1.0 / (1.0 + jnp.exp(-gate))
        silu = gate * gated
        hidden = (silu * up).astype(BF16)
        down = down_weight[gate_at, :]
        result_scr[...] += mm(hidden, down)
        hidden_grad = mm(grad_rows, down, 1, 1)
        gate_grad = (hidden_grad * up * (gated * (1.0 + gate * (1.0 - gated)))).astype(BF16)
        up_grad = (hidden_grad * silu).astype(BF16)
        back_scr[...] += mm(gate_grad, in_weight[:, gate_at], 1, 1) + mm(
            up_grad, in_weight[:, up_at], 1, 1
        )
        tile_scr[:, gate_at] = mm(normed, gate_grad, 0, 0).astype(BF16)
        tile_scr[:, up_at] = mm(normed, up_grad, 0, 0).astype(BF16)
        down_scr[gate_at, :width] = mm(hidden, grad_rows, 0, 0).astype(BF16)
        return carry

    lax.fori_loop(0, ff // FF_STEP, ff_step, 0)

    put_tiles(in_outs, me, tile_scr, (0, 2 * ff), 0)
    base = 2 * (ff // LANES) * in_rows
    for out in in_outs:
        if base < out.shape[0]:
            out[base:, :] = jnp.zeros((out.shape[0] - base, LANES), BF16)
    whole = width // LANES * LANES
    put_tiles(outs, me, down_scr, (0, whole), 0)
    base = whole // LANES * down_rows
    half = down_rows // 2
    for relative, out in enumerate(outs):
        start = pl.multiple_of((me ^ relative) * down_rows, 16)
        rest = jnp.concatenate(
            [
                down_scr[pl.ds(start, half), whole:width],
                down_scr[pl.ds(pl.multiple_of(start + half, 16), half), whole:width],
            ],
            -1,
        )
        out[base : base + half, :] = rest
    base += half

    layer_out[...] = result_scr[...].astype(BF16).T
    middle_back, gain_terms = rms_back(middle, gain, back_scr[...])
    gain_grad[...] = jnp.zeros_like(gain_grad)
    gain_grad[0:1, :] = jnp.sum(gain_terms, 0, keepdims=True)
    middle_grad = middle_back + grad_rows.astype(F32)
    middle_grad_out[...] = middle_grad
    branch = middle_grad.astype(BF16)
    attended_grad_out[...] = mm(branch, out_weight[...], 1, 1).astype(BF16)
    out_weight_grad = mm(attended_low, branch, 0, 0).astype(BF16)
    wide = -(-width // LANES) * LANES
    tile_scr[:, :wide] = jnp.concatenate(
        [out_weight_grad, jnp.zeros((width, wide - width), BF16)], -1
    )
    put_tiles(outs, me, tile_scr, (0, wide), base)
    base += wide // LANES * in_rows
    for out in outs:
        out[base:, :] = jnp.zeros((out.shape[0] - base, LANES), BF16)


def put_small(outs, me, tile_scr, query_grad, kv_grad, query_weight, kv_weight, gains, ffn_gain_grad):
    width = query_grad.shape[0]
    wide = -(-width // LANES) * LANES
    gain_columns = gains[...].T
    terms = jnp.sum(query_grad * query_weight.astype(F32), -1, keepdims=True) + jnp.sum(
        kv_grad * kv_weight.astype(F32), -1, keepdims=True
    )
    columns = jnp.concatenate(
        [
            terms / gain_columns[:, 0:1],
            ffn_gain_grad[...].T[:, 0:1],
            jnp.zeros((width, wide - width - 2), F32),
        ],
        -1,
    )
    tile_scr[:, :wide] = jnp.concatenate([query_grad, columns], -1).astype(BF16)
    tile_scr[:, wide : wide + 2 * KVW] = kv_grad.astype(BF16)
    put_tiles(outs, me, tile_scr, (0, wide + 2 * KVW), 0)


def backward_kernel(
    index, queries, kv_all, attended, attended_grad, lse, normed, query_weight, kv_weight, gains,
    ffn_gain_grad, cosine, sine,
    *refs,
):
    q_scr, g_scr, delta_scr, acc_scr, query_grad_scr, masks = refs[-6:]
    fill_masks(masks)
    rows = queries.shape[0]
    blocks = kv_all.shape[0] // rows
    here = index[0]
    whole = normed.shape[0] > rows
    if whole:
        kv_grads, normed_grad, mine, along, send, tile_scr, weight_scr = refs[:-6]
        weight_scr[...] = jnp.zeros_like(weight_scr)
        kv_grads[...] = jnp.zeros_like(kv_grads)
    else:
        kv_grads, normed_grad, query_weight_grad = refs[:-6]
    for group in range(KV):
        q_scr[group] = stacked_heads(queries, group)
        grads = stacked_heads(attended_grad, group)
        g_scr[group] = grads
        terms = (grads.astype(F32) * stacked_heads(attended, group)).T
        delta_scr[group, 0:1, :] = jnp.sum(terms, 0, keepdims=True)
    acc_scr[...] = jnp.zeros_like(acc_scr)

    def step(j, carry):
        keys_at = block_at(j, rows)
        mask = jnp.concatenate([masks[jnp.where(j == here, 1, 0)]] * GROUPS, -1)
        key_grads = []
        value_grads = []
        for group in range(KV):
            keys = kv_all[keys_at, group * HD : (group + 1) * HD]
            values = kv_all[keys_at, KVW + group * HD : KVW + (group + 1) * HD]
            group_q = q_scr[group]
            group_g = g_scr[group]
            scores = mm(keys, group_q, 1, 1) + mask
            prob = jnp.exp(scores - lse[group : group + 1, :])
            prob_grad = mm(values, group_g, 1, 1)
            score_grad = (prob * (prob_grad - delta_scr[group, 0:1, :])).astype(BF16)
            value_grads.append(mm(prob.astype(BF16), group_g))
            key_grads.append(mm(score_grad, group_q))
            acc_scr[group] += mm(keys, score_grad, 0, 0)
        key_grad = jnp.concatenate(key_grads, -1)
        value_grad = jnp.concatenate(value_grads, -1)
        both = jnp.concatenate([key_grad, value_grad], -1).astype(BF16)
        if whole:
            across = (j ^ here) & 1
            distance = (j // 2 - here // 2) & (blocks // 2 - 1)
            kv_grads[across * (blocks // 2) + distance] = both
            turned = rotated(key_grad, cosine[keys_at, :], sine[keys_at, :], -1.0)
            linear = jnp.concatenate([turned, value_grad], -1).astype(BF16)
            weight_scr[...] += mm(normed[keys_at, :], linear, 0, 0)
        else:
            kv_grads[keys_at, :] = both
        return carry

    def clear(j, carry):
        kv_grads[block_at(j, rows), :] = jnp.zeros((rows, kv_grads.shape[1]), BF16)
        return carry

    lax.fori_loop(0, here + 1, step, 0)
    if not whole:
        lax.fori_loop(here + 1, blocks, clear, 0)
    for group in range(KV):
        for g in range(GROUPS):
            head = group * GROUPS + g
            part = acc_scr[group, :, g * rows : (g + 1) * rows]
            query_grad_scr[:, head * HD : (head + 1) * HD] = part.T
    tables = (table_at(cosine, here, rows), table_at(sine, here, rows))
    back = rotated(query_grad_scr[...], *tables, -1.0) * (1.0 / math.sqrt(HD))
    back = back.astype(BF16)
    own_normed = normed[block_at(here, rows), :] if whole else normed[...]
    query_grad = mm(own_normed, back, 0, 0)
    normed_grad[...] = mm(back, query_weight[...], 1, 1)
    if whole:
        outs = (mine, send.at[0], along, send.at[1])
        put_small(
            outs, index[1], tile_scr, query_grad, weight_scr[...], query_weight[...],
            kv_weight[...], gains, ffn_gain_grad,
        )
    else:
        query_weight_grad[...] = query_grad


def small_kernel(
    index, query_grad, kv_grad, query_weight, kv_weight, gains, ffn_gain_grad,
    mine, along, send, tile_scr,
):
    outs = (mine, send.at[0], along, send.at[1])
    for out in outs:
        out[...] = jnp.zeros(out.shape, BF16)
    put_small(
        outs, index[1], tile_scr, query_grad[...], kv_grad[...], query_weight[...], kv_weight[...],
        gains, ffn_gain_grad,
    )


def tail_kernel(
    tokens, gains, normed_grad, middle_grad, kv_weight, cosine, sine, *refs
):
    kv_parts, tokens_grad = refs[:-1], refs[-1]
    rows = normed_grad.shape[0]
    if len(kv_parts) == 1:

        def add(j, total):
            return total + kv_parts[0][block_at(j, rows), :].astype(F32)

        parts = kv_parts[0].shape[0] // rows
        kv_grad = lax.fori_loop(0, parts, add, jnp.zeros((rows, 2 * KVW), F32))
    else:
        column, *moved = kv_parts
        kv_grad = column[0].astype(F32)
        for part in moved:
            kv_grad = kv_grad + part[...].astype(F32)
    key_back = rotated(kv_grad[:, :KVW], cosine[...], sine[...], -1.0)
    back = jnp.concatenate([key_back, kv_grad[:, KVW:]], -1).astype(BF16)
    total = normed_grad[...] + mm(back, kv_weight[...], 1, 1)
    values = tokens[...].T.astype(F32)
    input_grad, _ = rms_back(values, gains[0:1, :], total)
    tokens_grad[...] = (middle_grad[...] + input_grad).astype(BF16).T


def spread_kernel(index, *refs, count):
    *terms, keep, send = refs
    here = index[0]
    rows = keep.shape[1]
    for distance in range(count // 2):
        for across, out in enumerate((keep, send)):
            owner = ((here ^ across) + 2 * distance) & (count - 1)
            at = pl.ds(pl.multiple_of(owner * rows, 16), rows)
            total = terms[0][at, :].astype(F32)
            for term in terms[1:]:
                total = total + term[at, :].astype(F32)
            out[distance] = total.astype(BF16)


def spread_both_kernel(index, mine, along, got, keep_mine, keep_along, send, count):
    spread_kernel(index, mine, got.at[0], keep_mine, send.at[0], count=count)
    spread_kernel(index, along, got.at[1], keep_along, send.at[1], count=count)


def flattened(index, pieces, parts):
    here = index[0]
    if len(pieces) == 1:
        (piece,) = pieces
        total = sum(rows for _, rows in parts)
        count = piece.shape[0] // total
        owners = [(owner, piece, owner * total) for owner in range(count)]
    else:
        count = 2 * pieces[0].shape[0]
        owners = [
            (((here ^ across) + (count - 2 * distance)) & (count - 1), column.at[distance], 0)
            for across, column in enumerate(pieces)
            for distance in range(count // 2)
        ]
    for owner, piece, start in owners:
        for flat, rows in parts:
            at = pl.ds(pl.multiple_of(owner * rows, 16), rows)
            flat[at, :] = piece[start : start + rows, :]
            start += rows


def untile(out, flat, base, columns):
    rows = out.shape[0]
    for tile in range(columns // LANES):
        out[:, tile * LANES : (tile + 1) * LANES] = flat[base : base + rows, :].astype(F32)
        base += rows
    return base


def gate_up_kernel(index, *refs, rows):
    pieces, (gate_out, up_out, flat) = refs[:-3], refs[-3:]
    flattened(index, pieces, [(flat, rows)])
    base = untile(gate_out, flat, 0, gate_out.shape[1])
    untile(up_out, flat, base, up_out.shape[1])


def outputs_kernel(index, *refs, rows, more_rows):
    down_out, out_out, query_out, key_out, value_out, gain_out, flat, small = refs[-8:]
    flattened(index, refs[:-8], [(flat, rows), (small, more_rows)])
    base = 0
    width, rows = down_out.shape
    whole = width // LANES * LANES
    for tile in range(whole // LANES):
        part = flat[base : base + rows, :].astype(F32)
        down_out[tile * LANES : (tile + 1) * LANES, :] = part.T
        base += rows
    half = rows // 2
    rest = flat[base : base + half, :].astype(F32).T
    down_out[whole:, :] = jnp.concatenate([rest[: width - whole], rest[width - whole :]], -1)
    base = untile(out_out, flat, base + half, whole)
    rows = out_out.shape[0]
    out_out[:, whole:] = flat[base : base + rows, : width - whole].astype(F32)
    base = untile(query_out, small, 0, whole)
    tile = small[base : base + rows, :].astype(F32)
    query_out[:, whole:] = tile[:, : width - whole]
    gain_out[...] = tile[:, width - whole : width - whole + 8].T
    base += rows
    both = [
        small[base + at * rows : base + (at + 1) * rows, :].astype(F32)
        for at in range(2 * KVW // LANES)
    ]
    both = jnp.concatenate(both, -1)
    key_out[...] = both[:, :KVW]
    value_out[...] = both[:, KVW:]


def swap(value, axis, bit):
    count = lax.axis_size(axis)
    return lax.ppermute(value, axis, [(i, i ^ (1 << bit)) for i in range(count)])


def gathered_ws(value):
    along = swap(value, "ws", 1)
    return value, swap(value, "ws", 0), along, swap(along, "ws", 0)


def gathered_ctx(value):
    count = lax.axis_size("ctx")
    if count != 8:
        return (lax.all_gather(value, "ctx", axis=0, tiled=True),)
    column = jnp.stack([value] + [shifted(value, by, False) for by in (1, 2, 3)])
    return column, swap(column, "ctx", 0)


def shifted(value, by, upward_only):
    count = lax.axis_size("ctx")
    pairs = [(i, i + 2 * by) for i in range(count)]
    if upward_only:
        pairs = [(i, j) for i, j in pairs if j < count]
    return lax.ppermute(value, "ctx", [(i, j % count) for i, j in pairs])


def rms_scale(values, gain_vec):
    return values * lax.rsqrt(jnp.mean(values * values, -1, keepdims=True) + EPS) * gain_vec


def added(*values):
    total = values[0].astype(F32)
    for value in values[1:]:
        total = total + value.astype(F32)
    return total.astype(values[0].dtype)


def scattered_ctx(values, counts):
    count = lax.axis_size("ctx")
    value = jnp.concatenate(
        [v.reshape(count, rows, LANES) for v, rows in zip(values, counts)], 1
    ).reshape(-1, LANES)
    parts = lax.all_to_all(value, "ctx", split_axis=0, concat_axis=0, tiled=True)
    parts = parts.reshape(count, -1, LANES).astype(F32)
    return jnp.sum(parts, 0).astype(value.dtype)


def rope_tables(positions):
    frequency = jnp.exp(jnp.arange(HD // 2).astype(F32) * (-2.0 * math.log(THETA) / HD))
    angles = positions.astype(F32)[:, None] * frequency[None, :]
    return jnp.cos(angles), jnp.sin(angles)


def turned_heads(values, cosine, sine):
    heads = values.reshape(values.shape[0], -1, 2, HD // 2)
    cosine, sine = cosine[:, None], sine[:, None]
    first, second = heads[:, :, 0], heads[:, :, 1]
    pair = [first * cosine - second * sine, second * cosine + first * sine]
    return jnp.stack(pair, 2).reshape(values.shape)


def scattered_parts(column, downward_only):
    count = lax.axis_size("ctx")
    parts = []
    for by in (1, 2, 3):
        pairs = [(i, i + 2 * by) for i in range(count)]
        if downward_only:
            pairs = [(i, j) for i, j in pairs if j >= count]
        parts.append(lax.ppermute(column[by], "ctx", [(i, j % count) for i, j in pairs]))
    return parts


def spread(index, terms):
    count = lax.axis_size("ctx")
    shape = shaped((count // 2, terms[0].shape[0] // count, LANES), BF16)
    return call(
        functools.partial(spread_kernel, count=count),
        (shape, shape),
        (index, *terms),
        micros=2,
        smem=1,
    )


def spread_both(index, mine, along, got):
    count = lax.axis_size("ctx")
    shape = shaped((count // 2, mine.shape[0] // count, LANES), BF16)
    return call(
        functools.partial(spread_both_kernel, count=count),
        (shape, shape, shaped((2,) + shape.shape, BF16)),
        (index, mine, along, got),
        micros=3,
        smem=1,
    )


def padded_rows(rows, count):
    return -(-rows // (16 * count)) * 16 * count


def body(
    tokens,
    attn_gain,
    query_weight,
    key_weight,
    value_weight,
    output_weight,
    ffn_gain,
    gate_weight,
    up_weight,
    down_weight,
    out_grad,
):
    seq_count, rows, width = tokens.shape
    ctx_count = lax.axis_size("ctx")
    owners = lax.axis_size("ws")
    slice_rows = query_weight.shape[0]
    ff = gate_weight.shape[1]
    wide = -(-width // LANES) * LANES
    by_hops = ctx_count == 8
    tokens = tokens.reshape(rows, width).T
    out_grad = out_grad.reshape(rows, width).T
    ctx_index = lax.axis_index("ctx")
    index = jnp.stack([ctx_index, lax.axis_index("ws")]).astype(jnp.int32)

    if by_hops:
        behind_two = shifted(tokens, 2, True)

    gains = jnp.concatenate([attn_gain, ffn_gain]).reshape(2, slice_rows)
    packed = jnp.concatenate(
        [
            jnp.concatenate([key_weight, value_weight, query_weight], -1),
            jnp.pad(gains, ((0, 14), (0, 2 * KVW + width - slice_rows))),
        ],
        0,
    )
    packs = gathered_ws(packed)
    in_weight = jnp.concatenate([gate_weight, up_weight, output_weight], -1)
    in_along = swap(in_weight, "ws", 1)
    down_along = swap(down_weight, "ws", 1)

    def wide_tables(positions):
        cosine, sine = rope_tables(positions)
        return jnp.concatenate([cosine] * 4, -1), jnp.concatenate([-sine, sine] * 2, -1)

    first_pos = ctx_index * rows
    cosine, sine = wide_tables(first_pos + jnp.arange(rows, dtype=jnp.int32))
    if by_hops:
        tables = wide_tables(jnp.arange(ctx_count * rows, dtype=jnp.int32))
        later_tokens, tables = lax.optimization_barrier((tokens, tables))
        behind_one = shifted(later_tokens, 1, True)
        mate = swap(later_tokens, "ctx", 0)
        behind_three = shifted(behind_two, 1, True)
    else:
        tables = (cosine, sine)

    places = (0, 1, 4) if by_hops else (0,)
    late_places = (2, 5, 3, 6, 7) if by_hops else ()
    early = (tokens, mate, behind_two) if by_hops else (tokens,)
    early_normed, early_kv, queries, full_query, full_kv, gains = call(
        functools.partial(early_kernel, places=places, slice_rows=slice_rows),
        (
            shaped((len(places), rows, width), BF16),
            shaped((len(places), rows, 2 * KVW), BF16),
            shaped((rows, width), BF16),
            shaped((width, width), BF16),
            shaped((width, 2 * KVW), BF16),
            shaped((8, width), F32),
        ),
        (index,) + packs + tables + early,
        scratch=(
            pltpu.VMEM((owners * 16, 2 * LANES), BF16),
            pltpu.VMEM((len(places), width, rows), BF16),
        ),
        micros=6,
        smem=1,
        vmem=60,
    )
    if by_hops:
        behind_three, queries = lax.optimization_barrier((behind_three, queries))
        late = (
            behind_one,
            swap(behind_two, "ctx", 0),
            swap(behind_one, "ctx", 0),
            behind_three,
            swap(behind_three, "ctx", 0),
        )
        normed_shape = (shaped((ctx_count * rows, width), BF16),)
        raw_scr = (pltpu.VMEM((len(late_places), width, rows), BF16),)
    else:
        tokens_all = lax.all_gather(tokens.T, "ctx", axis=0, tiled=True).astype(F32)
        normed_all = rms_scale(tokens_all, gains[0]).astype(BF16)
        linear = jnp.dot(normed_all, full_kv, preferred_element_type=F32)
        full_tables = rope_tables(jnp.arange(ctx_count * rows, dtype=jnp.int32))
        early_kv = jnp.concatenate(
            [turned_heads(linear[:, :KVW], *full_tables), linear[:, KVW:]], -1
        ).astype(BF16)
        late = ()
        normed_shape = ()
        raw_scr = ()

    late, in_weight, down_weight, in_along = lax.optimization_barrier(
        (late, in_weight, down_weight, in_along)
    )
    in_pieces = (in_weight, swap(in_weight, "ws", 0), in_along, swap(in_along, "ws", 0))
    down_core = swap(down_weight, "ws", 0)

    attended, lse, kv_all, *normed_out = call(
        functools.partial(forward_kernel, places=places, late_places=late_places),
        (
            shaped((rows, width), F32),
            shaped((8, GROUPS * rows), F32),
            shaped((ctx_count * rows, 2 * KVW), BF16),
            *normed_shape,
        ),
        (index, queries, early_normed, early_kv, full_kv, gains, *tables, *late),
        scratch=(
            *raw_scr,
            pltpu.VMEM((KV, GROUPS * rows, HD), BF16),
            pltpu.VMEM((KV, HD, GROUPS * rows), F32),
            pltpu.VMEM((KV, 8, GROUPS * rows), F32),
            pltpu.VMEM((KV, 8, GROUPS * rows), F32),
            pltpu.VMEM((2, rows, rows), F32),
        ),
        micros=20,
        smem=1,
        vmem=60,
    )

    attended, down_along = lax.optimization_barrier((attended, down_along))
    down_pieces = (down_weight, down_core, down_along, swap(down_along, "ws", 0))

    first_count = padded_rows(2 * slice_rows * ff // LANES, ctx_count)
    second_count = padded_rows(((ff // owners) * width + slice_rows * wide) // LANES, ctx_count)
    small_count = padded_rows(slice_rows * (wide + 2 * KVW) // LANES, ctx_count)
    first_rows, second_rows, small_rows = (
        rows_of // ctx_count for rows_of in (first_count, second_count, small_count)
    )

    def tile_shapes(rows_of):
        return (
            shaped((rows_of, LANES), BF16),
            shaped((rows_of, LANES), BF16),
            shaped((2, rows_of, LANES), BF16),
        )

    layer_out, middle_grad, attended_grad, ffn_gain_grad, *tiles = call(
        ffn_kernel,
        (
            shaped((width, rows), BF16),
            shaped((rows, width), F32),
            shaped((rows, width), BF16),
            shaped((8, width), F32),
            *tile_shapes(first_count),
            *tile_shapes(second_count),
        ),
        (index, tokens, attended, gains, out_grad) + in_pieces + down_pieces,
        scratch=(
            pltpu.VMEM((width, 2 * ff + width), BF16),
            pltpu.VMEM((ff, width), BF16),
            pltpu.VMEM((rows, width), F32),
            pltpu.VMEM((rows, width), F32),
            pltpu.VMEM((width, 2 * ff), BF16),
            pltpu.VMEM((ff, wide), BF16),
        ),
        micros=14,
        smem=1,
        vmem=60,
    )

    in_mine, in_along, in_send, mine, along, send = tiles
    in_got = swap(in_send, "ws", 0)
    got = swap(send, "ws", 0)
    in_crossing = added(in_along, in_got[1])
    if by_hops:
        keep_mine, keep_along, to_mate = spread_both(index, mine, along, got)
    else:
        to_mate = added(along, got[1])
    attended_grad, in_crossing, to_mate = lax.optimization_barrier(
        (attended_grad, in_crossing, to_mate)
    )
    in_crossed = swap(in_crossing, "ws", 1)
    from_mate = swap(to_mate, "ctx", 0) if by_hops else swap(to_mate, "ws", 1)

    tile_scr = pltpu.VMEM((width, wide + 2 * KVW), BF16)
    if by_hops:
        kv_shape = shaped((ctx_count, rows, 2 * KVW), BF16)
        backward_normed = normed_out[0]
        more_shapes = tile_shapes(small_count)
        more_scratch = (tile_scr, pltpu.VMEM((width, 2 * KVW), F32))
    else:
        kv_shape = shaped((ctx_count * rows, 2 * KVW), BF16)
        backward_normed = early_normed[0]
        more_shapes = (shaped((width, width), F32),)
        more_scratch = ()
    kv_grads, normed_grad, *small = call(
        backward_kernel,
        (kv_shape, shaped((rows, width), F32), *more_shapes),
        (
            index, queries, kv_all, attended, attended_grad, lse, backward_normed, full_query,
            full_kv, gains, ffn_gain_grad, *tables,
        ),
        scratch=(
            *more_scratch,
            pltpu.VMEM((KV, GROUPS * rows, HD), BF16),
            pltpu.VMEM((KV, GROUPS * rows, HD), BF16),
            pltpu.VMEM((KV, 8, GROUPS * rows), F32),
            pltpu.VMEM((KV, HD, GROUPS * rows), F32),
            pltpu.VMEM((rows, width), F32),
            pltpu.VMEM((2, rows, rows), F32),
        ),
        micros=23,
        smem=1,
        vmem=32 if by_hops else 60,
    )
    if not by_hops:
        linear = turned_heads(kv_grads[:, :KVW].astype(F32), full_tables[0], -full_tables[1])
        linear = jnp.concatenate([linear.astype(BF16), kv_grads[:, KVW:]], -1)
        kv_weight_grad = jnp.einsum("nd,nh->dh", normed_all, linear, preferred_element_type=F32)
        small = call(
            small_kernel,
            tile_shapes(small_count),
            (index, small[0], kv_weight_grad, full_query, full_kv, gains, ffn_gain_grad),
            scratch=(tile_scr,),
            smem=1,
        )
    kv_grads, small, in_crossed, from_mate = lax.optimization_barrier(
        (kv_grads, tuple(small), in_crossed, from_mate)
    )
    small_mine, small_along, small_send = small
    small_got = swap(small_send, "ws", 0)
    small_crossed = swap(added(small_along, small_got[1]), "ws", 1)

    if by_hops:
        in_keep, in_to_mate = spread(index, (in_mine, in_got[0], in_crossed))
        in_from_mate = swap(in_to_mate, "ctx", 0)
        crossed = swap(added(keep_along, from_mate[1]), "ws", 1)
        in_from_mate, crossed, small_crossed = lax.optimization_barrier(
            (in_from_mate, crossed, small_crossed)
        )
        small_keep, small_to_mate = spread(index, (small_mine, small_got[0], small_crossed))
        small_to_mate, kv_to_mate = lax.optimization_barrier(
            (small_to_mate, kv_grads[ctx_count // 2 :])
        )
        small_from_mate = swap(small_to_mate, "ctx", 0)
        kv_from_mate = swap(kv_to_mate, "ctx", 0)
        in_column = added(in_keep, in_from_mate)
        in_share = added(in_column[0], *scattered_parts(in_column, False))
        column = jnp.concatenate(
            [added(keep_mine, from_mate[0], crossed), added(small_keep, small_from_mate)], 1
        )
        share = added(column[0], *scattered_parts(column, False))
        kv_column = added(kv_grads[: ctx_count // 2], kv_from_mate)
        kv_parts = (kv_column, *scattered_parts(kv_column, True))
    else:
        kv_parts = (lax.all_to_all(kv_grads, "ctx", split_axis=0, concat_axis=0, tiled=True),)
        in_total = added(in_mine, in_got[0], in_crossed)
        total = added(mine, got[0], from_mate)
        small_total = added(small_mine, small_got[0], small_crossed)
        in_share = scattered_ctx((in_total,), (first_rows,))
        share = scattered_ctx((total, small_total), (second_rows, small_rows))
    in_pieces = gathered_ctx(in_share)
    pieces = gathered_ctx(share)

    tokens_grad = call(
        tail_kernel,
        shaped((width, rows), BF16),
        (
            tokens, gains, normed_grad, middle_grad, full_kv, cosine, sine, *kv_parts,
        ),
        micros=4,
        vmem=16 if by_hops else 60,
    )

    gate_weight_grad, up_weight_grad = call(
        functools.partial(gate_up_kernel, rows=first_rows),
        (shaped(gate_weight.shape, F32), shaped(up_weight.shape, F32)),
        (index,) + in_pieces,
        scratch=(pltpu.VMEM((first_count, LANES), BF16),),
        micros=3,
        smem=1,
    )
    (
        down_weight_grad,
        output_weight_grad,
        query_weight_grad,
        key_weight_grad,
        value_weight_grad,
        gain_grads,
    ) = call(
        functools.partial(outputs_kernel, rows=second_rows, more_rows=small_rows),
        (
            shaped(down_weight.shape[::-1], F32),
            shaped(output_weight.shape, F32),
            shaped(query_weight.shape, F32),
            shaped(key_weight.shape, F32),
            shaped(value_weight.shape, F32),
            shaped((8, slice_rows), F32),
        ),
        (index,) + pieces,
        scratch=(pltpu.VMEM((second_count, LANES), BF16), pltpu.VMEM((small_count, LANES), BF16)),
        micros=3,
        smem=1,
    )
    return (
        layer_out.T.reshape(seq_count, rows, width),
        tokens_grad.T.reshape(seq_count, rows, width),
        gain_grads[0],
        query_weight_grad,
        key_weight_grad,
        value_weight_grad,
        output_weight_grad,
        gain_grads[1],
        gate_weight_grad,
        up_weight_grad,
        down_weight_grad.T,
    )


def solution(mesh):
    in_specs = (
        P("ws", "ctx", None),
        P("ws"),
        P("ws", None),
        P("ws", None),
        P("ws", None),
        P("ws", None),
        P("ws"),
        P("ws", None),
        P("ws", None),
        P("ws", None),
        P("ws", "ctx", None),
    )
    out_specs = (
        P("ws", "ctx", None),
        P("ws", "ctx", None),
        P("ws"),
        P("ws", None),
        P("ws", None),
        P("ws", None),
        P("ws", None),
        P("ws"),
        P("ws", None),
        P("ws", None),
        P("ws", None),
    )
    return jax.shard_map(body, mesh=mesh, in_specs=in_specs, out_specs=out_specs, check_vma=False)
```

```python
import functools
import math

import jax
import jax.numpy as jnp
from jax import lax
from jax.experimental import pallas as pl
from jax.experimental.pallas import tpu as pltpu
from jax.sharding import PartitionSpec as P

H = 9
KV = 3
HD = 64
GROUPS = H // KV
KVW = KV * HD

EPS = 1e-05
THETA = 100000.0
NEGATIVE = -1e30
LANES = 128
FF_STEP = 256
MIB = 1024 * 1024

BF16 = jnp.bfloat16
F32 = jnp.float32

SMEM_SPEC = pl.BlockSpec(memory_space=pltpu.SMEM)
VMEM_SPEC = pl.BlockSpec(memory_space=pltpu.VMEM)


def mm(left, right, left_dim=1, right_dim=0):
    return lax.dot_general(
        left, right, (((left_dim,), (right_dim,)), ((), ())), preferred_element_type=F32
    )


def call(kernel, outs, args, scratch=(), micros=1, smem=0, vmem=16):
    return pl.pallas_call(
        kernel,
        out_shape=outs,
        in_specs=[SMEM_SPEC] * smem + [VMEM_SPEC] * (len(args) - smem),
        out_specs=jax.tree.map(lambda _: VMEM_SPEC, outs),
        scratch_shapes=list(scratch),
        compiler_params=pltpu.CompilerParams(vmem_limit_bytes=vmem * MIB),
        cost_estimate=pl.CostEstimate(
            flops=micros * 1_000_000_000, bytes_accessed=0, transcendentals=0
        ),
    )(*args)


def shaped(shape, dtype):
    return jax.ShapeDtypeStruct(tuple(shape), dtype)


def swap_halves(part):
    lane = lax.broadcasted_iota(jnp.int32, part.shape, 1)
    return jnp.where(
        lane % HD < HD // 2,
        pltpu.roll(part, LANES - HD // 2, axis=1),
        pltpu.roll(part, HD // 2, axis=1),
    )


def rotated(values, cosine, signed_sine, sign):
    rows, width = values.shape
    parts = []
    for start in range(0, width, LANES):
        part = values[:, start : start + LANES]
        used = part.shape[1]
        if used < LANES:
            part = jnp.concatenate([part, jnp.zeros((rows, LANES - used), F32)], -1)
        turned = part * cosine + sign * (swap_halves(part) * signed_sine)
        parts.append(turned[:, :used])
    return jnp.concatenate(parts, -1)


def stacked_heads(ref, group):
    first = group * GROUPS
    return jnp.concatenate(
        [ref[:, (first + g) * HD : (first + g + 1) * HD] for g in range(GROUPS)], 0
    )


def assembled(full, pieces, me):
    rows = pieces[0].shape[0]
    for relative, piece in enumerate(pieces):
        start = pl.multiple_of((me ^ relative) * rows, 16)
        full[pl.ds(start, rows), :] = piece[...]


def projected(tokens, gain, weight, cosine, sine):
    values = tokens.astype(F32)
    scale = lax.rsqrt(jnp.mean(values * values, -1, keepdims=True) + EPS)
    normed = (values * scale * gain).astype(BF16)
    linear = mm(normed, weight)
    keys = rotated(linear[:, :KVW], cosine, sine, 1.0)
    return normed, jnp.concatenate([keys, linear[:, KVW:]], -1).astype(BF16)


def block_at(index, rows):
    return pl.ds(pl.multiple_of(index * rows, rows), rows)


def owner_of(place, here):
    return (here ^ (place % 2)) - 2 * (place // 2)


def table_at(table, owner, rows):
    if table.shape[0] == rows:
        return table[...]
    return table[block_at(jnp.clip(owner, 0, table.shape[0] // rows - 1), rows), :]


def early_kernel(index, here_pair, core_pair, cosine, sine, *refs, places, slice_rows):
    pieces = refs[: len(places)]
    (
        normed_out, kv_out, query_out, query_weight, kv_weight, gains_out, gain_scr, raw_scr,
    ) = refs[len(places) :]
    here = index[0]
    packs = (here_pair.at[0], core_pair.at[0], here_pair.at[1], core_pair.at[1])
    more = packs[0].shape[0] - slice_rows
    for relative, pack in enumerate(packs):
        owner = index[1] ^ relative
        at = pl.ds(pl.multiple_of(owner * slice_rows, 16), slice_rows)
        kv_weight[at, :] = pack[:slice_rows, : 2 * KVW]
        query_weight[at, :] = pack[:slice_rows, 2 * KVW :]
        gain_scr[pl.ds(pl.multiple_of(owner * more, 16), more), :] = pack[
            slice_rows:, : gain_scr.shape[1]
        ]
    gains = jnp.concatenate(
        [
            gain_scr[owner * more : owner * more + 8, :slice_rows].astype(F32)
            for owner in range(len(packs))
        ],
        -1,
    )
    gains_out[...] = gains
    rows = normed_out.shape[1]
    for slot, piece in enumerate(pieces):
        raw_scr[slot] = piece[...]

    def project(slot, carry):
        owner = owner_of(one_of(places, slot), here)
        tables = [table_at(table, owner, rows) for table in (cosine, sine)]
        normed, kv = projected(raw_scr[slot].T, gains_out[0:1, :], kv_weight[...], *tables)
        normed_out[slot] = normed
        kv_out[slot] = kv
        return carry

    lax.fori_loop(0, len(places), project, 0)
    tables = [table_at(table, here, rows) for table in (cosine, sine)]
    linear = mm(normed_out[0], query_weight[...])
    query_out[...] = (rotated(linear, *tables, 1.0) * (1.0 / math.sqrt(HD))).astype(BF16)


def fill_masks(masks):
    shape = masks.shape[1:]
    key_pos = lax.broadcasted_iota(jnp.int32, shape, 0)
    query_pos = lax.broadcasted_iota(jnp.int32, shape, 1)
    masks[0] = jnp.zeros(shape, F32)
    masks[1] = jnp.where(query_pos >= key_pos, 0.0, NEGATIVE)


def one_of(values, at):
    found = values[0]
    for place, value in enumerate(values[1:], 1):
        found = jnp.where(at == place, value, found)
    return found


def forward_kernel(
    index, queries, early_normed, early_kv, kv_weight, gains, cosine, sine, *refs, places, late_places
):
    late, rest = refs[: len(late_places)], refs[len(late_places) :]
    attended, lse_out, kv_all, *rest = rest
    q_scr, acc_scr, max_scr, sum_scr, masks = rest[-5:]
    fill_masks(masks)
    rows = queries.shape[0]
    here = index[0]
    if late_places:
        normed_all, raw_scr = rest[:2]
        for slot, piece in enumerate(late):
            raw_scr[slot] = piece[...]

        def copy(slot, carry):
            owner = owner_of(one_of(places, slot), here)

            @pl.when((owner >= 0) & (owner <= here))
            def _():
                normed_all[block_at(owner, rows), :] = early_normed[slot]
                kv_all[block_at(owner, rows), :] = early_kv[slot]

            return carry

        def project(slot, carry):
            owner = owner_of(one_of(late_places, slot), here)

            @pl.when((owner >= 0) & (owner <= here))
            def _():
                normed, kv = projected(
                    raw_scr[slot].T,
                    gains[0:1, :],
                    kv_weight[...],
                    table_at(cosine, owner, rows),
                    table_at(sine, owner, rows),
                )
                normed_all[block_at(owner, rows), :] = normed
                kv_all[block_at(owner, rows), :] = kv

            return carry

        lax.fori_loop(0, len(places), copy, 0)
        lax.fori_loop(0, len(late_places), project, 0)
    else:
        kv_all[...] = early_kv[...]

    for group in range(KV):
        q_scr[group] = stacked_heads(queries, group)
    acc_scr[...] = jnp.zeros_like(acc_scr)
    max_scr[...] = jnp.full_like(max_scr, NEGATIVE)
    sum_scr[...] = jnp.zeros_like(sum_scr)

    def step(j, carry):
        keys_at = block_at(j, rows)
        mask = jnp.concatenate([masks[jnp.where(j == here, 1, 0)]] * GROUPS, -1)
        for group in range(KV):
            keys = kv_all[keys_at, group * HD : (group + 1) * HD]
            values = kv_all[keys_at, KVW + group * HD : KVW + (group + 1) * HD]
            scores = mm(keys, q_scr[group], 1, 1) + mask
            old_max = max_scr[group, 0:1, :]
            new_max = jnp.maximum(old_max, jnp.max(scores, 0, keepdims=True))
            weights = jnp.exp(scores - new_max)
            factor = jnp.exp(old_max - new_max)
            max_scr[group, 0:1, :] = new_max
            sum_scr[group, 0:1, :] = sum_scr[group, 0:1, :] * factor + jnp.sum(
                weights, 0, keepdims=True
            )
            acc_scr[group] = acc_scr[group] * factor + mm(values, weights.astype(BF16), 0, 0)
        return carry

    lax.fori_loop(0, here + 1, step, 0)
    lse_out[...] = jnp.zeros_like(lse_out)
    for group in range(KV):
        total = sum_scr[group, 0:1, :]
        result = acc_scr[group] / total
        lse_out[group : group + 1, :] = max_scr[group, 0:1, :] + jnp.log(total)
        for g in range(GROUPS):
            head = group * GROUPS + g
            attended[:, head * HD : (head + 1) * HD] = result[:, g * rows : (g + 1) * rows].T


def rms_back(values, gain, grad):
    width = values.shape[-1]
    scale = lax.rsqrt(jnp.mean(values * values, -1, keepdims=True) + EPS)
    scaled = values * scale
    pulled = grad * gain
    along = jnp.sum(pulled * scaled, -1, keepdims=True) * (1.0 / width)
    return scale * (pulled - scaled * along), grad * scaled


def put_tiles(outs, me, grads, grad_lanes, first_row):
    rows = grads.shape[0] // len(outs)
    first, last = grad_lanes
    for relative, out in enumerate(outs):
        start = pl.multiple_of((me ^ relative) * rows, 16)
        for tile in range((last - first) // LANES):
            at = first + tile * LANES
            out[first_row + tile * rows : first_row + (tile + 1) * rows, :] = grads[
                pl.ds(start, rows), at : at + LANES
            ]


def ffn_kernel(
    index, tokens, attended, gains, out_grad,
    wi0, wi1, wi2, wi3, wd0, wd1, wd2, wd3,
    layer_out, middle_grad_out, attended_grad_out, gain_grad,
    in_mine, in_along, in_send, mine, along, send,
    in_weight, down_weight, result_scr, back_scr, tile_scr, down_scr,
):
    me = index[1]
    assembled(in_weight, (wi0, wi1, wi2, wi3), me)
    assembled(down_weight, (wd0, wd1, wd2, wd3), me)
    in_outs = (in_mine, in_send.at[0], in_along, in_send.at[1])
    outs = (mine, send.at[0], along, send.at[1])
    gain = gains[1:2, :]
    ff = down_weight.shape[0]
    out_weight = in_weight.at[:, 2 * ff :]
    owners = len(outs)
    in_rows = in_weight.shape[0] // owners
    down_rows = ff // owners
    attended_low = attended[...].astype(BF16)
    middle = tokens[...].T.astype(F32) + mm(attended_low, out_weight[...])
    scale = lax.rsqrt(jnp.mean(middle * middle, -1, keepdims=True) + EPS)
    normed = (middle * scale * gain).astype(BF16)
    grad_rows = out_grad[...].T
    result_scr[...] = middle
    back_scr[...] = jnp.zeros_like(back_scr)
    width = grad_rows.shape[1]

    def ff_step(step, carry):
        start = pl.multiple_of(step * FF_STEP, FF_STEP)
        gate_at = pl.ds(start, FF_STEP)
        up_at = pl.ds(pl.multiple_of(ff + start, FF_STEP), FF_STEP)
        gate = mm(normed, in_weight[:, gate_at])
        up = mm(normed, in_weight[:, up_at])
        gated = 1.0 / (1.0 + jnp.exp(-gate))
        silu = gate * gated
        hidden = (silu * up).astype(BF16)
        down = down_weight[gate_at, :]
        result_scr[...] += mm(hidden, down)
        hidden_grad = mm(grad_rows, down, 1, 1)
        gate_grad = (hidden_grad * up * (gated * (1.0 + gate * (1.0 - gated)))).astype(BF16)
        up_grad = (hidden_grad * silu).astype(BF16)
        back_scr[...] += mm(gate_grad, in_weight[:, gate_at], 1, 1) + mm(
            up_grad, in_weight[:, up_at], 1, 1
        )
        tile_scr[:, gate_at] = mm(normed, gate_grad, 0, 0).astype(BF16)
        tile_scr[:, up_at] = mm(normed, up_grad, 0, 0).astype(BF16)
        down_scr[gate_at, :width] = mm(hidden, grad_rows, 0, 0).astype(BF16)
        return carry

    lax.fori_loop(0, ff // FF_STEP, ff_step, 0)

    put_tiles(in_outs, me, tile_scr, (0, 2 * ff), 0)
    base = 2 * (ff // LANES) * in_rows
    for out in in_outs:
        if base < out.shape[0]:
            out[base:, :] = jnp.zeros((out.shape[0] - base, LANES), BF16)
    whole = width // LANES * LANES
    put_tiles(outs, me, down_scr, (0, whole), 0)
    base = whole // LANES * down_rows
    half = down_rows // 2
    for relative, out in enumerate(outs):
        start = pl.multiple_of((me ^ relative) * down_rows, 16)
        rest = jnp.concatenate(
            [
                down_scr[pl.ds(start, half), whole:width],
                down_scr[pl.ds(pl.multiple_of(start + half, 16), half), whole:width],
            ],
            -1,
        )
        out[base : base + half, :] = rest
    base += half

    layer_out[...] = result_scr[...].astype(BF16).T
    middle_back, gain_terms = rms_back(middle, gain, back_scr[...])
    gain_grad[...] = jnp.zeros_like(gain_grad)
    gain_grad[0:1, :] = jnp.sum(gain_terms, 0, keepdims=True)
    middle_grad = middle_back + grad_rows.astype(F32)
    middle_grad_out[...] = middle_grad
    branch = middle_grad.astype(BF16)
    attended_grad_out[...] = mm(branch, out_weight[...], 1, 1).astype(BF16)
    out_weight_grad = mm(attended_low, branch, 0, 0).astype(BF16)
    wide = -(-width // LANES) * LANES
    tile_scr[:, :wide] = jnp.concatenate(
        [out_weight_grad, jnp.zeros((width, wide - width), BF16)], -1
    )
    put_tiles(outs, me, tile_scr, (0, wide), base)
    base += wide // LANES * in_rows
    for out in outs:
        out[base:, :] = jnp.zeros((out.shape[0] - base, LANES), BF16)


def put_small(outs, me, tile_scr, query_grad, kv_grad, query_weight, kv_weight, gains, ffn_gain_grad):
    width = query_grad.shape[0]
    wide = -(-width // LANES) * LANES
    gain_columns = gains[...].T
    terms = jnp.sum(query_grad * query_weight.astype(F32), -1, keepdims=True) + jnp.sum(
        kv_grad * kv_weight.astype(F32), -1, keepdims=True
    )
    columns = jnp.concatenate(
        [
            terms / gain_columns[:, 0:1],
            ffn_gain_grad[...].T[:, 0:1],
            jnp.zeros((width, wide - width - 2), F32),
        ],
        -1,
    )
    tile_scr[:, :wide] = jnp.concatenate([query_grad, columns], -1).astype(BF16)
    tile_scr[:, wide : wide + 2 * KVW] = kv_grad.astype(BF16)
    put_tiles(outs, me, tile_scr, (0, wide + 2 * KVW), 0)


def backward_kernel(
    index, queries, kv_all, attended, attended_grad, lse, normed, query_weight, kv_weight, gains,
    ffn_gain_grad, cosine, sine,
    *refs,
):
    q_scr, g_scr, delta_scr, acc_scr, query_grad_scr, masks = refs[-6:]
    fill_masks(masks)
    rows = queries.shape[0]
    blocks = kv_all.shape[0] // rows
    here = index[0]
    whole = normed.shape[0] > rows
    if whole:
        kv_grads, normed_grad, mine, along, send, tile_scr, weight_scr = refs[:-6]
        weight_scr[...] = jnp.zeros_like(weight_scr)
        kv_grads[...] = jnp.zeros_like(kv_grads)
    else:
        kv_grads, normed_grad, query_weight_grad = refs[:-6]
    for group in range(KV):
        q_scr[group] = stacked_heads(queries, group)
        grads = stacked_heads(attended_grad, group)
        g_scr[group] = grads
        terms = (grads.astype(F32) * stacked_heads(attended, group)).T
        delta_scr[group, 0:1, :] = jnp.sum(terms, 0, keepdims=True)
    acc_scr[...] = jnp.zeros_like(acc_scr)

    def step(j, carry):
        keys_at = block_at(j, rows)
        mask = jnp.concatenate([masks[jnp.where(j == here, 1, 0)]] * GROUPS, -1)
        key_grads = []
        value_grads = []
        for group in range(KV):
            keys = kv_all[keys_at, group * HD : (group + 1) * HD]
            values = kv_all[keys_at, KVW + group * HD : KVW + (group + 1) * HD]
            group_q = q_scr[group]
            group_g = g_scr[group]
            scores = mm(keys, group_q, 1, 1) + mask
            prob = jnp.exp(scores - lse[group : group + 1, :])
            prob_grad = mm(values, group_g, 1, 1)
            score_grad = (prob * (prob_grad - delta_scr[group, 0:1, :])).astype(BF16)
            value_grads.append(mm(prob.astype(BF16), group_g))
            key_grads.append(mm(score_grad, group_q))
            acc_scr[group] += mm(keys, score_grad, 0, 0)
        key_grad = jnp.concatenate(key_grads, -1)
        value_grad = jnp.concatenate(value_grads, -1)
        both = jnp.concatenate([key_grad, value_grad], -1).astype(BF16)
        if whole:
            apart = j ^ here
            kv_grads[(apart & 1) * (blocks // 2) + apart // 2] = both
            turned = rotated(key_grad, cosine[keys_at, :], sine[keys_at, :], -1.0)
            linear = jnp.concatenate([turned, value_grad], -1).astype(BF16)
            weight_scr[...] += mm(normed[keys_at, :], linear, 0, 0)
        else:
            kv_grads[keys_at, :] = both
        return carry

    def clear(j, carry):
        kv_grads[block_at(j, rows), :] = jnp.zeros((rows, kv_grads.shape[1]), BF16)
        return carry

    lax.fori_loop(0, here + 1, step, 0)
    if not whole:
        lax.fori_loop(here + 1, blocks, clear, 0)
    for group in range(KV):
        for g in range(GROUPS):
            head = group * GROUPS + g
            part = acc_scr[group, :, g * rows : (g + 1) * rows]
            query_grad_scr[:, head * HD : (head + 1) * HD] = part.T
    tables = (table_at(cosine, here, rows), table_at(sine, here, rows))
    back = rotated(query_grad_scr[...], *tables, -1.0) * (1.0 / math.sqrt(HD))
    back = back.astype(BF16)
    own_normed = normed[block_at(here, rows), :] if whole else normed[...]
    query_grad = mm(own_normed, back, 0, 0)
    normed_grad[...] = mm(back, query_weight[...], 1, 1)
    if whole:
        outs = (mine, send.at[0], along, send.at[1])
        put_small(
            outs, index[1], tile_scr, query_grad, weight_scr[...], query_weight[...],
            kv_weight[...], gains, ffn_gain_grad,
        )
    else:
        query_weight_grad[...] = query_grad


def small_kernel(
    index, query_grad, kv_grad, query_weight, kv_weight, gains, ffn_gain_grad,
    mine, along, send, tile_scr,
):
    outs = (mine, send.at[0], along, send.at[1])
    for out in outs:
        out[...] = jnp.zeros(out.shape, BF16)
    put_small(
        outs, index[1], tile_scr, query_grad[...], kv_grad[...], query_weight[...], kv_weight[...],
        gains, ffn_gain_grad,
    )


def tail_kernel(
    tokens, gains, normed_grad, middle_grad, kv_weight, cosine, sine, *refs
):
    kv_parts, tokens_grad = refs[:-1], refs[-1]
    rows = normed_grad.shape[0]
    if kv_parts[0].shape[0] > rows:

        def add(j, total):
            return total + kv_parts[0][block_at(j, rows), :].astype(F32)

        parts = kv_parts[0].shape[0] // rows
        kv_grad = lax.fori_loop(0, parts, add, jnp.zeros((rows, 2 * KVW), F32))
    else:
        kv_grad = kv_parts[0][...].astype(F32)
    key_back = rotated(kv_grad[:, :KVW], cosine[...], sine[...], -1.0)
    back = jnp.concatenate([key_back, kv_grad[:, KVW:]], -1).astype(BF16)
    total = normed_grad[...] + mm(back, kv_weight[...], 1, 1)
    values = tokens[...].T.astype(F32)
    input_grad, _ = rms_back(values, gains[0:1, :], total)
    tokens_grad[...] = (middle_grad[...] + input_grad).astype(BF16).T


def spread_kernel(index, *refs, count):
    *terms, keep, send = refs
    here = index[0]
    rows = keep.shape[1]
    for apart in range(count):
        at = pl.ds(pl.multiple_of((here ^ apart) * rows, 16), rows)
        total = terms[0][at, :].astype(F32)
        for term in terms[1:]:
            total = total + term[at, :].astype(F32)
        (send if apart & 1 else keep)[apart // 2] = total.astype(BF16)


def spread_both_kernel(index, mine, along, got, keep_mine, keep_along, send, count):
    spread_kernel(index, mine, got.at[0], keep_mine, send.at[0], count=count)
    spread_kernel(index, along, got.at[1], keep_along, send.at[1], count=count)


def flattened(index, pieces, parts):
    here = index[0]
    if len(pieces) == 1:
        (piece,) = pieces
        total = sum(rows for _, rows in parts)
        count = piece.shape[0] // total
        owners = [(owner, piece, owner * total) for owner in range(count)]
    else:
        owners = [
            (here ^ (2 * slot + across), column.at[slot], 0)
            for across, column in enumerate(pieces)
            for slot in range(column.shape[0])
        ]
    for owner, piece, start in owners:
        for flat, rows in parts:
            at = pl.ds(pl.multiple_of(owner * rows, 16), rows)
            flat[at, :] = piece[start : start + rows, :]
            start += rows


def untile(out, flat, base, columns):
    rows = out.shape[0]
    for tile in range(columns // LANES):
        out[:, tile * LANES : (tile + 1) * LANES] = flat[base : base + rows, :].astype(F32)
        base += rows
    return base


def gate_up_kernel(index, *refs, rows):
    pieces, (gate_out, up_out, flat) = refs[:-3], refs[-3:]
    flattened(index, pieces, [(flat, rows)])
    base = untile(gate_out, flat, 0, gate_out.shape[1])
    untile(up_out, flat, base, up_out.shape[1])


def outputs_kernel(index, *refs, rows, more_rows):
    down_out, out_out, query_out, key_out, value_out, gain_out, flat, small = refs[-8:]
    flattened(index, refs[:-8], [(flat, rows), (small, more_rows)])
    base = 0
    width, rows = down_out.shape
    whole = width // LANES * LANES
    for tile in range(whole // LANES):
        part = flat[base : base + rows, :].astype(F32)
        down_out[tile * LANES : (tile + 1) * LANES, :] = part.T
        base += rows
    half = rows // 2
    rest = flat[base : base + half, :].astype(F32).T
    down_out[whole:, :] = jnp.concatenate([rest[: width - whole], rest[width - whole :]], -1)
    base = untile(out_out, flat, base + half, whole)
    rows = out_out.shape[0]
    out_out[:, whole:] = flat[base : base + rows, : width - whole].astype(F32)
    base = untile(query_out, small, 0, whole)
    tile = small[base : base + rows, :].astype(F32)
    query_out[:, whole:] = tile[:, : width - whole]
    gain_out[...] = tile[:, width - whole : width - whole + 8].T
    base += rows
    both = [
        small[base + at * rows : base + (at + 1) * rows, :].astype(F32)
        for at in range(2 * KVW // LANES)
    ]
    both = jnp.concatenate(both, -1)
    key_out[...] = both[:, :KVW]
    value_out[...] = both[:, KVW:]


def swap(value, axis, bit):
    count = lax.axis_size(axis)
    return lax.ppermute(value, axis, [(i, i ^ (1 << bit)) for i in range(count)])


def gathered_ws(value):
    pair = jnp.stack([value, swap(value, "ws", 1)])
    return pair, swap(pair, "ws", 0)


def column_of(value):
    far = swap(value, "ctx", 2)
    near = swap(jnp.stack([value, far]), "ctx", 1)
    return jnp.stack([value, near[0], far, near[1]])


def shifted(value, by, upward_only):
    count = lax.axis_size("ctx")
    pairs = [(i, i + 2 * by) for i in range(count)]
    if upward_only:
        pairs = [(i, j) for i, j in pairs if j < count]
    return lax.ppermute(value, "ctx", [(i, j % count) for i, j in pairs])


def rms_scale(values, gain_vec):
    return values * lax.rsqrt(jnp.mean(values * values, -1, keepdims=True) + EPS) * gain_vec


def added(*values):
    total = values[0].astype(F32)
    for value in values[1:]:
        total = total + value.astype(F32)
    return total.astype(values[0].dtype)


def scattered_ctx(values, counts):
    count = lax.axis_size("ctx")
    value = jnp.concatenate(
        [v.reshape(count, rows, LANES) for v, rows in zip(values, counts)], 1
    ).reshape(-1, LANES)
    parts = lax.all_to_all(value, "ctx", split_axis=0, concat_axis=0, tiled=True)
    parts = parts.reshape(count, -1, LANES).astype(F32)
    return jnp.sum(parts, 0).astype(value.dtype)


def rope_tables(positions):
    frequency = jnp.exp(jnp.arange(HD // 2).astype(F32) * (-2.0 * math.log(THETA) / HD))
    angles = positions.astype(F32)[:, None] * frequency[None, :]
    return jnp.cos(angles), jnp.sin(angles)


def turned_heads(values, cosine, sine):
    heads = values.reshape(values.shape[0], -1, 2, HD // 2)
    cosine, sine = cosine[:, None], sine[:, None]
    first, second = heads[:, :, 0], heads[:, :, 1]
    pair = [first * cosine - second * sine, second * cosine + first * sine]
    return jnp.stack(pair, 2).reshape(values.shape)


def summed_column(terms):
    def slot(at):
        return added(*[term[at] for term in terms])

    got = swap(jnp.stack([slot(1), slot(3)]), "ctx", 1)
    far = swap(added(*[term[2] for term in terms], got[1]), "ctx", 2)
    return added(*[term[0] for term in terms], got[0], far)


def spread(index, terms):
    count = lax.axis_size("ctx")
    shape = shaped((count // 2, terms[0].shape[0] // count, LANES), BF16)
    return call(
        functools.partial(spread_kernel, count=count),
        (shape, shape),
        (index, *terms),
        micros=2,
        smem=1,
    )


def spread_both(index, mine, along, got):
    count = lax.axis_size("ctx")
    shape = shaped((count // 2, mine.shape[0] // count, LANES), BF16)
    return call(
        functools.partial(spread_both_kernel, count=count),
        (shape, shape, shaped((2,) + shape.shape, BF16)),
        (index, mine, along, got),
        micros=3,
        smem=1,
    )


def padded_rows(rows, count):
    return -(-rows // (16 * count)) * 16 * count


def body(
    tokens,
    attn_gain,
    query_weight,
    key_weight,
    value_weight,
    output_weight,
    ffn_gain,
    gate_weight,
    up_weight,
    down_weight,
    out_grad,
):
    seq_count, rows, width = tokens.shape
    ctx_count = lax.axis_size("ctx")
    owners = lax.axis_size("ws")
    slice_rows = query_weight.shape[0]
    ff = gate_weight.shape[1]
    wide = -(-width // LANES) * LANES
    by_hops = ctx_count == 8
    tokens = tokens.reshape(rows, width).T
    out_grad = out_grad.reshape(rows, width).T
    ctx_index = lax.axis_index("ctx")
    index = jnp.stack([ctx_index, lax.axis_index("ws")]).astype(jnp.int32)

    if by_hops:
        behind_two = shifted(tokens, 2, True)

    gains = jnp.concatenate([attn_gain, ffn_gain]).reshape(2, slice_rows)
    packed = jnp.concatenate(
        [
            jnp.concatenate([key_weight, value_weight, query_weight], -1),
            jnp.pad(gains, ((0, 14), (0, 2 * KVW + width - slice_rows))),
        ],
        0,
    )
    packs = gathered_ws(packed)
    in_weight = jnp.concatenate([gate_weight, up_weight, output_weight], -1)
    in_along = swap(in_weight, "ws", 1)
    down_along = swap(down_weight, "ws", 1)

    def wide_tables(positions):
        cosine, sine = rope_tables(positions)
        return jnp.concatenate([cosine] * 4, -1), jnp.concatenate([-sine, sine] * 2, -1)

    first_pos = ctx_index * rows
    cosine, sine = wide_tables(first_pos + jnp.arange(rows, dtype=jnp.int32))
    if by_hops:
        tables = wide_tables(jnp.arange(ctx_count * rows, dtype=jnp.int32))
        later_tokens, tables = lax.optimization_barrier((tokens, tables))
        behind_one = shifted(later_tokens, 1, True)
        mate = swap(later_tokens, "ctx", 0)
        last = [(i - 2, i) for i in range(ctx_count - 2, ctx_count)]
        behind_three = lax.ppermute(behind_two, "ctx", last)
    else:
        tables = (cosine, sine)

    places = (0, 1, 4) if by_hops else (0,)
    late_places = (2, 5, 3, 6, 7) if by_hops else ()
    early = (tokens, mate, behind_two) if by_hops else (tokens,)
    early_normed, early_kv, queries, full_query, full_kv, gains = call(
        functools.partial(early_kernel, places=places, slice_rows=slice_rows),
        (
            shaped((len(places), rows, width), BF16),
            shaped((len(places), rows, 2 * KVW), BF16),
            shaped((rows, width), BF16),
            shaped((width, width), BF16),
            shaped((width, 2 * KVW), BF16),
            shaped((8, width), F32),
        ),
        (index,) + packs + tables + early,
        scratch=(
            pltpu.VMEM((owners * 16, 2 * LANES), BF16),
            pltpu.VMEM((len(places), width, rows), BF16),
        ),
        micros=6,
        smem=1,
        vmem=60,
    )
    if by_hops:
        behind_three, queries = lax.optimization_barrier((behind_three, queries))
        late = (
            behind_one,
            swap(behind_two, "ctx", 0),
            swap(behind_one, "ctx", 0),
            behind_three,
            swap(behind_three, "ctx", 0),
        )
        normed_shape = (shaped((ctx_count * rows, width), BF16),)
        raw_scr = (pltpu.VMEM((len(late_places), width, rows), BF16),)
    else:
        tokens_all = lax.all_gather(tokens.T, "ctx", axis=0, tiled=True).astype(F32)
        normed_all = rms_scale(tokens_all, gains[0]).astype(BF16)
        linear = jnp.dot(normed_all, full_kv, preferred_element_type=F32)
        full_tables = rope_tables(jnp.arange(ctx_count * rows, dtype=jnp.int32))
        early_kv = jnp.concatenate(
            [turned_heads(linear[:, :KVW], *full_tables), linear[:, KVW:]], -1
        ).astype(BF16)
        late = ()
        normed_shape = ()
        raw_scr = ()

    late, in_weight, down_weight, in_along = lax.optimization_barrier(
        (late, in_weight, down_weight, in_along)
    )
    in_pieces = (in_weight, swap(in_weight, "ws", 0), in_along, swap(in_along, "ws", 0))
    down_core = swap(down_weight, "ws", 0)

    attended, lse, kv_all, *normed_out = call(
        functools.partial(forward_kernel, places=places, late_places=late_places),
        (
            shaped((rows, width), F32),
            shaped((8, GROUPS * rows), F32),
            shaped((ctx_count * rows, 2 * KVW), BF16),
            *normed_shape,
        ),
        (index, queries, early_normed, early_kv, full_kv, gains, *tables, *late),
        scratch=(
            *raw_scr,
            pltpu.VMEM((KV, GROUPS * rows, HD), BF16),
            pltpu.VMEM((KV, HD, GROUPS * rows), F32),
            pltpu.VMEM((KV, 8, GROUPS * rows), F32),
            pltpu.VMEM((KV, 8, GROUPS * rows), F32),
            pltpu.VMEM((2, rows, rows), F32),
        ),
        micros=20,
        smem=1,
        vmem=60,
    )

    attended, down_along = lax.optimization_barrier((attended, down_along))
    down_pieces = (down_weight, down_core, down_along, swap(down_along, "ws", 0))

    first_count = padded_rows(2 * slice_rows * ff // LANES, ctx_count)
    second_count = padded_rows(((ff // owners) * width + slice_rows * wide) // LANES, ctx_count)
    small_count = padded_rows(slice_rows * (wide + 2 * KVW) // LANES, ctx_count)
    first_rows, second_rows, small_rows = (
        rows_of // ctx_count for rows_of in (first_count, second_count, small_count)
    )

    def tile_shapes(rows_of):
        return (
            shaped((rows_of, LANES), BF16),
            shaped((rows_of, LANES), BF16),
            shaped((2, rows_of, LANES), BF16),
        )

    layer_out, middle_grad, attended_grad, ffn_gain_grad, *tiles = call(
        ffn_kernel,
        (
            shaped((width, rows), BF16),
            shaped((rows, width), F32),
            shaped((rows, width), BF16),
            shaped((8, width), F32),
            *tile_shapes(first_count),
            *tile_shapes(second_count),
        ),
        (index, tokens, attended, gains, out_grad) + in_pieces + down_pieces,
        scratch=(
            pltpu.VMEM((width, 2 * ff + width), BF16),
            pltpu.VMEM((ff, width), BF16),
            pltpu.VMEM((rows, width), F32),
            pltpu.VMEM((rows, width), F32),
            pltpu.VMEM((width, 2 * ff), BF16),
            pltpu.VMEM((ff, wide), BF16),
        ),
        micros=14,
        smem=1,
        vmem=60,
    )

    in_mine, in_along, in_send, mine, along, send = tiles
    got = swap(send, "ws", 0)
    in_got = swap(in_send, "ws", 0)
    in_crossing = added(in_along, in_got[1])
    if by_hops:
        keep_mine, keep_along, to_mate = spread_both(index, mine, along, got)
    else:
        to_mate = added(along, got[1])
    attended_grad, in_crossing, to_mate = lax.optimization_barrier(
        (attended_grad, in_crossing, to_mate)
    )
    in_crossed = swap(in_crossing, "ws", 1)
    from_mate = swap(to_mate, "ctx", 0) if by_hops else swap(to_mate, "ws", 1)

    tile_scr = pltpu.VMEM((width, wide + 2 * KVW), BF16)
    if by_hops:
        kv_shape = shaped((ctx_count, rows, 2 * KVW), BF16)
        backward_normed = normed_out[0]
        more_shapes = tile_shapes(small_count)
        more_scratch = (tile_scr, pltpu.VMEM((width, 2 * KVW), F32))
    else:
        kv_shape = shaped((ctx_count * rows, 2 * KVW), BF16)
        backward_normed = early_normed[0]
        more_shapes = (shaped((width, width), F32),)
        more_scratch = ()
    kv_grads, normed_grad, *small = call(
        backward_kernel,
        (kv_shape, shaped((rows, width), F32), *more_shapes),
        (
            index, queries, kv_all, attended, attended_grad, lse, backward_normed, full_query,
            full_kv, gains, ffn_gain_grad, *tables,
        ),
        scratch=(
            *more_scratch,
            pltpu.VMEM((KV, GROUPS * rows, HD), BF16),
            pltpu.VMEM((KV, GROUPS * rows, HD), BF16),
            pltpu.VMEM((KV, 8, GROUPS * rows), F32),
            pltpu.VMEM((KV, HD, GROUPS * rows), F32),
            pltpu.VMEM((rows, width), F32),
            pltpu.VMEM((2, rows, rows), F32),
        ),
        micros=23,
        smem=1,
        vmem=32 if by_hops else 60,
    )
    if not by_hops:
        linear = turned_heads(kv_grads[:, :KVW].astype(F32), full_tables[0], -full_tables[1])
        linear = jnp.concatenate([linear.astype(BF16), kv_grads[:, KVW:]], -1)
        kv_weight_grad = jnp.einsum("nd,nh->dh", normed_all, linear, preferred_element_type=F32)
        small = call(
            small_kernel,
            tile_shapes(small_count),
            (index, small[0], kv_weight_grad, full_query, full_kv, gains, ffn_gain_grad),
            scratch=(tile_scr,),
            smem=1,
        )
    kv_grads, small, in_crossed, from_mate = lax.optimization_barrier(
        (kv_grads, tuple(small), in_crossed, from_mate)
    )
    small_mine, small_along, small_send = small
    small_got = swap(small_send, "ws", 0)

    if by_hops:
        in_keep, in_to_mate = spread(index, (in_mine, in_got[0], in_crossed))
        in_from_mate = swap(in_to_mate, "ctx", 0)
        more_rows = keep_along.shape[0] * second_rows
        crossing = jnp.concatenate(
            [
                added(keep_along, from_mate[1]).reshape(more_rows, LANES),
                added(small_along, small_got[1]),
            ],
            0,
        )
        crossed = swap(crossing, "ws", 1)
        in_from_mate, crossed = lax.optimization_barrier((in_from_mate, crossed))
        small_keep, small_to_mate = spread(
            index, (small_mine, small_got[0], crossed[more_rows:])
        )
        crossed = crossed[:more_rows].reshape(keep_mine.shape)
        small_to_mate, kv_to_mate = lax.optimization_barrier(
            (small_to_mate, kv_grads[ctx_count // 2 :])
        )
        small_from_mate = swap(small_to_mate, "ctx", 0)
        kv_from_mate = swap(kv_to_mate, "ctx", 0)
        in_share = summed_column((in_keep, in_from_mate))
        share = summed_column(
            (
                jnp.concatenate([added(keep_mine, from_mate[0], crossed), small_keep], 1),
                jnp.concatenate([jnp.zeros_like(keep_mine), small_from_mate], 1),
            )
        )
        share, kv_from_mate = lax.optimization_barrier((share, kv_from_mate))
        in_column = column_of(in_share)
        in_pieces = (in_column, swap(in_column, "ctx", 0))
        column = column_of(share)
        pieces = (column, swap(column, "ctx", 0))
        kv_parts = (summed_column((kv_grads[: ctx_count // 2], kv_from_mate)),)
    else:
        kv_parts = (lax.all_to_all(kv_grads, "ctx", split_axis=0, concat_axis=0, tiled=True),)
        in_total = added(in_mine, in_got[0], in_crossed)
        total = added(mine, got[0], from_mate)
        small_crossed = swap(added(small_along, small_got[1]), "ws", 1)
        small_total = added(small_mine, small_got[0], small_crossed)
        in_share = scattered_ctx((in_total,), (first_rows,))
        share = scattered_ctx((total, small_total), (second_rows, small_rows))
        in_pieces, pieces = (
            (lax.all_gather(value, "ctx", axis=0, tiled=True),) for value in (in_share, share)
        )

    tokens_grad = call(
        tail_kernel,
        shaped((width, rows), BF16),
        (
            tokens, gains, normed_grad, middle_grad, full_kv, cosine, sine, *kv_parts,
        ),
        micros=4,
        vmem=16 if by_hops else 60,
    )

    gate_weight_grad, up_weight_grad = call(
        functools.partial(gate_up_kernel, rows=first_rows),
        (shaped(gate_weight.shape, F32), shaped(up_weight.shape, F32)),
        (index,) + in_pieces,
        scratch=(pltpu.VMEM((first_count, LANES), BF16),),
        micros=3,
        smem=1,
    )
    (
        down_weight_grad,
        output_weight_grad,
        query_weight_grad,
        key_weight_grad,
        value_weight_grad,
        gain_grads,
    ) = call(
        functools.partial(outputs_kernel, rows=second_rows, more_rows=small_rows),
        (
            shaped(down_weight.shape[::-1], F32),
            shaped(output_weight.shape, F32),
            shaped(query_weight.shape, F32),
            shaped(key_weight.shape, F32),
            shaped(value_weight.shape, F32),
            shaped((8, slice_rows), F32),
        ),
        (index,) + pieces,
        scratch=(pltpu.VMEM((second_count, LANES), BF16), pltpu.VMEM((small_count, LANES), BF16)),
        micros=3,
        smem=1,
    )
    return (
        layer_out.T.reshape(seq_count, rows, width),
        tokens_grad.T.reshape(seq_count, rows, width),
        gain_grads[0],
        query_weight_grad,
        key_weight_grad,
        value_weight_grad,
        output_weight_grad,
        gain_grads[1],
        gate_weight_grad,
        up_weight_grad,
        down_weight_grad.T,
    )


def solution(mesh):
    in_specs = (
        P("ws", "ctx", None),
        P("ws"),
        P("ws", None),
        P("ws", None),
        P("ws", None),
        P("ws", None),
        P("ws"),
        P("ws", None),
        P("ws", None),
        P("ws", None),
        P("ws", "ctx", None),
    )
    out_specs = (
        P("ws", "ctx", None),
        P("ws", "ctx", None),
        P("ws"),
        P("ws", None),
        P("ws", None),
        P("ws", None),
        P("ws", None),
        P("ws"),
        P("ws", None),
        P("ws", None),
        P("ws", None),
    )
    return jax.shard_map(body, mesh=mesh, in_specs=in_specs, out_specs=out_specs, check_vma=False)
```

```python
import functools
import math

import jax
import jax.numpy as jnp
from jax import lax
from jax.experimental import pallas as pl
from jax.experimental.pallas import tpu as pltpu
from jax.sharding import PartitionSpec as P

H = 9
KV = 3
HD = 64
GROUPS = H // KV
KVW = KV * HD

EPS = 1e-05
THETA = 100000.0
NEGATIVE = -1e30
LANES = 128
FF_STEP = 768
MIB = 1024 * 1024

BF16 = jnp.bfloat16
F32 = jnp.float32

SMEM_SPEC = pl.BlockSpec(memory_space=pltpu.SMEM)
VMEM_SPEC = pl.BlockSpec(memory_space=pltpu.VMEM)


def mm(left, right, left_dim=1, right_dim=0):
    return lax.dot_general(
        left, right, (((left_dim,), (right_dim,)), ((), ())), preferred_element_type=F32
    )


def call(kernel, outs, args, scratch=(), micros=1, smem=0, vmem=16):
    return pl.pallas_call(
        kernel,
        out_shape=outs,
        in_specs=[SMEM_SPEC] * smem + [VMEM_SPEC] * (len(args) - smem),
        out_specs=jax.tree.map(lambda _: VMEM_SPEC, outs),
        scratch_shapes=list(scratch),
        compiler_params=pltpu.CompilerParams(vmem_limit_bytes=vmem * MIB),
        cost_estimate=pl.CostEstimate(
            flops=micros * 1_000_000_000, bytes_accessed=0, transcendentals=0
        ),
    )(*args)


def shaped(shape, dtype):
    return jax.ShapeDtypeStruct(tuple(shape), dtype)


def swap_halves(part):
    lane = lax.broadcasted_iota(jnp.int32, part.shape, 1)
    return jnp.where(
        lane % HD < HD // 2,
        pltpu.roll(part, LANES - HD // 2, axis=1),
        pltpu.roll(part, HD // 2, axis=1),
    )


def rotated(values, cosine, signed_sine, sign):
    rows, width = values.shape
    parts = []
    for start in range(0, width, LANES):
        part = values[:, start : start + LANES]
        used = part.shape[1]
        if used < LANES:
            part = jnp.concatenate([part, jnp.zeros((rows, LANES - used), F32)], -1)
        turned = part * cosine + sign * (swap_halves(part) * signed_sine)
        parts.append(turned[:, :used])
    return jnp.concatenate(parts, -1)


def stacked_heads(ref, group):
    first = group * GROUPS
    return jnp.concatenate(
        [ref[:, (first + g) * HD : (first + g + 1) * HD] for g in range(GROUPS)], 0
    )


def assembled(full, pieces, me):
    rows = pieces[0].shape[0]
    for relative, piece in enumerate(pieces):
        start = pl.multiple_of((me ^ relative) * rows, 16)
        full[pl.ds(start, rows), :] = piece[...]


def projected(tokens, gain, weight, cosine, sine):
    values = tokens.astype(F32)
    scale = lax.rsqrt(jnp.mean(values * values, -1, keepdims=True) + EPS)
    normed = (values * scale * gain).astype(BF16)
    linear = mm(normed, weight)
    keys = rotated(linear[:, :KVW], cosine, sine, 1.0)
    return normed, jnp.concatenate([keys, linear[:, KVW:]], -1).astype(BF16)


def block_at(index, rows):
    return pl.ds(pl.multiple_of(index * rows, rows), rows)


def owner_of(place, here):
    return (here ^ (place % 2)) - 2 * (place // 2)


def table_at(table, owner, rows):
    if table.shape[0] == rows:
        return table[...]
    return table[block_at(jnp.clip(owner, 0, table.shape[0] // rows - 1), rows), :]


def early_kernel(index, here_pair, core_pair, cosine, sine, *refs, places, slice_rows):
    pieces = refs[: len(places)]
    (
        normed_out, kv_out, query_out, query_weight, kv_weight, gains_out, gain_scr, raw_scr,
    ) = refs[len(places) :]
    here = index[0]
    packs = (here_pair.at[0], core_pair.at[0], here_pair.at[1], core_pair.at[1])
    more = packs[0].shape[0] - slice_rows
    for relative, pack in enumerate(packs):
        owner = index[1] ^ relative
        at = pl.ds(pl.multiple_of(owner * slice_rows, 16), slice_rows)
        kv_weight[at, :] = pack[:slice_rows, : 2 * KVW]
        query_weight[at, :] = pack[:slice_rows, 2 * KVW :]
        gain_scr[pl.ds(pl.multiple_of(owner * more, 16), more), :] = pack[
            slice_rows:, : gain_scr.shape[1]
        ]
    gains = jnp.concatenate(
        [
            gain_scr[owner * more : owner * more + 8, :slice_rows].astype(F32)
            for owner in range(len(packs))
        ],
        -1,
    )
    gains_out[...] = gains
    rows = normed_out.shape[1]
    for slot, piece in enumerate(pieces):
        raw_scr[slot] = piece[...]

    def project(slot, carry):
        owner = owner_of(one_of(places, slot), here)
        tables = [table_at(table, owner, rows) for table in (cosine, sine)]
        normed, kv = projected(raw_scr[slot].T, gains_out[0:1, :], kv_weight[...], *tables)
        normed_out[slot] = normed
        kv_out[slot] = kv
        return carry

    lax.fori_loop(0, len(places), project, 0)
    tables = [table_at(table, here, rows) for table in (cosine, sine)]
    linear = mm(normed_out[0], query_weight[...])
    query_out[...] = (rotated(linear, *tables, 1.0) * (1.0 / math.sqrt(HD))).astype(BF16)


def project_kernel(index, kv_weight, gains, cosine, sine, *refs, places):
    pieces, (normed_out, kv_out) = refs[: len(places)], refs[len(places) :]
    for slot, (place, piece) in enumerate(zip(places, pieces)):
        owner = owner_of(place, index[0])
        tables = [table_at(table, owner, normed_out.shape[1]) for table in (cosine, sine)]
        normed_out[slot], kv_out[slot] = projected(
            piece[...].T, gains[0:1, :], kv_weight[...], *tables
        )


def fill_masks(masks):
    shape = masks.shape[1:]
    key_pos = lax.broadcasted_iota(jnp.int32, shape, 0)
    query_pos = lax.broadcasted_iota(jnp.int32, shape, 1)
    masks[0] = jnp.zeros(shape, F32)
    masks[1] = jnp.where(query_pos >= key_pos, 0.0, NEGATIVE)


def one_of(values, at):
    found = values[0]
    for place, value in enumerate(values[1:], 1):
        found = jnp.where(at == place, value, found)
    return found


def forward_kernel(
    index, queries, early_normed, early_kv, kv_weight, gains, cosine, sine, *refs,
    places, more_places, late_places,
):
    if more_places:
        more, refs = refs[:2], refs[2:]
    late, rest = refs[: len(late_places)], refs[len(late_places) :]
    attended, lse_out, kv_all, *rest = rest
    q_scr, acc_scr, max_scr, sum_scr, masks = rest[-5:]
    fill_masks(masks)
    rows = queries.shape[0]
    here = index[0]
    if late_places:
        normed_all, raw_scr = rest[:2]
        for slot, piece in enumerate(late):
            raw_scr[slot] = piece[...]

        def copies(places, normed, kv):
            def copy(slot, carry):
                owner = owner_of(one_of(places, slot), here)

                @pl.when((owner >= 0) & (owner <= here))
                def _():
                    normed_all[block_at(owner, rows), :] = normed[slot]
                    kv_all[block_at(owner, rows), :] = kv[slot]

                return carry

            lax.fori_loop(0, len(places), copy, 0)

        def project(slot, carry):
            owner = owner_of(one_of(late_places, slot), here)

            @pl.when((owner >= 0) & (owner <= here))
            def _():
                normed, kv = projected(
                    raw_scr[slot].T,
                    gains[0:1, :],
                    kv_weight[...],
                    table_at(cosine, owner, rows),
                    table_at(sine, owner, rows),
                )
                normed_all[block_at(owner, rows), :] = normed
                kv_all[block_at(owner, rows), :] = kv

            return carry

        copies(places, early_normed, early_kv)
        copies(more_places, *more)
        lax.fori_loop(0, len(late_places), project, 0)
    else:
        kv_all[...] = early_kv[...]

    for group in range(KV):
        q_scr[group] = stacked_heads(queries, group)
    acc_scr[...] = jnp.zeros_like(acc_scr)
    max_scr[...] = jnp.full_like(max_scr, NEGATIVE)
    sum_scr[...] = jnp.zeros_like(sum_scr)

    def step(j, carry):
        keys_at = block_at(j, rows)
        mask = jnp.concatenate([masks[jnp.where(j == here, 1, 0)]] * GROUPS, -1)
        for group in range(KV):
            keys = kv_all[keys_at, group * HD : (group + 1) * HD]
            values = kv_all[keys_at, KVW + group * HD : KVW + (group + 1) * HD]
            scores = mm(keys, q_scr[group], 1, 1) + mask
            old_max = max_scr[group, 0:1, :]
            new_max = jnp.maximum(old_max, jnp.max(scores, 0, keepdims=True))
            weights = jnp.exp(scores - new_max)
            factor = jnp.exp(old_max - new_max)
            max_scr[group, 0:1, :] = new_max
            sum_scr[group, 0:1, :] = sum_scr[group, 0:1, :] * factor + jnp.sum(
                weights, 0, keepdims=True
            )
            acc_scr[group] = acc_scr[group] * factor + mm(values, weights.astype(BF16), 0, 0)
        return carry

    lax.fori_loop(0, here + 1, step, 0)
    lse_out[...] = jnp.zeros_like(lse_out)
    for group in range(KV):
        total = sum_scr[group, 0:1, :]
        result = acc_scr[group] / total
        lse_out[group : group + 1, :] = max_scr[group, 0:1, :] + jnp.log(total)
        for g in range(GROUPS):
            head = group * GROUPS + g
            attended[:, head * HD : (head + 1) * HD] = result[:, g * rows : (g + 1) * rows].T


def rms_back(values, gain, grad):
    width = values.shape[-1]
    scale = lax.rsqrt(jnp.mean(values * values, -1, keepdims=True) + EPS)
    scaled = values * scale
    pulled = grad * gain
    along = jnp.sum(pulled * scaled, -1, keepdims=True) * (1.0 / width)
    return scale * (pulled - scaled * along), grad * scaled


def put_tiles(outs, me, grads, grad_lanes, first_row):
    rows = grads.shape[0] // len(outs)
    first, last = grad_lanes
    for relative, out in enumerate(outs):
        start = pl.multiple_of((me ^ relative) * rows, 16)
        for tile in range((last - first) // LANES):
            at = first + tile * LANES
            out[first_row + tile * rows : first_row + (tile + 1) * rows, :] = grads[
                pl.ds(start, rows), at : at + LANES
            ]


def ffn_kernel(
    index, tokens, attended, gains, out_grad,
    wi0, wi1, wi2, wi3, wd0, wd1, wd2, wd3,
    layer_out, middle_grad_out, attended_grad_out, gain_grad,
    in_mine, in_along, in_send, mine, along, send,
    in_weight, down_weight, result_scr, back_scr, tile_scr, down_scr, in_flat, flat,
    count,
):
    me = index[1]
    assembled(in_weight, (wi0, wi1, wi2, wi3), me)
    assembled(down_weight, (wd0, wd1, wd2, wd3), me)
    in_outs = [in_flat.at[relative] for relative in range(in_flat.shape[0])]
    outs = [flat.at[relative] for relative in range(flat.shape[0])]
    gain = gains[1:2, :]
    ff = down_weight.shape[0]
    out_weight = in_weight.at[:, 2 * ff :]
    owners = len(outs)
    in_rows = in_weight.shape[0] // owners
    down_rows = ff // owners
    attended_low = attended[...].astype(BF16)
    middle = tokens[...].T.astype(F32) + mm(attended_low, out_weight[...])
    scale = lax.rsqrt(jnp.mean(middle * middle, -1, keepdims=True) + EPS)
    normed = (middle * scale * gain).astype(BF16)
    grad_rows = out_grad[...].T
    result_scr[...] = middle
    back_scr[...] = jnp.zeros_like(back_scr)
    width = grad_rows.shape[1]

    def ff_step(step, carry):
        start = pl.multiple_of(step * FF_STEP, FF_STEP)
        gate_at = pl.ds(start, FF_STEP)
        up_at = pl.ds(pl.multiple_of(ff + start, FF_STEP), FF_STEP)
        gate = mm(normed, in_weight[:, gate_at])
        up = mm(normed, in_weight[:, up_at])
        gated = 1.0 / (1.0 + jnp.exp(-gate))
        silu = gate * gated
        hidden = (silu * up).astype(BF16)
        down = down_weight[gate_at, :]
        result_scr[...] += mm(hidden, down)
        hidden_grad = mm(grad_rows, down, 1, 1)
        gate_grad = (hidden_grad * up * (gated * (1.0 + gate * (1.0 - gated)))).astype(BF16)
        up_grad = (hidden_grad * silu).astype(BF16)
        back_scr[...] += mm(gate_grad, in_weight[:, gate_at], 1, 1) + mm(
            up_grad, in_weight[:, up_at], 1, 1
        )
        tile_scr[:, gate_at] = mm(normed, gate_grad, 0, 0).astype(BF16)
        tile_scr[:, up_at] = mm(normed, up_grad, 0, 0).astype(BF16)
        down_scr[gate_at, :width] = mm(hidden, grad_rows, 0, 0).astype(BF16)
        return carry

    lax.fori_loop(0, ff // FF_STEP, ff_step, 0)

    put_tiles(in_outs, me, tile_scr, (0, 2 * ff), 0)
    base = 2 * (ff // LANES) * in_rows
    for out in in_outs:
        if base < out.shape[0]:
            out[base:, :] = jnp.zeros((out.shape[0] - base, LANES), BF16)
    whole = width // LANES * LANES
    put_tiles(outs, me, down_scr, (0, whole), 0)
    base = whole // LANES * down_rows
    half = down_rows // 2
    for relative, out in enumerate(outs):
        start = pl.multiple_of((me ^ relative) * down_rows, 16)
        rest = jnp.concatenate(
            [
                down_scr[pl.ds(start, half), whole:width],
                down_scr[pl.ds(pl.multiple_of(start + half, 16), half), whole:width],
            ],
            -1,
        )
        out[base : base + half, :] = rest
    base += half

    layer_out[...] = result_scr[...].astype(BF16).T
    middle_back, gain_terms = rms_back(middle, gain, back_scr[...])
    gain_grad[...] = jnp.zeros_like(gain_grad)
    gain_grad[0:1, :] = jnp.sum(gain_terms, 0, keepdims=True)
    middle_grad = middle_back + grad_rows.astype(F32)
    middle_grad_out[...] = middle_grad
    branch = middle_grad.astype(BF16)
    attended_grad_out[...] = mm(branch, out_weight[...], 1, 1).astype(BF16)
    out_weight_grad = mm(attended_low, branch, 0, 0).astype(BF16)
    wide = -(-width // LANES) * LANES
    tile_scr[:, :wide] = jnp.concatenate(
        [out_weight_grad, jnp.zeros((width, wide - width), BF16)], -1
    )
    put_tiles(outs, me, tile_scr, (0, wide), base)
    base += wide // LANES * in_rows
    for out in outs:
        out[base:, :] = jnp.zeros((out.shape[0] - base, LANES), BF16)
    for parts, to in (
        (in_outs, (in_mine, in_send.at[0], in_along, in_send.at[1])),
        (outs, (mine, send.at[0], along, send.at[1])),
    ):
        for part, out in zip(parts, to):
            in_slots(index[0], part, out, count)


def in_slots(here, flat, out, count):
    rows = flat.shape[0] // count
    for apart in range(count):
        slot = (apart & 1) * (count // 2) + apart // 2
        start = pl.multiple_of((here ^ apart) * rows, 16)
        out[slot * rows : (slot + 1) * rows, :] = flat[pl.ds(start, rows), :]


def put_small(outs, me, tile_scr, query_grad, kv_grad, query_weight, kv_weight, gains, ffn_gain_grad):
    width = query_grad.shape[0]
    wide = -(-width // LANES) * LANES
    gain_columns = gains[...].T
    terms = jnp.sum(query_grad * query_weight.astype(F32), -1, keepdims=True) + jnp.sum(
        kv_grad * kv_weight.astype(F32), -1, keepdims=True
    )
    columns = jnp.concatenate(
        [
            terms / gain_columns[:, 0:1],
            ffn_gain_grad[...].T[:, 0:1],
            jnp.zeros((width, wide - width - 2), F32),
        ],
        -1,
    )
    tile_scr[:, :wide] = jnp.concatenate([query_grad, columns], -1).astype(BF16)
    tile_scr[:, wide : wide + 2 * KVW] = kv_grad.astype(BF16)
    put_tiles(outs, me, tile_scr, (0, wide + 2 * KVW), 0)


def backward_kernel(
    index, queries, kv_all, attended, attended_grad, lse, normed, query_weight, kv_weight, gains,
    ffn_gain_grad, cosine, sine,
    *refs,
):
    q_scr, g_scr, delta_scr, acc_scr, query_grad_scr, masks = refs[-6:]
    fill_masks(masks)
    rows = queries.shape[0]
    blocks = kv_all.shape[0] // rows
    here = index[0]
    whole = normed.shape[0] > rows
    if whole:
        kv_grads, normed_grad, mine, along, send, tile_scr, weight_scr = refs[:-6]
        weight_scr[...] = jnp.zeros_like(weight_scr)
        kv_grads[...] = jnp.zeros_like(kv_grads)
    else:
        kv_grads, normed_grad, query_weight_grad = refs[:-6]
    for group in range(KV):
        q_scr[group] = stacked_heads(queries, group)
        grads = stacked_heads(attended_grad, group)
        g_scr[group] = grads
        terms = (grads.astype(F32) * stacked_heads(attended, group)).T
        delta_scr[group, 0:1, :] = jnp.sum(terms, 0, keepdims=True)
    acc_scr[...] = jnp.zeros_like(acc_scr)

    def step(j, carry):
        keys_at = block_at(j, rows)
        mask = jnp.concatenate([masks[jnp.where(j == here, 1, 0)]] * GROUPS, -1)
        key_grads = []
        value_grads = []
        for group in range(KV):
            keys = kv_all[keys_at, group * HD : (group + 1) * HD]
            values = kv_all[keys_at, KVW + group * HD : KVW + (group + 1) * HD]
            group_q = q_scr[group]
            group_g = g_scr[group]
            scores = mm(keys, group_q, 1, 1) + mask
            prob = jnp.exp(scores - lse[group : group + 1, :])
            prob_grad = mm(values, group_g, 1, 1)
            score_grad = (prob * (prob_grad - delta_scr[group, 0:1, :])).astype(BF16)
            value_grads.append(mm(prob.astype(BF16), group_g))
            key_grads.append(mm(score_grad, group_q))
            acc_scr[group] += mm(keys, score_grad, 0, 0)
        key_grad = jnp.concatenate(key_grads, -1)
        value_grad = jnp.concatenate(value_grads, -1)
        both = jnp.concatenate([key_grad, value_grad], -1).astype(BF16)
        if whole:
            apart = j ^ here
            kv_grads[(apart & 1) * (blocks // 2) + apart // 2] = both
            turned = rotated(key_grad, cosine[keys_at, :], sine[keys_at, :], -1.0)
            linear = jnp.concatenate([turned, value_grad], -1).astype(BF16)
            weight_scr[...] += mm(normed[keys_at, :], linear, 0, 0)
        else:
            kv_grads[keys_at, :] = both
        return carry

    def clear(j, carry):
        kv_grads[block_at(j, rows), :] = jnp.zeros((rows, kv_grads.shape[1]), BF16)
        return carry

    lax.fori_loop(0, here + 1, step, 0)
    if not whole:
        lax.fori_loop(here + 1, blocks, clear, 0)
    for group in range(KV):
        for g in range(GROUPS):
            head = group * GROUPS + g
            part = acc_scr[group, :, g * rows : (g + 1) * rows]
            query_grad_scr[:, head * HD : (head + 1) * HD] = part.T
    tables = (table_at(cosine, here, rows), table_at(sine, here, rows))
    back = rotated(query_grad_scr[...], *tables, -1.0) * (1.0 / math.sqrt(HD))
    back = back.astype(BF16)
    own_normed = normed[block_at(here, rows), :] if whole else normed[...]
    query_grad = mm(own_normed, back, 0, 0)
    normed_grad[...] = mm(back, query_weight[...], 1, 1)
    if whole:
        outs = (mine, send.at[0], along, send.at[1])
        put_small(
            outs, index[1], tile_scr, query_grad, weight_scr[...], query_weight[...],
            kv_weight[...], gains, ffn_gain_grad,
        )
    else:
        query_weight_grad[...] = query_grad


def small_kernel(
    index, query_grad, kv_grad, query_weight, kv_weight, gains, ffn_gain_grad,
    mine, along, send, tile_scr,
):
    outs = (mine, send.at[0], along, send.at[1])
    for out in outs:
        out[...] = jnp.zeros(out.shape, BF16)
    put_small(
        outs, index[1], tile_scr, query_grad[...], kv_grad[...], query_weight[...], kv_weight[...],
        gains, ffn_gain_grad,
    )


def tail_kernel(
    tokens, gains, normed_grad, middle_grad, kv_weight, cosine, sine, *refs
):
    kv_parts, tokens_grad = refs[:-1], refs[-1]
    rows = normed_grad.shape[0]
    if kv_parts[0].shape[0] > rows:

        def add(j, total):
            return total + kv_parts[0][block_at(j, rows), :].astype(F32)

        parts = kv_parts[0].shape[0] // rows
        kv_grad = lax.fori_loop(0, parts, add, jnp.zeros((rows, 2 * KVW), F32))
    else:
        kv_grad = kv_parts[0][...].astype(F32)
    key_back = rotated(kv_grad[:, :KVW], cosine[...], sine[...], -1.0)
    back = jnp.concatenate([key_back, kv_grad[:, KVW:]], -1).astype(BF16)
    total = normed_grad[...] + mm(back, kv_weight[...], 1, 1)
    values = tokens[...].T.astype(F32)
    input_grad, _ = rms_back(values, gains[0:1, :], total)
    tokens_grad[...] = (middle_grad[...] + input_grad).astype(BF16).T


def spread_kernel(index, *refs, count):
    *terms, keep, send = refs
    here = index[0]
    rows = keep.shape[1]
    for apart in range(count):
        at = pl.ds(pl.multiple_of((here ^ apart) * rows, 16), rows)
        total = terms[0][at, :].astype(F32)
        for term in terms[1:]:
            total = total + term[at, :].astype(F32)
        (send if apart & 1 else keep)[apart // 2] = total.astype(BF16)


def flattened(index, pieces, parts):
    here = index[0]
    if len(pieces) == 1:
        (piece,) = pieces
        total = sum(rows for _, rows in parts)
        count = piece.shape[0] // total
        owners = [(owner, piece, owner * total) for owner in range(count)]
    else:
        owners = [
            (here ^ (2 * slot + across), column.at[slot], 0)
            for across, column in enumerate(pieces)
            for slot in range(column.shape[0])
        ]
    for owner, piece, start in owners:
        for flat, rows in parts:
            at = pl.ds(pl.multiple_of(owner * rows, 16), rows)
            flat[at, :] = piece[start : start + rows, :]
            start += rows


def untile(out, flat, base, columns):
    rows = out.shape[0]
    for tile in range(columns // LANES):
        out[:, tile * LANES : (tile + 1) * LANES] = flat[base : base + rows, :].astype(F32)
        base += rows
    return base


def gate_up_kernel(index, *refs, rows):
    pieces, (gate_out, up_out, flat) = refs[:-3], refs[-3:]
    flattened(index, pieces, [(flat, rows)])
    base = untile(gate_out, flat, 0, gate_out.shape[1])
    untile(up_out, flat, base, up_out.shape[1])


def outputs_kernel(index, *refs, rows, more_rows):
    down_out, out_out, query_out, key_out, value_out, gain_out, flat, small = refs[-8:]
    flattened(index, refs[:-8], [(flat, rows), (small, more_rows)])
    base = 0
    width, rows = down_out.shape
    whole = width // LANES * LANES
    for tile in range(whole // LANES):
        part = flat[base : base + rows, :].astype(F32)
        down_out[tile * LANES : (tile + 1) * LANES, :] = part.T
        base += rows
    half = rows // 2
    rest = flat[base : base + half, :].astype(F32).T
    down_out[whole:, :] = jnp.concatenate([rest[: width - whole], rest[width - whole :]], -1)
    base = untile(out_out, flat, base + half, whole)
    rows = out_out.shape[0]
    out_out[:, whole:] = flat[base : base + rows, : width - whole].astype(F32)
    base = untile(query_out, small, 0, whole)
    tile = small[base : base + rows, :].astype(F32)
    query_out[:, whole:] = tile[:, : width - whole]
    gain_out[...] = tile[:, width - whole : width - whole + 8].T
    base += rows
    both = [
        small[base + at * rows : base + (at + 1) * rows, :].astype(F32)
        for at in range(2 * KVW // LANES)
    ]
    both = jnp.concatenate(both, -1)
    key_out[...] = both[:, :KVW]
    value_out[...] = both[:, KVW:]


def swap(value, axis, bit):
    count = lax.axis_size(axis)
    return lax.ppermute(value, axis, [(i, i ^ (1 << bit)) for i in range(count)])


def gathered_ws(value):
    pair = jnp.stack([value, swap(value, "ws", 1)])
    return pair, swap(pair, "ws", 0)


def column_of(value):
    far = swap(value, "ctx", 2)
    near = swap(jnp.stack([value, far]), "ctx", 1)
    return jnp.stack([value, near[0], far, near[1]])


def shifted(value, by, upward_only):
    count = lax.axis_size("ctx")
    pairs = [(i, i + 2 * by) for i in range(count)]
    if upward_only:
        pairs = [(i, j) for i, j in pairs if j < count]
    return lax.ppermute(value, "ctx", [(i, j % count) for i, j in pairs])


def rms_scale(values, gain_vec):
    return values * lax.rsqrt(jnp.mean(values * values, -1, keepdims=True) + EPS) * gain_vec


def added(*values):
    total = values[0].astype(F32)
    for value in values[1:]:
        total = total + value.astype(F32)
    return total.astype(values[0].dtype)


def scattered_ctx(values, counts):
    count = lax.axis_size("ctx")
    value = jnp.concatenate(
        [v.reshape(count, rows, LANES) for v, rows in zip(values, counts)], 1
    ).reshape(-1, LANES)
    parts = lax.all_to_all(value, "ctx", split_axis=0, concat_axis=0, tiled=True)
    parts = parts.reshape(count, -1, LANES).astype(F32)
    return jnp.sum(parts, 0).astype(value.dtype)


def rope_tables(positions):
    frequency = jnp.exp(jnp.arange(HD // 2).astype(F32) * (-2.0 * math.log(THETA) / HD))
    angles = positions.astype(F32)[:, None] * frequency[None, :]
    return jnp.cos(angles), jnp.sin(angles)


def turned_heads(values, cosine, sine):
    heads = values.reshape(values.shape[0], -1, 2, HD // 2)
    cosine, sine = cosine[:, None], sine[:, None]
    first, second = heads[:, :, 0], heads[:, :, 1]
    pair = [first * cosine - second * sine, second * cosine + first * sine]
    return jnp.stack(pair, 2).reshape(values.shape)


def summed_column(terms):
    def slot(at):
        return added(*[term[at] for term in terms])

    got = swap(jnp.stack([slot(1), slot(3)]), "ctx", 1)
    far = swap(added(*[term[2] for term in terms], got[1]), "ctx", 2)
    return added(*[term[0] for term in terms], got[0], far)


def spread(index, terms):
    count = lax.axis_size("ctx")
    shape = shaped((count // 2, terms[0].shape[0] // count, LANES), BF16)
    return call(
        functools.partial(spread_kernel, count=count),
        (shape, shape),
        (index, *terms),
        micros=2,
        smem=1,
    )


def padded_rows(rows, count):
    return -(-rows // (16 * count)) * 16 * count


def body(
    tokens,
    attn_gain,
    query_weight,
    key_weight,
    value_weight,
    output_weight,
    ffn_gain,
    gate_weight,
    up_weight,
    down_weight,
    out_grad,
):
    seq_count, rows, width = tokens.shape
    ctx_count = lax.axis_size("ctx")
    owners = lax.axis_size("ws")
    slice_rows = query_weight.shape[0]
    ff = gate_weight.shape[1]
    wide = -(-width // LANES) * LANES
    by_hops = ctx_count == 8
    tokens = tokens.reshape(rows, width).T
    out_grad = out_grad.reshape(rows, width).T
    ctx_index = lax.axis_index("ctx")
    index = jnp.stack([ctx_index, lax.axis_index("ws")]).astype(jnp.int32)

    if by_hops:
        behind_two = shifted(tokens, 2, True)

    gains = jnp.concatenate([attn_gain, ffn_gain]).reshape(2, slice_rows)
    packed = jnp.concatenate(
        [
            jnp.concatenate([key_weight, value_weight, query_weight], -1),
            jnp.pad(gains, ((0, 14), (0, 2 * KVW + width - slice_rows))),
        ],
        0,
    )
    packs = gathered_ws(packed)
    in_weight = jnp.concatenate([gate_weight, up_weight, output_weight], -1)
    in_along = swap(in_weight, "ws", 1)
    down_along = swap(down_weight, "ws", 1)

    def wide_tables(positions):
        cosine, sine = rope_tables(positions)
        return jnp.concatenate([cosine] * 4, -1), jnp.concatenate([-sine, sine] * 2, -1)

    first_pos = ctx_index * rows
    cosine, sine = wide_tables(first_pos + jnp.arange(rows, dtype=jnp.int32))
    if by_hops:
        tables = wide_tables(jnp.arange(ctx_count * rows, dtype=jnp.int32))
        later_tokens, tables = lax.optimization_barrier((tokens, tables))
        behind_one = shifted(later_tokens, 1, True)
        mate = swap(later_tokens, "ctx", 0)
        last = [(i - 2, i) for i in range(ctx_count - 2, ctx_count)]
        behind_three = lax.ppermute(behind_two, "ctx", last)
    else:
        tables = (cosine, sine)

    places = (0, 1, 4) if by_hops else (0,)
    more_places = (2, 5) if by_hops else ()
    late_places = (3, 6, 7) if by_hops else ()
    early = (tokens, mate, behind_two) if by_hops else (tokens,)
    early_normed, early_kv, queries, full_query, full_kv, gains = call(
        functools.partial(early_kernel, places=places, slice_rows=slice_rows),
        (
            shaped((len(places), rows, width), BF16),
            shaped((len(places), rows, 2 * KVW), BF16),
            shaped((rows, width), BF16),
            shaped((width, width), BF16),
            shaped((width, 2 * KVW), BF16),
            shaped((8, width), F32),
        ),
        (index,) + packs + tables + early,
        scratch=(
            pltpu.VMEM((owners * 16, 2 * LANES), BF16),
            pltpu.VMEM((len(places), width, rows), BF16),
        ),
        micros=6,
        smem=1,
        vmem=60,
    )
    if by_hops:
        behind_three, queries = lax.optimization_barrier((behind_three, queries))
        more = call(
            functools.partial(project_kernel, places=more_places),
            (
                shaped((len(more_places), rows, width), BF16),
                shaped((len(more_places), rows, 2 * KVW), BF16),
            ),
            (index, full_kv, gains, *tables, behind_one, swap(behind_two, "ctx", 0)),
            micros=3,
            smem=1,
            vmem=60,
        )
        late = (swap(behind_one, "ctx", 0), behind_three, swap(behind_three, "ctx", 0))
        normed_shape = (shaped((ctx_count * rows, width), BF16),)
        raw_scr = (pltpu.VMEM((len(late_places), width, rows), BF16),)
    else:
        tokens_all = lax.all_gather(tokens.T, "ctx", axis=0, tiled=True).astype(F32)
        normed_all = rms_scale(tokens_all, gains[0]).astype(BF16)
        linear = jnp.dot(normed_all, full_kv, preferred_element_type=F32)
        full_tables = rope_tables(jnp.arange(ctx_count * rows, dtype=jnp.int32))
        early_kv = jnp.concatenate(
            [turned_heads(linear[:, :KVW], *full_tables), linear[:, KVW:]], -1
        ).astype(BF16)
        more = ()
        late = ()
        normed_shape = ()
        raw_scr = ()

    late, in_weight, down_weight, in_along = lax.optimization_barrier(
        (late, in_weight, down_weight, in_along)
    )
    in_pieces = (in_weight, swap(in_weight, "ws", 0), in_along, swap(in_along, "ws", 0))
    down_core = swap(down_weight, "ws", 0)

    attended, lse, kv_all, *normed_out = call(
        functools.partial(
            forward_kernel, places=places, more_places=more_places, late_places=late_places
        ),
        (
            shaped((rows, width), F32),
            shaped((8, GROUPS * rows), F32),
            shaped((ctx_count * rows, 2 * KVW), BF16),
            *normed_shape,
        ),
        (index, queries, early_normed, early_kv, full_kv, gains, *tables, *more, *late),
        scratch=(
            *raw_scr,
            pltpu.VMEM((KV, GROUPS * rows, HD), BF16),
            pltpu.VMEM((KV, HD, GROUPS * rows), F32),
            pltpu.VMEM((KV, 8, GROUPS * rows), F32),
            pltpu.VMEM((KV, 8, GROUPS * rows), F32),
            pltpu.VMEM((2, rows, rows), F32),
        ),
        micros=20,
        smem=1,
        vmem=60,
    )

    attended, down_along = lax.optimization_barrier((attended, down_along))
    down_pieces = (down_weight, down_core, down_along, swap(down_along, "ws", 0))

    first_count = padded_rows(2 * slice_rows * ff // LANES, ctx_count)
    second_count = padded_rows(((ff // owners) * width + slice_rows * wide) // LANES, ctx_count)
    small_count = padded_rows(slice_rows * (wide + 2 * KVW) // LANES, ctx_count)
    first_rows, second_rows, small_rows = (
        rows_of // ctx_count for rows_of in (first_count, second_count, small_count)
    )

    def tile_shapes(rows_of):
        return (
            shaped((rows_of, LANES), BF16),
            shaped((rows_of, LANES), BF16),
            shaped((2, rows_of, LANES), BF16),
        )

    layer_out, middle_grad, attended_grad, ffn_gain_grad, *tiles = call(
        functools.partial(ffn_kernel, count=ctx_count if by_hops else 1),
        (
            shaped((width, rows), BF16),
            shaped((rows, width), F32),
            shaped((rows, width), BF16),
            shaped((8, width), F32),
            *tile_shapes(first_count),
            *tile_shapes(second_count),
        ),
        (index, tokens, attended, gains, out_grad) + in_pieces + down_pieces,
        scratch=(
            pltpu.VMEM((width, 2 * ff + width), BF16),
            pltpu.VMEM((ff, width), BF16),
            pltpu.VMEM((rows, width), F32),
            pltpu.VMEM((rows, width), F32),
            pltpu.VMEM((width, 2 * ff), BF16),
            pltpu.VMEM((ff, wide), BF16),
            pltpu.VMEM((owners, first_count, LANES), BF16),
            pltpu.VMEM((owners, second_count, LANES), BF16),
        ),
        micros=14,
        smem=1,
        vmem=60,
    )

    in_mine, in_along, in_send, mine, along, send = tiles
    got = swap(send, "ws", 0)
    in_got = swap(in_send, "ws", 0)
    in_crossing = added(in_along, in_got[1])
    if by_hops:
        half = second_count // 2

        def halves(value):
            return value[:half].reshape(ctx_count // 2, second_rows, LANES), value[half:]

        keep_mine, mine_to_mate = halves(added(mine, got[0]))
        keep_along, along_to_mate = halves(added(along, got[1]))
        to_mate = jnp.stack([mine_to_mate, along_to_mate])
        to_mate = to_mate.reshape(2, ctx_count // 2, second_rows, LANES)
    else:
        to_mate = added(along, got[1])
    attended_grad, in_crossing, to_mate = lax.optimization_barrier(
        (attended_grad, in_crossing, to_mate)
    )
    in_crossed = swap(in_crossing, "ws", 1)
    from_mate = swap(to_mate, "ctx", 0) if by_hops else swap(to_mate, "ws", 1)

    tile_scr = pltpu.VMEM((width, wide + 2 * KVW), BF16)
    if by_hops:
        kv_shape = shaped((ctx_count, rows, 2 * KVW), BF16)
        backward_normed = normed_out[0]
        more_shapes = tile_shapes(small_count)
        more_scratch = (tile_scr, pltpu.VMEM((width, 2 * KVW), F32))
    else:
        kv_shape = shaped((ctx_count * rows, 2 * KVW), BF16)
        backward_normed = early_normed[0]
        more_shapes = (shaped((width, width), F32),)
        more_scratch = ()
    kv_grads, normed_grad, *small = call(
        backward_kernel,
        (kv_shape, shaped((rows, width), F32), *more_shapes),
        (
            index, queries, kv_all, attended, attended_grad, lse, backward_normed, full_query,
            full_kv, gains, ffn_gain_grad, *tables,
        ),
        scratch=(
            *more_scratch,
            pltpu.VMEM((KV, GROUPS * rows, HD), BF16),
            pltpu.VMEM((KV, GROUPS * rows, HD), BF16),
            pltpu.VMEM((KV, 8, GROUPS * rows), F32),
            pltpu.VMEM((KV, HD, GROUPS * rows), F32),
            pltpu.VMEM((rows, width), F32),
            pltpu.VMEM((2, rows, rows), F32),
        ),
        micros=23,
        smem=1,
        vmem=32 if by_hops else 60,
    )
    if not by_hops:
        linear = turned_heads(kv_grads[:, :KVW].astype(F32), full_tables[0], -full_tables[1])
        linear = jnp.concatenate([linear.astype(BF16), kv_grads[:, KVW:]], -1)
        kv_weight_grad = jnp.einsum("nd,nh->dh", normed_all, linear, preferred_element_type=F32)
        small = call(
            small_kernel,
            tile_shapes(small_count),
            (index, small[0], kv_weight_grad, full_query, full_kv, gains, ffn_gain_grad),
            scratch=(tile_scr,),
            smem=1,
        )
    kv_grads, small, in_crossed, from_mate = lax.optimization_barrier(
        (kv_grads, tuple(small), in_crossed, from_mate)
    )
    small_mine, small_along, small_send = small
    small_got = swap(small_send, "ws", 0)

    if by_hops:
        in_keep, in_to_mate = (
            added(in_mine[at], in_got[0, at], in_crossed[at]).reshape(-1, first_rows, LANES)
            for at in (slice(first_count // 2), slice(first_count // 2, None))
        )
        in_from_mate = swap(in_to_mate, "ctx", 0)
        more_rows = keep_along.shape[0] * second_rows
        crossing = jnp.concatenate(
            [
                added(keep_along, from_mate[1]).reshape(more_rows, LANES),
                added(small_along, small_got[1]),
            ],
            0,
        )
        crossed = swap(crossing, "ws", 1)
        in_from_mate, crossed = lax.optimization_barrier((in_from_mate, crossed))
        small_keep, small_to_mate = spread(
            index, (small_mine, small_got[0], crossed[more_rows:])
        )
        crossed = crossed[:more_rows].reshape(keep_mine.shape)
        small_to_mate, kv_to_mate = lax.optimization_barrier(
            (small_to_mate, kv_grads[ctx_count // 2 :])
        )
        small_from_mate = swap(small_to_mate, "ctx", 0)
        kv_from_mate = swap(kv_to_mate, "ctx", 0)
        in_share = summed_column((in_keep, in_from_mate))
        share = summed_column(
            (
                jnp.concatenate([added(keep_mine, from_mate[0], crossed), small_keep], 1),
                jnp.concatenate([jnp.zeros_like(keep_mine), small_from_mate], 1),
            )
        )
        share, kv_from_mate = lax.optimization_barrier((share, kv_from_mate))
        in_column = column_of(in_share)
        in_pieces = (in_column, swap(in_column, "ctx", 0))
        column = column_of(share)
        pieces = (column, swap(column, "ctx", 0))
        kv_parts = (summed_column((kv_grads[: ctx_count // 2], kv_from_mate)),)
    else:
        kv_parts = (lax.all_to_all(kv_grads, "ctx", split_axis=0, concat_axis=0, tiled=True),)
        in_total = added(in_mine, in_got[0], in_crossed)
        total = added(mine, got[0], from_mate)
        small_crossed = swap(added(small_along, small_got[1]), "ws", 1)
        small_total = added(small_mine, small_got[0], small_crossed)
        in_share = scattered_ctx((in_total,), (first_rows,))
        share = scattered_ctx((total, small_total), (second_rows, small_rows))
        in_pieces, pieces = (
            (lax.all_gather(value, "ctx", axis=0, tiled=True),) for value in (in_share, share)
        )

    tokens_grad = call(
        tail_kernel,
        shaped((width, rows), BF16),
        (
            tokens, gains, normed_grad, middle_grad, full_kv, cosine, sine, *kv_parts,
        ),
        micros=4,
        vmem=16 if by_hops else 60,
    )

    gate_weight_grad, up_weight_grad = call(
        functools.partial(gate_up_kernel, rows=first_rows),
        (shaped(gate_weight.shape, F32), shaped(up_weight.shape, F32)),
        (index,) + in_pieces,
        scratch=(pltpu.VMEM((first_count, LANES), BF16),),
        micros=3,
        smem=1,
    )
    (
        down_weight_grad,
        output_weight_grad,
        query_weight_grad,
        key_weight_grad,
        value_weight_grad,
        gain_grads,
    ) = call(
        functools.partial(outputs_kernel, rows=second_rows, more_rows=small_rows),
        (
            shaped(down_weight.shape[::-1], F32),
            shaped(output_weight.shape, F32),
            shaped(query_weight.shape, F32),
            shaped(key_weight.shape, F32),
            shaped(value_weight.shape, F32),
            shaped((8, slice_rows), F32),
        ),
        (index,) + pieces,
        scratch=(pltpu.VMEM((second_count, LANES), BF16), pltpu.VMEM((small_count, LANES), BF16)),
        micros=3,
        smem=1,
    )
    return (
        layer_out.T.reshape(seq_count, rows, width),
        tokens_grad.T.reshape(seq_count, rows, width),
        gain_grads[0],
        query_weight_grad,
        key_weight_grad,
        value_weight_grad,
        output_weight_grad,
        gain_grads[1],
        gate_weight_grad,
        up_weight_grad,
        down_weight_grad.T,
    )


def solution(mesh):
    in_specs = (
        P("ws", "ctx", None),
        P("ws"),
        P("ws", None),
        P("ws", None),
        P("ws", None),
        P("ws", None),
        P("ws"),
        P("ws", None),
        P("ws", None),
        P("ws", None),
        P("ws", "ctx", None),
    )
    out_specs = (
        P("ws", "ctx", None),
        P("ws", "ctx", None),
        P("ws"),
        P("ws", None),
        P("ws", None),
        P("ws", None),
        P("ws", None),
        P("ws"),
        P("ws", None),
        P("ws", None),
        P("ws", None),
    )
    return jax.shard_map(body, mesh=mesh, in_specs=in_specs, out_specs=out_specs, check_vma=False)
```

```python
import functools
import math

import jax
import jax.numpy as jnp
from jax import lax
from jax.experimental import pallas as pl
from jax.experimental.pallas import tpu as pltpu
from jax.sharding import PartitionSpec as P

H = 9
KV = 3
HD = 64
GROUPS = H // KV
KVW = KV * HD

EPS = 1e-05
THETA = 100000.0
NEGATIVE = -1e30
LANES = 128
FF_STEP = 768
MIB = 1024 * 1024

BF16 = jnp.bfloat16
F32 = jnp.float32

SMEM_SPEC = pl.BlockSpec(memory_space=pltpu.SMEM)
VMEM_SPEC = pl.BlockSpec(memory_space=pltpu.VMEM)


def mm(left, right, left_dim=1, right_dim=0):
    return lax.dot_general(
        left, right, (((left_dim,), (right_dim,)), ((), ())), preferred_element_type=F32
    )


def call(kernel, outs, args, scratch=(), micros=1, smem=0, vmem=16):
    return pl.pallas_call(
        kernel,
        out_shape=outs,
        in_specs=[SMEM_SPEC] * smem + [VMEM_SPEC] * (len(args) - smem),
        out_specs=jax.tree.map(lambda _: VMEM_SPEC, outs),
        scratch_shapes=list(scratch),
        compiler_params=pltpu.CompilerParams(vmem_limit_bytes=vmem * MIB),
        cost_estimate=pl.CostEstimate(
            flops=micros * 1_000_000_000, bytes_accessed=0, transcendentals=0
        ),
    )(*args)


def shaped(shape, dtype):
    return jax.ShapeDtypeStruct(tuple(shape), dtype)


def swap_halves(part):
    lane = lax.broadcasted_iota(jnp.int32, part.shape, 1)
    return jnp.where(
        lane % HD < HD // 2,
        pltpu.roll(part, LANES - HD // 2, axis=1),
        pltpu.roll(part, HD // 2, axis=1),
    )


def rotated(values, cosine, signed_sine, sign):
    rows, width = values.shape
    parts = []
    for start in range(0, width, LANES):
        part = values[:, start : start + LANES]
        used = part.shape[1]
        if used < LANES:
            part = jnp.concatenate([part, jnp.zeros((rows, LANES - used), F32)], -1)
        turned = part * cosine + sign * (swap_halves(part) * signed_sine)
        parts.append(turned[:, :used])
    return jnp.concatenate(parts, -1)


def stacked_heads(ref, group):
    first = group * GROUPS
    return jnp.concatenate(
        [ref[:, (first + g) * HD : (first + g + 1) * HD] for g in range(GROUPS)], 0
    )


def assembled(full, pieces, me):
    rows = pieces[0].shape[0]
    for relative, piece in enumerate(pieces):
        start = pl.multiple_of((me ^ relative) * rows, 16)
        full[pl.ds(start, rows), :] = piece[...]


def projected(tokens, gain, weight, cosine, sine):
    values = tokens.astype(F32)
    scale = lax.rsqrt(jnp.mean(values * values, -1, keepdims=True) + EPS)
    normed = (values * scale * gain).astype(BF16)
    linear = mm(normed, weight)
    keys = rotated(linear[:, :KVW], cosine, sine, 1.0)
    return normed, jnp.concatenate([keys, linear[:, KVW:]], -1).astype(BF16)


def block_at(index, rows):
    return pl.ds(pl.multiple_of(index * rows, rows), rows)


def owner_of(place, here):
    return (here ^ (place % 2)) - 2 * (place // 2)


def table_at(table, owner, rows):
    if table.shape[0] == rows:
        return table[...]
    return table[block_at(jnp.clip(owner, 0, table.shape[0] // rows - 1), rows), :]


def early_kernel(index, here_pair, core_pair, cosine, sine, *refs, places, slice_rows):
    pieces = refs[: len(places)]
    (
        normed_out, kv_out, query_out, query_weight, kv_weight, gains_out, gain_scr, raw_scr,
    ) = refs[len(places) :]
    here = index[0]
    packs = (here_pair.at[0], core_pair.at[0], here_pair.at[1], core_pair.at[1])
    more = packs[0].shape[0] - slice_rows
    for relative, pack in enumerate(packs):
        owner = index[1] ^ relative
        at = pl.ds(pl.multiple_of(owner * slice_rows, 16), slice_rows)
        kv_weight[at, :] = pack[:slice_rows, : 2 * KVW]
        query_weight[at, :] = pack[:slice_rows, 2 * KVW :]
        gain_scr[pl.ds(pl.multiple_of(owner * more, 16), more), :] = pack[
            slice_rows:, : gain_scr.shape[1]
        ]
    gains = jnp.concatenate(
        [
            gain_scr[owner * more : owner * more + 8, :slice_rows].astype(F32)
            for owner in range(len(packs))
        ],
        -1,
    )
    gains_out[...] = gains
    rows = normed_out.shape[1]
    for slot, piece in enumerate(pieces):
        raw_scr[slot] = piece[...]

    def project(slot, carry):
        owner = owner_of(one_of(places, slot), here)
        tables = [table_at(table, owner, rows) for table in (cosine, sine)]
        normed, kv = projected(raw_scr[slot].T, gains_out[0:1, :], kv_weight[...], *tables)
        normed_out[slot] = normed
        kv_out[slot] = kv
        return carry

    lax.fori_loop(0, len(places), project, 0)
    tables = [table_at(table, here, rows) for table in (cosine, sine)]
    linear = mm(normed_out[0], query_weight[...])
    query_out[...] = (rotated(linear, *tables, 1.0) * (1.0 / math.sqrt(HD))).astype(BF16)


def project_kernel(index, kv_weight, gains, cosine, sine, *refs, places):
    pieces, (normed_out, kv_out) = refs[: len(places)], refs[len(places) :]
    for slot, (place, piece) in enumerate(zip(places, pieces)):
        owner = owner_of(place, index[0])
        tables = [table_at(table, owner, normed_out.shape[1]) for table in (cosine, sine)]
        normed_out[slot], kv_out[slot] = projected(
            piece[...].T, gains[0:1, :], kv_weight[...], *tables
        )


def fill_masks(masks):
    shape = masks.shape[1:]
    key_pos = lax.broadcasted_iota(jnp.int32, shape, 0)
    query_pos = lax.broadcasted_iota(jnp.int32, shape, 1)
    masks[0] = jnp.zeros(shape, F32)
    masks[1] = jnp.where(query_pos >= key_pos, 0.0, NEGATIVE)


def one_of(values, at):
    found = values[0]
    for place, value in enumerate(values[1:], 1):
        found = jnp.where(at == place, value, found)
    return found


def forward_kernel(
    index, queries, early_normed, early_kv, kv_weight, gains, cosine, sine, *refs,
    places, more_places, late_places,
):
    if more_places:
        more, refs = refs[:2], refs[2:]
    late, rest = refs[: len(late_places)], refs[len(late_places) :]
    attended, lse_out, kv_all, *rest = rest
    q_scr, acc_scr, max_scr, sum_scr, masks = rest[-5:]
    fill_masks(masks)
    rows = queries.shape[0]
    here = index[0]
    if late_places:
        normed_all, raw_scr = rest[:2]
        for slot, piece in enumerate(late):
            raw_scr[slot] = piece[...]

        def copies(places, normed, kv):
            def copy(slot, carry):
                owner = owner_of(one_of(places, slot), here)

                @pl.when((owner >= 0) & (owner <= here))
                def _():
                    normed_all[block_at(owner, rows), :] = normed[slot]
                    kv_all[block_at(owner, rows), :] = kv[slot]

                return carry

            lax.fori_loop(0, len(places), copy, 0)

        def project(slot, carry):
            owner = owner_of(one_of(late_places, slot), here)

            @pl.when((owner >= 0) & (owner <= here))
            def _():
                normed, kv = projected(
                    raw_scr[slot].T,
                    gains[0:1, :],
                    kv_weight[...],
                    table_at(cosine, owner, rows),
                    table_at(sine, owner, rows),
                )
                normed_all[block_at(owner, rows), :] = normed
                kv_all[block_at(owner, rows), :] = kv

            return carry

        copies(places, early_normed, early_kv)
        copies(more_places, *more)
        lax.fori_loop(0, len(late_places), project, 0)
    else:
        kv_all[...] = early_kv[...]

    for group in range(KV):
        q_scr[group] = stacked_heads(queries, group)
    acc_scr[...] = jnp.zeros_like(acc_scr)
    max_scr[...] = jnp.full_like(max_scr, NEGATIVE)
    sum_scr[...] = jnp.zeros_like(sum_scr)

    def step(j, carry):
        keys_at = block_at(j, rows)
        mask = jnp.concatenate([masks[jnp.where(j == here, 1, 0)]] * GROUPS, -1)
        for group in range(KV):
            keys = kv_all[keys_at, group * HD : (group + 1) * HD]
            values = kv_all[keys_at, KVW + group * HD : KVW + (group + 1) * HD]
            scores = mm(keys, q_scr[group], 1, 1) + mask
            old_max = max_scr[group, 0:1, :]
            new_max = jnp.maximum(old_max, jnp.max(scores, 0, keepdims=True))
            weights = jnp.exp(scores - new_max)
            factor = jnp.exp(old_max - new_max)
            max_scr[group, 0:1, :] = new_max
            sum_scr[group, 0:1, :] = sum_scr[group, 0:1, :] * factor + jnp.sum(
                weights, 0, keepdims=True
            )
            acc_scr[group] = acc_scr[group] * factor + mm(values, weights.astype(BF16), 0, 0)
        return carry

    lax.fori_loop(0, here + 1, step, 0)
    lse_out[...] = jnp.zeros_like(lse_out)
    for group in range(KV):
        total = sum_scr[group, 0:1, :]
        result = acc_scr[group] / total
        lse_out[group : group + 1, :] = max_scr[group, 0:1, :] + jnp.log(total)
        for g in range(GROUPS):
            head = group * GROUPS + g
            attended[:, head * HD : (head + 1) * HD] = result[:, g * rows : (g + 1) * rows].T


def rms_back(values, gain, grad):
    width = values.shape[-1]
    scale = lax.rsqrt(jnp.mean(values * values, -1, keepdims=True) + EPS)
    scaled = values * scale
    pulled = grad * gain
    along = jnp.sum(pulled * scaled, -1, keepdims=True) * (1.0 / width)
    return scale * (pulled - scaled * along), grad * scaled


def put_tiles(outs, me, grads, grad_lanes, first_row):
    rows = grads.shape[0] // len(outs)
    first, last = grad_lanes
    for relative, out in enumerate(outs):
        start = pl.multiple_of((me ^ relative) * rows, 16)
        for tile in range((last - first) // LANES):
            at = first + tile * LANES
            out[first_row + tile * rows : first_row + (tile + 1) * rows, :] = grads[
                pl.ds(start, rows), at : at + LANES
            ]


def ffn_kernel(
    index, tokens, attended, gains, out_grad,
    wi0, wi1, wi2, wi3, wd0, wd1, wd2, wd3,
    layer_out, middle_grad_out, attended_grad_out, gain_grad,
    in_mine, in_along, in_send, mine, along, send,
    in_weight, down_weight, result_scr, back_scr, tile_scr, down_scr, in_flat, flat,
    count,
):
    me = index[1]
    assembled(in_weight, (wi0, wi1, wi2, wi3), me)
    assembled(down_weight, (wd0, wd1, wd2, wd3), me)
    in_outs = [in_flat.at[relative] for relative in range(in_flat.shape[0])]
    outs = [flat.at[relative] for relative in range(flat.shape[0])]
    gain = gains[1:2, :]
    ff = down_weight.shape[0]
    out_weight = in_weight.at[:, 2 * ff :]
    owners = len(outs)
    in_rows = in_weight.shape[0] // owners
    down_rows = ff // owners
    attended_low = attended[...].astype(BF16)
    middle = tokens[...].T.astype(F32) + mm(attended_low, out_weight[...])
    scale = lax.rsqrt(jnp.mean(middle * middle, -1, keepdims=True) + EPS)
    normed = (middle * scale * gain).astype(BF16)
    grad_rows = out_grad[...].T
    result_scr[...] = middle
    back_scr[...] = jnp.zeros_like(back_scr)
    width = grad_rows.shape[1]

    def ff_step(step, carry):
        start = pl.multiple_of(step * FF_STEP, FF_STEP)
        gate_at = pl.ds(start, FF_STEP)
        up_at = pl.ds(pl.multiple_of(ff + start, FF_STEP), FF_STEP)
        gate = mm(normed, in_weight[:, gate_at])
        up = mm(normed, in_weight[:, up_at])
        gated = 1.0 / (1.0 + jnp.exp(-gate))
        silu = gate * gated
        hidden = (silu * up).astype(BF16)
        down = down_weight[gate_at, :]
        result_scr[...] += mm(hidden, down)
        hidden_grad = mm(grad_rows, down, 1, 1)
        gate_grad = (hidden_grad * up * (gated * (1.0 + gate * (1.0 - gated)))).astype(BF16)
        up_grad = (hidden_grad * silu).astype(BF16)
        back_scr[...] += mm(gate_grad, in_weight[:, gate_at], 1, 1) + mm(
            up_grad, in_weight[:, up_at], 1, 1
        )
        tile_scr[:, gate_at] = mm(normed, gate_grad, 0, 0).astype(BF16)
        tile_scr[:, up_at] = mm(normed, up_grad, 0, 0).astype(BF16)
        down_scr[gate_at, :width] = mm(hidden, grad_rows, 0, 0).astype(BF16)
        return carry

    lax.fori_loop(0, ff // FF_STEP, ff_step, 0)

    put_tiles(in_outs, me, tile_scr, (0, 2 * ff), 0)
    base = 2 * (ff // LANES) * in_rows
    for out in in_outs:
        if base < out.shape[0]:
            out[base:, :] = jnp.zeros((out.shape[0] - base, LANES), BF16)
    whole = width // LANES * LANES
    put_tiles(outs, me, down_scr, (0, whole), 0)
    base = whole // LANES * down_rows
    half = down_rows // 2
    for relative, out in enumerate(outs):
        start = pl.multiple_of((me ^ relative) * down_rows, 16)
        rest = jnp.concatenate(
            [
                down_scr[pl.ds(start, half), whole:width],
                down_scr[pl.ds(pl.multiple_of(start + half, 16), half), whole:width],
            ],
            -1,
        )
        out[base : base + half, :] = rest
    base += half

    layer_out[...] = result_scr[...].astype(BF16).T
    middle_back, gain_terms = rms_back(middle, gain, back_scr[...])
    gain_grad[...] = jnp.zeros_like(gain_grad)
    gain_grad[0:1, :] = jnp.sum(gain_terms, 0, keepdims=True)
    middle_grad = middle_back + grad_rows.astype(F32)
    middle_grad_out[...] = middle_grad
    branch = middle_grad.astype(BF16)
    attended_grad_out[...] = mm(branch, out_weight[...], 1, 1).astype(BF16)
    out_weight_grad = mm(attended_low, branch, 0, 0).astype(BF16)
    wide = -(-width // LANES) * LANES
    tile_scr[:, :wide] = jnp.concatenate(
        [out_weight_grad, jnp.zeros((width, wide - width), BF16)], -1
    )
    put_tiles(outs, me, tile_scr, (0, wide), base)
    base += wide // LANES * in_rows
    for out in outs:
        out[base:, :] = jnp.zeros((out.shape[0] - base, LANES), BF16)
    for parts, to in (
        (in_outs, (in_mine, in_send.at[0], in_along, in_send.at[1])),
        (outs, (mine, send.at[0], along, send.at[1])),
    ):
        for part, out in zip(parts, to):
            in_slots(index[0], part, out, count)


def in_slots(here, flat, out, count):
    rows = flat.shape[0] // count
    for apart in range(count):
        slot = (apart & 1) * (count // 2) + apart // 2
        start = pl.multiple_of((here ^ apart) * rows, 16)
        out[slot * rows : (slot + 1) * rows, :] = flat[pl.ds(start, rows), :]


def put_small(outs, me, tile_scr, query_grad, kv_grad, query_weight, kv_weight, gains, ffn_gain_grad):
    width = query_grad.shape[0]
    wide = -(-width // LANES) * LANES
    gain_columns = gains[...].T
    terms = jnp.sum(query_grad * query_weight.astype(F32), -1, keepdims=True) + jnp.sum(
        kv_grad * kv_weight.astype(F32), -1, keepdims=True
    )
    columns = jnp.concatenate(
        [
            terms / gain_columns[:, 0:1],
            ffn_gain_grad[...].T[:, 0:1],
            jnp.zeros((width, wide - width - 2), F32),
        ],
        -1,
    )
    tile_scr[:, :wide] = jnp.concatenate([query_grad, columns], -1).astype(BF16)
    tile_scr[:, wide : wide + 2 * KVW] = kv_grad.astype(BF16)
    put_tiles(outs, me, tile_scr, (0, wide + 2 * KVW), 0)


def backward_kernel(
    index, queries, kv_all, attended, attended_grad, lse, normed, query_weight, kv_weight, gains,
    ffn_gain_grad, cosine, sine,
    *refs,
):
    q_scr, g_scr, delta_scr, acc_scr, query_grad_scr, masks = refs[-6:]
    fill_masks(masks)
    rows = queries.shape[0]
    blocks = kv_all.shape[0] // rows
    here = index[0]
    whole = normed.shape[0] > rows
    if whole:
        kv_grads, normed_grad, mine, along, send, tile_scr, weight_scr = refs[:-6]
        weight_scr[...] = jnp.zeros_like(weight_scr)
        kv_grads[...] = jnp.zeros_like(kv_grads)
    else:
        kv_grads, normed_grad, query_weight_grad = refs[:-6]
    for group in range(KV):
        q_scr[group] = stacked_heads(queries, group)
        grads = stacked_heads(attended_grad, group)
        g_scr[group] = grads
        terms = (grads.astype(F32) * stacked_heads(attended, group)).T
        delta_scr[group, 0:1, :] = jnp.sum(terms, 0, keepdims=True)
    acc_scr[...] = jnp.zeros_like(acc_scr)

    def step(j, carry):
        keys_at = block_at(j, rows)
        mask = jnp.concatenate([masks[jnp.where(j == here, 1, 0)]] * GROUPS, -1)
        key_grads = []
        value_grads = []
        for group in range(KV):
            keys = kv_all[keys_at, group * HD : (group + 1) * HD]
            values = kv_all[keys_at, KVW + group * HD : KVW + (group + 1) * HD]
            group_q = q_scr[group]
            group_g = g_scr[group]
            scores = mm(keys, group_q, 1, 1) + mask
            prob = jnp.exp(scores - lse[group : group + 1, :])
            prob_grad = mm(values, group_g, 1, 1)
            score_grad = (prob * (prob_grad - delta_scr[group, 0:1, :])).astype(BF16)
            value_grads.append(mm(prob.astype(BF16), group_g))
            key_grads.append(mm(score_grad, group_q))
            acc_scr[group] += mm(keys, score_grad, 0, 0)
        key_grad = jnp.concatenate(key_grads, -1)
        value_grad = jnp.concatenate(value_grads, -1)
        both = jnp.concatenate([key_grad, value_grad], -1).astype(BF16)
        if whole:
            apart = j ^ here
            kv_grads[(apart & 1) * (blocks // 2) + apart // 2] = both
            turned = rotated(key_grad, cosine[keys_at, :], sine[keys_at, :], -1.0)
            linear = jnp.concatenate([turned, value_grad], -1).astype(BF16)
            weight_scr[...] += mm(normed[keys_at, :], linear, 0, 0)
        else:
            kv_grads[keys_at, :] = both
        return carry

    def clear(j, carry):
        kv_grads[block_at(j, rows), :] = jnp.zeros((rows, kv_grads.shape[1]), BF16)
        return carry

    lax.fori_loop(0, here + 1, step, 0)
    if not whole:
        lax.fori_loop(here + 1, blocks, clear, 0)
    for group in range(KV):
        for g in range(GROUPS):
            head = group * GROUPS + g
            part = acc_scr[group, :, g * rows : (g + 1) * rows]
            query_grad_scr[:, head * HD : (head + 1) * HD] = part.T
    tables = (table_at(cosine, here, rows), table_at(sine, here, rows))
    back = rotated(query_grad_scr[...], *tables, -1.0) * (1.0 / math.sqrt(HD))
    back = back.astype(BF16)
    own_normed = normed[block_at(here, rows), :] if whole else normed[...]
    query_grad = mm(own_normed, back, 0, 0)
    normed_grad[...] = mm(back, query_weight[...], 1, 1)
    if whole:
        outs = (mine, send.at[0], along, send.at[1])
        put_small(
            outs, index[1], tile_scr, query_grad, weight_scr[...], query_weight[...],
            kv_weight[...], gains, ffn_gain_grad,
        )
    else:
        query_weight_grad[...] = query_grad


def small_kernel(
    index, query_grad, kv_grad, query_weight, kv_weight, gains, ffn_gain_grad,
    mine, along, send, tile_scr,
):
    outs = (mine, send.at[0], along, send.at[1])
    for out in outs:
        out[...] = jnp.zeros(out.shape, BF16)
    put_small(
        outs, index[1], tile_scr, query_grad[...], kv_grad[...], query_weight[...], kv_weight[...],
        gains, ffn_gain_grad,
    )


def tail_kernel(
    tokens, gains, normed_grad, middle_grad, kv_weight, cosine, sine, *refs
):
    kv_parts, tokens_grad = refs[:-1], refs[-1]
    rows = normed_grad.shape[0]
    if kv_parts[0].shape[0] > rows:

        def add(j, total):
            return total + kv_parts[0][block_at(j, rows), :].astype(F32)

        parts = kv_parts[0].shape[0] // rows
        kv_grad = lax.fori_loop(0, parts, add, jnp.zeros((rows, 2 * KVW), F32))
    else:
        kv_grad = kv_parts[0][...].astype(F32)
    key_back = rotated(kv_grad[:, :KVW], cosine[...], sine[...], -1.0)
    back = jnp.concatenate([key_back, kv_grad[:, KVW:]], -1).astype(BF16)
    total = normed_grad[...] + mm(back, kv_weight[...], 1, 1)
    values = tokens[...].T.astype(F32)
    input_grad, _ = rms_back(values, gains[0:1, :], total)
    tokens_grad[...] = (middle_grad[...] + input_grad).astype(BF16).T


def spread_kernel(index, *refs, count):
    *terms, keep, send = refs
    here = index[0]
    rows = keep.shape[1]
    for apart in range(count):
        at = pl.ds(pl.multiple_of((here ^ apart) * rows, 16), rows)
        total = terms[0][at, :].astype(F32)
        for term in terms[1:]:
            total = total + term[at, :].astype(F32)
        (send if apart & 1 else keep)[apart // 2] = total.astype(BF16)


def flattened(index, pieces, parts):
    here = index[0]
    if len(pieces) == 1:
        (piece,) = pieces
        total = sum(rows for _, rows in parts)
        count = piece.shape[0] // total
        owners = [(owner, piece, owner * total) for owner in range(count)]
    else:
        owners = [
            (here ^ (2 * slot + across), column.at[slot], 0)
            for across, column in enumerate(pieces)
            for slot in range(column.shape[0])
        ]
    for owner, piece, start in owners:
        for flat, rows in parts:
            at = pl.ds(pl.multiple_of(owner * rows, 16), rows)
            flat[at, :] = piece[start : start + rows, :]
            start += rows


def untile(out, flat, base, columns):
    rows = out.shape[0]
    for tile in range(columns // LANES):
        out[:, tile * LANES : (tile + 1) * LANES] = flat[base : base + rows, :].astype(F32)
        base += rows
    return base


def gate_up_kernel(index, *refs, rows):
    pieces, (gate_out, up_out, flat) = refs[:-3], refs[-3:]
    flattened(index, pieces, [(flat, rows)])
    base = untile(gate_out, flat, 0, gate_out.shape[1])
    untile(up_out, flat, base, up_out.shape[1])


def outputs_kernel(index, *refs, rows, more_rows):
    down_out, out_out, query_out, key_out, value_out, gain_out, flat, small = refs[-8:]
    flattened(index, refs[:-8], [(flat, rows), (small, more_rows)])
    base = 0
    width, rows = down_out.shape
    whole = width // LANES * LANES
    for tile in range(whole // LANES):
        part = flat[base : base + rows, :].astype(F32)
        down_out[tile * LANES : (tile + 1) * LANES, :] = part.T
        base += rows
    half = rows // 2
    rest = flat[base : base + half, :].astype(F32).T
    down_out[whole:, :] = jnp.concatenate([rest[: width - whole], rest[width - whole :]], -1)
    base = untile(out_out, flat, base + half, whole)
    rows = out_out.shape[0]
    out_out[:, whole:] = flat[base : base + rows, : width - whole].astype(F32)
    base = untile(query_out, small, 0, whole)
    tile = small[base : base + rows, :].astype(F32)
    query_out[:, whole:] = tile[:, : width - whole]
    gain_out[...] = tile[:, width - whole : width - whole + 8].T
    base += rows
    both = [
        small[base + at * rows : base + (at + 1) * rows, :].astype(F32)
        for at in range(2 * KVW // LANES)
    ]
    both = jnp.concatenate(both, -1)
    key_out[...] = both[:, :KVW]
    value_out[...] = both[:, KVW:]


def swap(value, axis, bit):
    count = lax.axis_size(axis)
    return lax.ppermute(value, axis, [(i, i ^ (1 << bit)) for i in range(count)])


def gathered_ws(value):
    pair = jnp.stack([value, swap(value, "ws", 1)])
    return pair, swap(pair, "ws", 0)


def column_of(value):
    far = swap(value, "ctx", 2)
    near = swap(jnp.stack([value, far]), "ctx", 1)
    return jnp.stack([value, near[0], far, near[1]])


def shifted(value, by, upward_only):
    count = lax.axis_size("ctx")
    pairs = [(i, i + 2 * by) for i in range(count)]
    if upward_only:
        pairs = [(i, j) for i, j in pairs if j < count]
    return lax.ppermute(value, "ctx", [(i, j % count) for i, j in pairs])


def rms_scale(values, gain_vec):
    return values * lax.rsqrt(jnp.mean(values * values, -1, keepdims=True) + EPS) * gain_vec


def added(*values):
    total = values[0].astype(F32)
    for value in values[1:]:
        total = total + value.astype(F32)
    return total.astype(values[0].dtype)


def scattered_ctx(values, counts):
    count = lax.axis_size("ctx")
    value = jnp.concatenate(
        [v.reshape(count, rows, LANES) for v, rows in zip(values, counts)], 1
    ).reshape(-1, LANES)
    parts = lax.all_to_all(value, "ctx", split_axis=0, concat_axis=0, tiled=True)
    parts = parts.reshape(count, -1, LANES).astype(F32)
    return jnp.sum(parts, 0).astype(value.dtype)


def rope_tables(positions):
    frequency = jnp.exp(jnp.arange(HD // 2).astype(F32) * (-2.0 * math.log(THETA) / HD))
    angles = positions.astype(F32)[:, None] * frequency[None, :]
    return jnp.cos(angles), jnp.sin(angles)


def turned_heads(values, cosine, sine):
    heads = values.reshape(values.shape[0], -1, 2, HD // 2)
    cosine, sine = cosine[:, None], sine[:, None]
    first, second = heads[:, :, 0], heads[:, :, 1]
    pair = [first * cosine - second * sine, second * cosine + first * sine]
    return jnp.stack(pair, 2).reshape(values.shape)


def summed_column(terms):
    def slot(at):
        return added(*[term[at] for term in terms])

    got = swap(jnp.stack([slot(1), slot(3)]), "ctx", 1)
    far = swap(added(*[term[2] for term in terms], got[1]), "ctx", 2)
    return added(*[term[0] for term in terms], got[0], far)


def spread(index, terms):
    count = lax.axis_size("ctx")
    shape = shaped((count // 2, terms[0].shape[0] // count, LANES), BF16)
    return call(
        functools.partial(spread_kernel, count=count),
        (shape, shape),
        (index, *terms),
        micros=2,
        smem=1,
    )


def padded_rows(rows, count):
    return -(-rows // (16 * count)) * 16 * count


def body(
    tokens,
    attn_gain,
    query_weight,
    key_weight,
    value_weight,
    output_weight,
    ffn_gain,
    gate_weight,
    up_weight,
    down_weight,
    out_grad,
):
    seq_count, rows, width = tokens.shape
    ctx_count = lax.axis_size("ctx")
    owners = lax.axis_size("ws")
    slice_rows = query_weight.shape[0]
    ff = gate_weight.shape[1]
    wide = -(-width // LANES) * LANES
    by_hops = ctx_count == 8
    tokens = tokens.reshape(rows, width).T
    out_grad = out_grad.reshape(rows, width).T
    ctx_index = lax.axis_index("ctx")
    index = jnp.stack([ctx_index, lax.axis_index("ws")]).astype(jnp.int32)

    if by_hops:
        behind_two = shifted(tokens, 2, True)

    gains = jnp.concatenate([attn_gain, ffn_gain]).reshape(2, slice_rows)
    packed = jnp.concatenate(
        [
            jnp.concatenate([key_weight, value_weight, query_weight], -1),
            jnp.pad(gains, ((0, 14), (0, 2 * KVW + width - slice_rows))),
        ],
        0,
    )
    packs = gathered_ws(packed)
    in_weight = jnp.concatenate([gate_weight, up_weight, output_weight], -1)
    in_along = swap(in_weight, "ws", 1)
    down_along = swap(down_weight, "ws", 1)

    def wide_tables(positions):
        cosine, sine = rope_tables(positions)
        return jnp.concatenate([cosine] * 4, -1), jnp.concatenate([-sine, sine] * 2, -1)

    first_pos = ctx_index * rows
    cosine, sine = wide_tables(first_pos + jnp.arange(rows, dtype=jnp.int32))
    if by_hops:
        tables = wide_tables(jnp.arange(ctx_count * rows, dtype=jnp.int32))
        later_tokens, tables = lax.optimization_barrier((tokens, tables))
        behind_one = shifted(later_tokens, 1, True)
        mate = swap(later_tokens, "ctx", 0)
        last = [(i - 2, i) for i in range(ctx_count - 2, ctx_count)]
        behind_three = lax.ppermute(behind_two, "ctx", last)
    else:
        tables = (cosine, sine)

    places = (0, 1, 4) if by_hops else (0,)
    more_places = (2, 5) if by_hops else ()
    late_places = (3, 6, 7) if by_hops else ()
    early = (tokens, mate, behind_two) if by_hops else (tokens,)
    early_normed, early_kv, queries, full_query, full_kv, gains = call(
        functools.partial(early_kernel, places=places, slice_rows=slice_rows),
        (
            shaped((len(places), rows, width), BF16),
            shaped((len(places), rows, 2 * KVW), BF16),
            shaped((rows, width), BF16),
            shaped((width, width), BF16),
            shaped((width, 2 * KVW), BF16),
            shaped((8, width), F32),
        ),
        (index,) + packs + tables + early,
        scratch=(
            pltpu.VMEM((owners * 16, 2 * LANES), BF16),
            pltpu.VMEM((len(places), width, rows), BF16),
        ),
        micros=6,
        smem=1,
        vmem=60,
    )
    if by_hops:
        behind_three, queries = lax.optimization_barrier((behind_three, queries))
        more = call(
            functools.partial(project_kernel, places=more_places),
            (
                shaped((len(more_places), rows, width), BF16),
                shaped((len(more_places), rows, 2 * KVW), BF16),
            ),
            (index, full_kv, gains, *tables, behind_one, swap(behind_two, "ctx", 0)),
            micros=3,
            smem=1,
            vmem=60,
        )
        late = (swap(behind_one, "ctx", 0), behind_three, swap(behind_three, "ctx", 0))
        normed_shape = (shaped((ctx_count * rows, width), BF16),)
        raw_scr = (pltpu.VMEM((len(late_places), width, rows), BF16),)
    else:
        tokens_all = lax.all_gather(tokens.T, "ctx", axis=0, tiled=True).astype(F32)
        normed_all = rms_scale(tokens_all, gains[0]).astype(BF16)
        linear = jnp.dot(normed_all, full_kv, preferred_element_type=F32)
        full_tables = rope_tables(jnp.arange(ctx_count * rows, dtype=jnp.int32))
        early_kv = jnp.concatenate(
            [turned_heads(linear[:, :KVW], *full_tables), linear[:, KVW:]], -1
        ).astype(BF16)
        more = ()
        late = ()
        normed_shape = ()
        raw_scr = ()

    late, in_weight, down_weight, in_along = lax.optimization_barrier(
        (late, in_weight, down_weight, in_along)
    )
    in_pieces = (in_weight, swap(in_weight, "ws", 0), in_along, swap(in_along, "ws", 0))
    down_core = swap(down_weight, "ws", 0)

    attended, lse, kv_all, *normed_out = call(
        functools.partial(
            forward_kernel, places=places, more_places=more_places, late_places=late_places
        ),
        (
            shaped((rows, width), F32),
            shaped((8, GROUPS * rows), F32),
            shaped((ctx_count * rows, 2 * KVW), BF16),
            *normed_shape,
        ),
        (index, queries, early_normed, early_kv, full_kv, gains, *tables, *more, *late),
        scratch=(
            *raw_scr,
            pltpu.VMEM((KV, GROUPS * rows, HD), BF16),
            pltpu.VMEM((KV, HD, GROUPS * rows), F32),
            pltpu.VMEM((KV, 8, GROUPS * rows), F32),
            pltpu.VMEM((KV, 8, GROUPS * rows), F32),
            pltpu.VMEM((2, rows, rows), F32),
        ),
        micros=20,
        smem=1,
        vmem=60,
    )

    attended, down_along = lax.optimization_barrier((attended, down_along))
    down_pieces = (down_weight, down_core, down_along, swap(down_along, "ws", 0))

    first_count = padded_rows(2 * slice_rows * ff // LANES, ctx_count)
    second_count = padded_rows(((ff // owners) * width + slice_rows * wide) // LANES, ctx_count)
    small_count = padded_rows(slice_rows * (wide + 2 * KVW) // LANES, ctx_count)
    first_rows, second_rows, small_rows = (
        rows_of // ctx_count for rows_of in (first_count, second_count, small_count)
    )

    def tile_shapes(rows_of):
        return (
            shaped((rows_of, LANES), BF16),
            shaped((rows_of, LANES), BF16),
            shaped((2, rows_of, LANES), BF16),
        )

    layer_out, middle_grad, attended_grad, ffn_gain_grad, *tiles = call(
        functools.partial(ffn_kernel, count=ctx_count if by_hops else 1),
        (
            shaped((width, rows), BF16),
            shaped((rows, width), F32),
            shaped((rows, width), BF16),
            shaped((8, width), F32),
            *tile_shapes(first_count),
            *tile_shapes(second_count),
        ),
        (index, tokens, attended, gains, out_grad) + in_pieces + down_pieces,
        scratch=(
            pltpu.VMEM((width, 2 * ff + width), BF16),
            pltpu.VMEM((ff, width), BF16),
            pltpu.VMEM((rows, width), F32),
            pltpu.VMEM((rows, width), F32),
            pltpu.VMEM((width, 2 * ff), BF16),
            pltpu.VMEM((ff, wide), BF16),
            pltpu.VMEM((owners, first_count, LANES), BF16),
            pltpu.VMEM((owners, second_count, LANES), BF16),
        ),
        micros=14,
        smem=1,
        vmem=60,
    )

    in_mine, in_along, in_send, mine, along, send = tiles
    got = swap(send, "ws", 0)
    in_got = swap(in_send, "ws", 0)
    in_crossing = added(in_along, in_got[1])
    if by_hops:
        half = second_count // 2

        def halves(value):
            shape = (ctx_count // 2, second_rows, LANES)
            return value[:half].reshape(shape), value[half:].reshape(shape)

        keep, to_mate = (
            jnp.concatenate(both, 1)
            for both in zip(halves(added(mine, got[0])), halves(added(along, got[1])))
        )
    else:
        to_mate = added(along, got[1])
    attended_grad, in_crossing, to_mate = lax.optimization_barrier(
        (attended_grad, in_crossing, to_mate)
    )
    in_crossed = swap(in_crossing, "ws", 1)
    from_mate = swap(to_mate, "ctx", 0) if by_hops else swap(to_mate, "ws", 1)

    tile_scr = pltpu.VMEM((width, wide + 2 * KVW), BF16)
    if by_hops:
        kv_shape = shaped((ctx_count, rows, 2 * KVW), BF16)
        backward_normed = normed_out[0]
        more_shapes = tile_shapes(small_count)
        more_scratch = (tile_scr, pltpu.VMEM((width, 2 * KVW), F32))
    else:
        kv_shape = shaped((ctx_count * rows, 2 * KVW), BF16)
        backward_normed = early_normed[0]
        more_shapes = (shaped((width, width), F32),)
        more_scratch = ()
    kv_grads, normed_grad, *small = call(
        backward_kernel,
        (kv_shape, shaped((rows, width), F32), *more_shapes),
        (
            index, queries, kv_all, attended, attended_grad, lse, backward_normed, full_query,
            full_kv, gains, ffn_gain_grad, *tables,
        ),
        scratch=(
            *more_scratch,
            pltpu.VMEM((KV, GROUPS * rows, HD), BF16),
            pltpu.VMEM((KV, GROUPS * rows, HD), BF16),
            pltpu.VMEM((KV, 8, GROUPS * rows), F32),
            pltpu.VMEM((KV, HD, GROUPS * rows), F32),
            pltpu.VMEM((rows, width), F32),
            pltpu.VMEM((2, rows, rows), F32),
        ),
        micros=23,
        smem=1,
        vmem=32 if by_hops else 60,
    )
    if not by_hops:
        linear = turned_heads(kv_grads[:, :KVW].astype(F32), full_tables[0], -full_tables[1])
        linear = jnp.concatenate([linear.astype(BF16), kv_grads[:, KVW:]], -1)
        kv_weight_grad = jnp.einsum("nd,nh->dh", normed_all, linear, preferred_element_type=F32)
        small = call(
            small_kernel,
            tile_shapes(small_count),
            (index, small[0], kv_weight_grad, full_query, full_kv, gains, ffn_gain_grad),
            scratch=(tile_scr,),
            smem=1,
        )
    kv_grads, small, in_crossed, from_mate = lax.optimization_barrier(
        (kv_grads, tuple(small), in_crossed, from_mate)
    )
    small_mine, small_along, small_send = small
    small_got = swap(small_send, "ws", 0)

    if by_hops:
        in_keep, in_to_mate = (
            added(in_mine[at], in_got[0, at], in_crossed[at]).reshape(-1, first_rows, LANES)
            for at in (slice(first_count // 2), slice(first_count // 2, None))
        )
        small_crossing = added(small_along, small_got[1])
        in_to_mate, small_crossing, from_mate = lax.optimization_barrier(
            (in_to_mate, small_crossing, from_mate)
        )
        in_from_mate = swap(in_to_mate, "ctx", 0)
        small_crossed = swap(small_crossing, "ws", 1)
        share = summed_column((keep, from_mate))
        in_from_mate, small_crossed = lax.optimization_barrier((in_from_mate, small_crossed))
        small_keep, small_to_mate = spread(index, (small_mine, small_got[0], small_crossed))
        small_to_mate, kv_to_mate, share = lax.optimization_barrier(
            (small_to_mate, kv_grads[ctx_count // 2 :], share)
        )
        small_from_mate = swap(small_to_mate, "ctx", 0)
        kv_from_mate = swap(kv_to_mate, "ctx", 0)
        in_share = summed_column((in_keep, in_from_mate))
        share = added(share[:second_rows], swap(share[second_rows:], "ws", 1))
        share = jnp.concatenate([share, summed_column((small_keep, small_from_mate))], 0)
        share, kv_from_mate = lax.optimization_barrier((share, kv_from_mate))
        in_column = column_of(in_share)
        in_pieces = (in_column, swap(in_column, "ctx", 0))
        column = column_of(share)
        pieces = (column, swap(column, "ctx", 0))
        kv_parts = (summed_column((kv_grads[: ctx_count // 2], kv_from_mate)),)
    else:
        kv_parts = (lax.all_to_all(kv_grads, "ctx", split_axis=0, concat_axis=0, tiled=True),)
        in_total = added(in_mine, in_got[0], in_crossed)
        total = added(mine, got[0], from_mate)
        small_crossed = swap(added(small_along, small_got[1]), "ws", 1)
        small_total = added(small_mine, small_got[0], small_crossed)
        in_share = scattered_ctx((in_total,), (first_rows,))
        share = scattered_ctx((total, small_total), (second_rows, small_rows))
        in_pieces, pieces = (
            (lax.all_gather(value, "ctx", axis=0, tiled=True),) for value in (in_share, share)
        )

    tokens_grad = call(
        tail_kernel,
        shaped((width, rows), BF16),
        (
            tokens, gains, normed_grad, middle_grad, full_kv, cosine, sine, *kv_parts,
        ),
        micros=4,
        vmem=16 if by_hops else 60,
    )

    gate_weight_grad, up_weight_grad = call(
        functools.partial(gate_up_kernel, rows=first_rows),
        (shaped(gate_weight.shape, F32), shaped(up_weight.shape, F32)),
        (index,) + in_pieces,
        scratch=(pltpu.VMEM((first_count, LANES), BF16),),
        micros=3,
        smem=1,
    )
    (
        down_weight_grad,
        output_weight_grad,
        query_weight_grad,
        key_weight_grad,
        value_weight_grad,
        gain_grads,
    ) = call(
        functools.partial(outputs_kernel, rows=second_rows, more_rows=small_rows),
        (
            shaped(down_weight.shape[::-1], F32),
            shaped(output_weight.shape, F32),
            shaped(query_weight.shape, F32),
            shaped(key_weight.shape, F32),
            shaped(value_weight.shape, F32),
            shaped((8, slice_rows), F32),
        ),
        (index,) + pieces,
        scratch=(pltpu.VMEM((second_count, LANES), BF16), pltpu.VMEM((small_count, LANES), BF16)),
        micros=3,
        smem=1,
    )
    return (
        layer_out.T.reshape(seq_count, rows, width),
        tokens_grad.T.reshape(seq_count, rows, width),
        gain_grads[0],
        query_weight_grad,
        key_weight_grad,
        value_weight_grad,
        output_weight_grad,
        gain_grads[1],
        gate_weight_grad,
        up_weight_grad,
        down_weight_grad.T,
    )


def solution(mesh):
    in_specs = (
        P("ws", "ctx", None),
        P("ws"),
        P("ws", None),
        P("ws", None),
        P("ws", None),
        P("ws", None),
        P("ws"),
        P("ws", None),
        P("ws", None),
        P("ws", None),
        P("ws", "ctx", None),
    )
    out_specs = (
        P("ws", "ctx", None),
        P("ws", "ctx", None),
        P("ws"),
        P("ws", None),
        P("ws", None),
        P("ws", None),
        P("ws", None),
        P("ws"),
        P("ws", None),
        P("ws", None),
        P("ws", None),
    )
    return jax.shard_map(body, mesh=mesh, in_specs=in_specs, out_specs=out_specs, check_vma=False)
```
